32 devices in a mesh: dp: 4 (over y, x), fsdp: 8 (over z, core).
Axes of the slice: x: 2, y: 2, z: 4, core: 2. Of those that a mesh axis runs over, the one named last changes fastest.
Arguments:
- tokens: bfloat16 [512, 196, 512], P(('dp', 'fsdp')), may hold values from -6 to 6
- valid_mask: int32 [512, 196], P(('dp', 'fsdp')), may hold values from 0 to 1, as said below
- keep_mask: int32 [512], P(('dp', 'fsdp')), may hold values 0 or 1
- out_cotangent: bfloat16 [512, 196, 512], P(('dp', 'fsdp')), may hold values from -6 to 6
- pool_cotangent: bfloat16 [512, 512], P(('dp', 'fsdp')), may hold values from -256 to 256
- inner_weight: float32 [2, 512, 1536], P(None, None, ('dp', 'fsdp')), may hold values from -0.25 to 0.25
- outer_weight: float32 [1536, 512], P(('dp', 'fsdp')), may hold values from -0.3125 to 0.3125
- vectors: float32 [7680], P(('dp', 'fsdp')), may hold values from -1.2 to 3
- spatial: float32 [197, 196], replicated, may hold values from -0.6 to 0.6
- inner_first: float32 [2, 512, 1536], P(None, None, ('dp', 'fsdp')), may hold values from -0.0004272461 to 0.0004272461
- inner_second: float32 [2, 512, 1536], P(None, None, ('dp', 'fsdp')), may hold values from 2.2032035e-08 to 8.729675e-08
- outer_first: float32 [1536, 512], P(('dp', 'fsdp')), may hold values from -0.0004272461 to 0.0004272461
- outer_second: float32 [1536, 512], P(('dp', 'fsdp')), may hold values from 2.2032035e-08 to 8.729675e-08
- vector_first: float32 [7680], P(('dp', 'fsdp')), may hold values from -0.0012207031 to 0.0012207031
- vector_second: float32 [7680], P(('dp', 'fsdp')), may hold values from 1.9537843e-07 to 7.898277e-07
- spatial_first: float32 [197, 196], replicated, may hold values from -0.0017089844 to 0.0017089844
- spatial_second: float32 [197, 196], replicated, may hold values from 3.444525e-07 to 1.3726303e-06
Outputs:
- output: float32 [512, 196, 512], P(('dp', 'fsdp'))
- input_grad: float32 [512, 196, 512], P(('dp', 'fsdp'))
- pooled: float32 [512, 512], P(('dp', 'fsdp'))
- grad_norm: float32 [], replicated
- inner_new: float32 [2, 512, 1536], P(None, None, ('dp', 'fsdp'))
- inner_first_new: float32 [2, 512, 1536], P(None, None, ('dp', 'fsdp'))
- inner_second_new: float32 [2, 512, 1536], P(None, None, ('dp', 'fsdp'))
- outer_new: float32 [1536, 512], P(('dp', 'fsdp'))
- outer_first_new: float32 [1536, 512], P(('dp', 'fsdp'))
- outer_second_new: float32 [1536, 512], P(('dp', 'fsdp'))
- vectors_new: float32 [7680], P(('dp', 'fsdp'))
- vector_first_new: float32 [7680], P(('dp', 'fsdp'))
- vector_second_new: float32 [7680], P(('dp', 'fsdp'))
- spatial_new: float32 [197, 196], replicated
- spatial_first_new: float32 [197, 196], replicated
- spatial_second_new: float32 [197, 196], replicated
The draws below stay inside these ranges and needn't reach their ends.
Inputs may be any that keep to these rules, and one draw needn't show every extreme that they name: `valid_mask`: each image's valid patch slots come first, at least 49 of them.
All inputs are finite; a program needn't handle non-finite values. No bound on the sum of `keep_mask` on one device may be relied on, other than what follows from the above.
Results may differ from the reference program's by a relative error of at most 0.0084.
Values may be sent and summed in bfloat16 or wider, within the bound.
A program may use at most 448 MiB of HBM per device.

```python
import math
import jax
import jax.numpy as jnp
from jax import lax

D = 512
GATE = 1536
P_SIZE = 196
IMG_DEV = 16
STEP = 10
IMAGES = 512
VEC = 7680


def draw_valid_mask(key, part):
    counts = jax.random.randint(key, (IMAGES, 1), P_SIZE // 4, P_SIZE + 1)
    positions = jnp.arange(P_SIZE, dtype=jnp.int32)[None, :]
    return jnp.where(positions < counts, 1, 0).astype(jnp.int32)


def draw_out_cotangent(key, part):
    key = jax.random.fold_in(key, 11)
    subkeys = jax.random.split(key, 2)
    common = jnp.clip(jax.random.normal(subkeys[0], (1, P_SIZE, D), jnp.float32), -4.0, 4.0)
    own_part = jnp.clip(jax.random.normal(subkeys[1], (IMAGES, P_SIZE, D), jnp.float32), -4.0, 4.0)
    return (0.5 * common + 0.85 * own_part).astype(jnp.bfloat16)


def draw_vectors(key, part):
    key = jax.random.fold_in(key, 5)
    subkeys = jax.random.split(key, 3)
    ramp_up = jnp.arange(GATE, dtype=jnp.float32) / GATE
    offsets = jnp.clip(0.3 * jax.random.normal(subkeys[0], (3 * D + 4 * GATE,), jnp.float32), -1.2, 1.2)
    rising = 0.5 * jnp.exp(jnp.log(3.2) * ramp_up)
    shift_two = jnp.clip(0.9 * jax.random.normal(subkeys[2], (GATE,), jnp.float32), -1.2, 1.2)
    roughness = jnp.exp(jax.random.uniform(subkeys[1], (D + GATE,), jnp.float32, -0.35, 0.35))
    gain_one = roughness[:D]
    gain_two = rising * roughness[D:]
    return jnp.concatenate([gain_one, offsets[D:3 * D], gain_two, shift_two, offsets[3 * D + 2 * GATE:]])


def draw_spatial(key, part):
    key = jax.random.fold_in(key, 7)
    subkeys = jax.random.split(key, 2)
    entry_spread = 0.4 / P_SIZE ** 0.5
    matrix = jnp.clip(jax.random.normal(subkeys[0], (P_SIZE, P_SIZE), jnp.float32) * entry_spread, -4.0 * entry_spread, 4.0 * entry_spread)
    bias_row = jnp.clip(0.25 * jax.random.normal(subkeys[1], (1, P_SIZE), jnp.float32), -0.6, 0.6)
    return jnp.concatenate([matrix, bias_row], axis=0)


def place_ends(array, key, smallest, top_value):
    longest = array.shape.index(max(array.shape))
    spots = []
    for shift in (0, 1):
        where = [jax.random.randint(jax.random.fold_in(key, axis), (), 0, length) for axis, length in enumerate(array.shape)]
        where[longest] = (where[longest] + shift) % array.shape[longest]
        spots.append(tuple(where))
    return array.at[spots[0]].set(smallest).at[spots[1]].set(top_value)


def levels(key, dims, cuts, least, largest):
    def one(axis_at, shards_of):
        draws = jax.random.uniform(jax.random.fold_in(jax.random.fold_in(key, 6), axis_at), (shards_of,), jnp.float32, least / len(cuts), largest / len(cuts))
        return jnp.repeat(jnp.exp(draws), dims[axis_at] // shards_of).reshape((-1,) + (1,) * (len(dims) - axis_at - 1))

    level = one(*cuts[0])
    for cut in cuts[1:]:
        level = level * one(*cut)
    return level


def bell_draw(stream_key, shape, scale, most, cuts=(), held_as=jnp.bfloat16):
    drawn = scale * jax.random.normal(stream_key, shape, jnp.float32)
    if cuts:
        drawn = drawn * levels(stream_key, shape, cuts, -0.22, 0.18)
    return jnp.clip(drawn, -most, most).astype(held_as)


def setup_inputs(seed: int = 0) -> dict:
    arg_keys = jax.random.split(jax.random.key(seed), 18)
    tokens = bell_draw(arg_keys[0], (IMAGES, P_SIZE, D), 1.0, 6.0, ((0, 32),))
    valid_mask = draw_valid_mask(jax.random.fold_in(arg_keys[17], 71), 0)
    keep_mask = place_ends((jax.random.randint(arg_keys[2], (IMAGES,), 0, 10) < 9).astype(jnp.int32), jax.random.fold_in(arg_keys[2], 1), 0, 1)
    out_cotangent = draw_out_cotangent(jax.random.fold_in(arg_keys[17], 71), 0)
    pool_cotangent = bell_draw(arg_keys[4], (IMAGES, D), (P_SIZE // 4), 256.0, ((0, 32),))
    inner_weight = bell_draw(arg_keys[5], (2, D, GATE), D ** -0.5, 0.25, ((2, 32),), jnp.float32)
    outer_weight = bell_draw(arg_keys[6], (GATE, D), (GATE // 4) ** -0.5, 0.3125, ((0, 32),), jnp.float32)
    vectors = draw_vectors(jax.random.fold_in(arg_keys[17], 71), 0)
    spatial = draw_spatial(jax.random.fold_in(arg_keys[17], 71), 0)
    inner_first = bell_draw(arg_keys[9], (2, D, GATE), (0.111 * (3 * D * GATE + 3 * D + 4 * GATE + P_SIZE * P_SIZE + P_SIZE) ** -0.5), 0.0004272461, ((2, 32),), jnp.float32)
    inner_second = jnp.clip(jnp.exp(math.log(8.729674760843409e-08) - 1.3768157 * jax.random.uniform(arg_keys[10], (2, D, GATE), jnp.float32) ** levels(arg_keys[10], (2, D, GATE), ((2, 32),), -0.2, 0.2)), 2.2032034863173067e-08, 8.729674760843409e-08)
    outer_first = bell_draw(arg_keys[11], (GATE, D), (0.111 * (3 * D * GATE + 3 * D + 4 * GATE + P_SIZE * P_SIZE + P_SIZE) ** -0.5), 0.0004272461, ((0, 32),), jnp.float32)
    outer_second = jnp.clip(jnp.exp(math.log(8.729674760843409e-08) - 1.3768157 * jax.random.uniform(arg_keys[12], (GATE, D), jnp.float32) ** levels(arg_keys[12], (GATE, D), ((0, 32),), -0.2, 0.2)), 2.2032034863173067e-08, 8.729674760843409e-08)
    vector_first = bell_draw(arg_keys[13], (VEC,), (0.333 * (3 * D * GATE + 3 * D + 4 * GATE + P_SIZE * P_SIZE + P_SIZE) ** -0.5), 0.0012207031, ((0, 32),), jnp.float32)
    vector_second = jnp.clip(jnp.exp(math.log(7.898277090134798e-07) - 1.3968765 * jax.random.uniform(arg_keys[14], (VEC,), jnp.float32) ** levels(arg_keys[14], (VEC,), ((0, 32),), -0.2, 0.2)), 1.9537843343186978e-07, 7.898277090134798e-07)
    spatial_first = bell_draw(arg_keys[15], (P_SIZE + 1, P_SIZE), (0.0555 * ((P_SIZE + 1) * P_SIZE) ** -0.5), 0.0017089844, (), jnp.float32)
    spatial_second = jnp.clip(jnp.exp(jax.random.uniform(arg_keys[16], (P_SIZE + 1, P_SIZE), jnp.float32, math.log(3.4445250207681966e-07), math.log(1.372630322293844e-06))), 3.4445250207681966e-07, 1.372630322293844e-06)
    return {"tokens": tokens, "valid_mask": valid_mask, "keep_mask": keep_mask, "out_cotangent": out_cotangent, "pool_cotangent": pool_cotangent, "inner_weight": inner_weight, "outer_weight": outer_weight, "vectors": vectors, "spatial": spatial, "inner_first": inner_first, "inner_second": inner_second, "outer_first": outer_first, "outer_second": outer_second, "vector_first": vector_first, "vector_second": vector_second, "spatial_first": spatial_first, "spatial_second": spatial_second}


NORM_EPS = 1e-05
DROP_RATE = 0.1
BETA_FIRST = 0.9
BETA_SECOND = 0.95
ADAM_EPS = 1e-08
DECAY_RATE = 0.05
RATE_MATRIX = 0.05
RATE_VECTOR = 0.8
CLIP_BOUND = 1.0
HIGHEST_PRECISION = lax.Precision.HIGHEST

@jax.custom_vjp
def low(v):
    return lax.optimization_barrier(v.astype(jnp.bfloat16)).astype(jnp.float32)

@jax.custom_vjp
def low_back(v):
    return v

def low_keep(v):
    return (low(v), None)

def low_pass(kept, grad):
    return (grad,)

def back_keep(v):
    return (v, None)

def back_low(kept, grad):
    return (low(grad),)
low.defvjp(low_keep, low_pass)
low_back.defvjp(back_keep, back_low)

def layer_norm(values, scaling, offset):
    center = values - lax.optimization_barrier(jnp.mean(values, axis=-1, keepdims=True))
    spread = lax.optimization_barrier(jnp.mean(center * center, axis=-1, keepdims=True))
    return center * lax.rsqrt(spread + NORM_EPS) * scaling + offset

def unpack(packed):
    gain_one = packed[0:D]
    shift_one = packed[D:2 * D]
    bias_out = packed[2 * D:3 * D]
    gain_two = packed[3 * D:3 * D + GATE]
    shift_two = packed[3 * D + GATE:3 * D + 2 * GATE]
    bias_in = packed[3 * D + 2 * GATE:].reshape(2, GATE)
    return (gain_one, shift_one, bias_out, gain_two, shift_two, bias_in)

def block(inner_low, outer_low, vector_low, spatial_low, spatial_bias, tokens_block, valid_block, scale_block):
    gain_one, shift_one, bias_out, gain_two, shift_two, bias_in = unpack(vector_low)
    patch_mask = valid_block[:, :, None]
    normed = low(layer_norm(tokens_block, gain_one, shift_one))
    before = low_back(jnp.einsum('bpd,adg->abpg', normed, inner_low, precision=HIGHEST_PRECISION) + bias_in[:, None, None, :])
    hidden = jax.nn.gelu(before, approximate=True)
    mixed_in = low(layer_norm(hidden[1], gain_two, shift_two) * patch_mask)
    spatial_out = low_back(jnp.einsum('ij,bjg->big', spatial_low, mixed_in, precision=HIGHEST_PRECISION) + spatial_bias[None, :, None])
    gated = low(hidden[0] * spatial_out * patch_mask)
    branch = low_back(jnp.einsum('bpg,gd->bpd', gated, outer_low, precision=HIGHEST_PRECISION) + bias_out)
    output = tokens_block + scale_block[:, None, None] * branch
    patch_count = lax.optimization_barrier(jnp.sum(valid_block, axis=1))
    pooled = lax.optimization_barrier(jnp.sum(output * patch_mask, axis=1)) / patch_count[:, None]
    return (output, pooled)

def adam_step(weight, first, second, gradient, step_rate, weight_decay):
    first_new = BETA_FIRST * first + (1.0 - BETA_FIRST) * gradient
    second_new = BETA_SECOND * second + (1.0 - BETA_SECOND) * gradient * gradient
    first_hat = first_new / (1.0 - BETA_FIRST ** STEP)
    second_hat = second_new / (1.0 - BETA_SECOND ** STEP)
    weight_new = weight - step_rate * (first_hat / (jnp.sqrt(second_hat) + ADAM_EPS) + weight_decay * weight)
    return (weight_new, first_new, second_new)

def reference(tokens, valid_mask, keep_mask, out_cotangent, pool_cotangent, inner_weight, outer_weight, vectors, spatial, inner_first, inner_second, outer_first, outer_second, vector_first, vector_second, spatial_first, spatial_second):
    blocks = IMAGES // IMG_DEV
    tokens_all = tokens.astype(jnp.float32).reshape(blocks, IMG_DEV, P_SIZE, D)
    valid_all = valid_mask.astype(jnp.float32).reshape(blocks, IMG_DEV, P_SIZE)
    scale_all = (keep_mask.astype(jnp.float32) / (1.0 - DROP_RATE)).reshape(blocks, IMG_DEV)

    def forward(params, inputs):
        inner_low = low(params[0])
        outer_low = low(params[1])
        vector_low = low(params[2])
        spatial_low = low(params[3][:P_SIZE])
        spatial_bias = params[3][P_SIZE]

        def one_block(pieces):
            return jax.checkpoint(block)(inner_low, outer_low, vector_low, spatial_low, spatial_bias, pieces[0], pieces[1], pieces[2])
        return lax.map(one_block, (inputs, valid_all, scale_all))
    params = (inner_weight, outer_weight, vectors, spatial)
    (output, pooled), pullback = jax.vjp(forward, params, tokens_all)
    cotangents = (out_cotangent.astype(jnp.float32).reshape(output.shape), pool_cotangent.astype(jnp.float32).reshape(pooled.shape))
    gradients, input_grad = pullback(cotangents)
    inner_grad, outer_grad, vector_grad, spatial_grad = gradients
    squares_total = jnp.sum(inner_grad * inner_grad) + jnp.sum(outer_grad * outer_grad)
    squares_total = squares_total + jnp.sum(vector_grad * vector_grad) + jnp.sum(spatial_grad * spatial_grad)
    grad_norm = jnp.sqrt(squares_total)
    clip_factor = CLIP_BOUND / jnp.maximum(grad_norm, CLIP_BOUND)
    inner_new, inner_first_new, inner_second_new = adam_step(inner_weight, inner_first, inner_second, inner_grad * clip_factor, RATE_MATRIX, DECAY_RATE)
    outer_new, outer_first_new, outer_second_new = adam_step(outer_weight, outer_first, outer_second, outer_grad * clip_factor, RATE_MATRIX, DECAY_RATE)
    vectors_new, vector_first_new, vector_second_new = adam_step(vectors, vector_first, vector_second, vector_grad * clip_factor, RATE_VECTOR, 0.0)
    row_index = jnp.arange(P_SIZE + 1)[:, None]
    spatial_rate = jnp.where(row_index < P_SIZE, RATE_MATRIX, RATE_VECTOR)
    spatial_decay = jnp.where(row_index < P_SIZE, DECAY_RATE, 0.0)
    spatial_new, spatial_first_new, spatial_second_new = adam_step(spatial, spatial_first, spatial_second, spatial_grad * clip_factor, spatial_rate, spatial_decay)
    return (output.reshape(IMAGES, P_SIZE, D), input_grad.reshape(IMAGES, P_SIZE, D), pooled.reshape(IMAGES, D), grad_norm, inner_new, inner_first_new, inner_second_new, outer_new, outer_first_new, outer_second_new, vectors_new, vector_first_new, vector_second_new, spatial_new, spatial_first_new, spatial_second_new)
```

```python
import functools
import jax
import jax.numpy as jnp
from jax import lax
from jax.experimental import pallas as pl
from jax.experimental.pallas import tpu as pltpu
from jax.sharding import PartitionSpec as P

NORM_EPS = 1e-05
DROP_RATE = 0.1
BF = jnp.bfloat16
F32 = jnp.float32
GELU_K = 0.7978845608
GELU_C = 0.044715
NN = (((1,), (0,)), ((), ()))
NT = (((1,), (1,)), ((), ()))
TN = (((0,), (0,)), ((), ()))


def dot(a, b, dims):
    return lax.dot_general(a, b, dims, preferred_element_type=F32)


def gelu_pair(v):
    u = v * v
    s = 0.5 * jnp.tanh(v * (GELU_K + (GELU_K * GELU_C) * u)) + 0.5
    h = v * s
    d = s + (h - h * s) * (2.0 * GELU_K + (6.0 * GELU_K * GELU_C) * u)
    return h, d


def fold8(x):
    rows = x.shape[0]
    total = x[0:8]
    for r in range(8, rows, 8):
        total = total + x[r : r + 8]
    return total


def lanes(x):
    total = x[:, 0:128]
    for c in range(128, x.shape[1], 128):
        total = total + x[:, c : c + 128]
    return total


def block_kernel(
    cfg,
    counts,
    keeps,
    tokens_hbm,
    cot_hbm,
    pool_ref,
    wt_ref,
    outer_ref,
    vec_ref,
    sp_ref,
    spt_ref,
    sbias_ref,
    out_hbm,
    ig_hbm,
    pooled_ref,
    inner_acc,
    outer_acc,
    vecg_ref,
    sg_ref,
    sbg_ref,
    off_s,
    gend_s,
    grows_s,
    x_all,
    c_all,
    normed_b,
    bg_b,
    h0_b,
    e0_b,
    mg_b,
    xm_b,
    u2_b,
    d1_b,
    stat_b,
    br_b,
    ng_b,
    h1_s,
    t_s,
    out_st,
    ig_st,
    vacc,
    in_sem,
    out_sem,
):
    images, patches, width, gate, rows_cap, tm, kw, classes = cfg
    nv = width // 512
    del nv
    cw = 256
    nj = gate // cw

    def vrow(base, j):
        start = base + j * cw
        return vec_ref[start // 512 : start // 512 + 1, start % 512 : start % 512 + cw]

    gain_one = vec_ref[0:1, :]
    shift_one = vec_ref[1:2, :]
    bias_out = vec_ref[2:3, :]
    g2_base, s2_base, b0_base, b1_base = 3 * width, 3 * width + gate, 3 * width + 2 * gate, 3 * width + 3 * gate

    def in_copies(b):
        return (
            pltpu.make_async_copy(tokens_hbm.at[b], x_all.at[b], in_sem.at[0, b]),
            pltpu.make_async_copy(cot_hbm.at[b], c_all.at[b], in_sem.at[1, b]),
        )

    for b in range(images):
        for cp in in_copies(b):
            cp.start()

    def plan(b, carry):
        group, row = carry
        need = keeps[b] * (((counts[b] + 15) // 16) * 16)
        over = (row + need > rows_cap).astype(jnp.int32)
        group = group + over
        row = jnp.where(over == 1, 0, row)
        off_s[b] = row
        row = row + need
        gend_s[group] = b + 1
        grows_s[group] = row
        return group, row

    last_group, _ = lax.fori_loop(0, images, plan, (jnp.int32(0), jnp.int32(0)))

    def zero_rows(ref, n_chunks, start):
        z = jnp.zeros((16, ref.shape[1]), ref.dtype)

        def body(i, c):
            ref[pl.ds(pl.multiple_of(start + i * 16, 16), 16), :] = z
            return c

        lax.fori_loop(0, n_chunks, body, 0)

    for ref in (normed_b, bg_b, h0_b, e0_b, mg_b, xm_b, u2_b, d1_b):
        zero_rows(ref, ref.shape[0] // 16, 0)
    vacc[...] = jnp.zeros_like(vacc)
    inner_acc[...] = jnp.zeros_like(inner_acc)
    outer_acc[...] = jnp.zeros_like(outer_acc)
    sg_ref[...] = jnp.zeros_like(sg_ref)
    sbg_ref[...] = jnp.zeros_like(sbg_ref)
    stat_b[...] = jnp.zeros_like(stat_b)

    row_chunks = [(r, min(32, patches - r)) for r in range(0, patches // 16 * 16, 32)]
    row_chunks = []
    r = 0
    full = patches // 16 * 16
    while r < full:
        step = min(32, full - r)
        row_chunks.append((r, step))
        r += step
    tail = (full, patches - full) if full < patches else None

    def load_rows(ref, b, r, rs):
        return ref[b, r : r + rs, :].astype(F32)

    def norm(x):
        c = x - jnp.mean(x, axis=-1, keepdims=True)
        inv = lax.rsqrt(jnp.mean(c * c, axis=-1, keepdims=True) + NORM_EPS)
        return c * inv, inv

    def row_ids(r, rs):
        return lax.broadcasted_iota(jnp.int32, (rs, 1), 0) + r

    def scale_of(b):
        return keeps[b].astype(F32) * (1.0 / (1.0 - DROP_RATE))

    def phase_in(b):
        for cp in in_copies(b):
            cp.wait()

        @pl.when(keeps[b] == 1)
        def _():
            n = counts[b]
            o = pl.multiple_of(off_s[b], 16)
            ks = scale_of(b)
            pool = pool_ref[b]
            bsum = jnp.zeros((8, width), F32)
            for r, rs in row_chunks + ([tail] if tail else []):
                x = load_rows(x_all, b, r, rs)
                c = load_rows(c_all, b, r, rs)
                unit, _ = norm(x)
                normed = unit * gain_one + shift_one
                valid = row_ids(r, rs) < n
                og = c + jnp.where(valid, pool, 0.0)
                bg = (ks * og).astype(BF).astype(F32)
                bgm = jnp.where(valid, bg, 0.0)
                if rs % 16:
                    pad = 16 - rs
                    z = jnp.zeros((pad, width), F32)
                    normed = jnp.concatenate([normed, z], axis=0)
                    bg = jnp.concatenate([bg, z], axis=0)
                    bgm = jnp.concatenate([bgm, z], axis=0)
                    rs = 16
                bsum = bsum + fold8(bg)
                normed_b[pl.ds(o + r, rs), :] = normed.astype(BF)
                bg_b[pl.ds(o + r, rs), :] = bgm.astype(BF)
            vacc[2] += bsum

    def phase_a(t):
        r0 = pl.multiple_of(t * tm, tm)
        rows = pl.ds(r0, tm)
        nb = normed_b[rows, :]
        bgt = bg_b[rows, :]
        s1 = jnp.zeros((tm, 128), F32)
        for j in range(nj):
            cols = slice(j * cw, (j + 1) * cw)
            a1 = dot(nb, wt_ref[1, cols, :], NT) + vrow(b1_base, j)
            h1, d1 = gelu_pair(a1)
            h1_s[:, cols] = h1
            d1_b[rows, cols] = d1.astype(BF)
            s1 = s1 + lanes(h1)
        mean = jnp.sum(s1, axis=1, keepdims=True) * (1.0 / gate)
        q1 = jnp.zeros((tm, 128), F32)
        rs1 = jnp.zeros((tm, 128), F32)
        for j in range(nj):
            cols = slice(j * cw, (j + 1) * cw)
            a0 = dot(nb, wt_ref[0, cols, :], NT) + vrow(b0_base, j)
            h0, d0 = gelu_pair(a0)
            gg = dot(bgt, outer_ref[cols, :], NT)
            mg = gg * h0
            h0_b[rows, cols] = h0.astype(BF)
            mg_b[rows, cols] = mg.astype(BF)
            e0_b[rows, cols] = (gg * d0).astype(BF)
            rs1 = rs1 + lanes(mg)
            c = h1_s[:, cols] - mean
            q1 = q1 + lanes(c * c)
        inv = lax.rsqrt(jnp.sum(q1, axis=1, keepdims=True) * (1.0 / gate) + NORM_EPS)
        stat_b[rows, 0:128] = jnp.broadcast_to(inv, (tm, 128))
        stat_b[rows, 128:256] = rs1
        for j in range(nj):
            cols = slice(j * cw, (j + 1) * cw)
            u2 = (h1_s[:, cols] - mean) * inv
            u2_b[rows, cols] = u2.astype(BF)
            xm_b[rows, cols] = (u2 * vrow(g2_base, j) + vrow(s2_base, j)).astype(BF)

    def phase_b(b, m):
        n = counts[b]
        o = pl.multiple_of(off_s[b], 16)
        need = ((n + 15) // 16) * 16
        rows = pl.ds(o, m)
        rid = lax.broadcasted_iota(jnp.int32, (m, 1), 0)
        cid = lax.broadcasted_iota(jnp.int32, (m, m), 1)
        rid2 = lax.broadcasted_iota(jnp.int32, (m, m), 0)
        both = (cid < n) & (rid2 < n)
        sp = jnp.where(both, sp_ref[0:m, 0:m], 0.0).astype(BF)
        spt = jnp.where(both, spt_ref[0:m, 0:m], 0.0).astype(BF)
        sbias = sbias_ref[0:m, :]
        inside = rid < need
        inv = stat_b[rows, 0:1]
        tsum = jnp.zeros((m, 128), F32)
        tdot = jnp.zeros((m, 128), F32)
        sg = jnp.zeros((m, m), F32)
        for j in range(nj):
            cols = slice(j * cw, (j + 1) * cw)
            xm = xm_b[rows, cols]
            mg = mg_b[rows, cols]
            so = dot(sp, xm, NN) + sbias
            so = jnp.where(inside, so, 1.0)
            mix = dot(spt, mg, NN)
            sg = sg + dot(mg, xm, NT)
            h0_b[rows, cols] = (h0_b[rows, cols].astype(F32) * so).astype(BF)
            e0_b[rows, cols] = (e0_b[rows, cols].astype(F32) * so).astype(BF)
            u2 = u2_b[rows, cols].astype(F32)
            mu = mix * u2
            gain = vrow(g2_base, j)
            t = mix * gain
            t_s[0:m, cols] = t
            tsum = tsum + lanes(t)
            tdot = tdot + lanes(mu * gain)
            start = j * cw
            vi = start // 512
            lo = start % 512
            vacc[3 + vi, :, lo : lo + cw] += fold8(mu)
            vacc[3 + gate // 512 + vi, :, lo : lo + cw] += fold8(mix)
        sg_ref[0:m, 0:m] += jnp.where(both, sg, 0.0)
        sbg_ref[0:m, :] += jnp.where(rid < n, stat_b[rows, 128:256], 0.0)
        m1 = jnp.sum(tsum, axis=1, keepdims=True) * (1.0 / gate)
        m2 = jnp.sum(tdot, axis=1, keepdims=True) * (1.0 / gate)
        for j in range(nj):
            cols = slice(j * cw, (j + 1) * cw)
            u2 = u2_b[rows, cols].astype(F32)
            sec = inv * (t_s[0:m, cols] - m1 - u2 * m2)
            sec = jnp.where(inside, sec, 1.0)
            d1_b[rows, cols] = (d1_b[rows, cols].astype(F32) * sec).astype(BF)

    def phase_c(t):
        r0 = pl.multiple_of(t * tm, tm)
        rows = pl.ds(r0, tm)
        br_b[rows, :] = dot(h0_b[rows, :], outer_ref[...], NN)
        ng_b[rows, :] = dot(e0_b[rows, :], wt_ref[0], NN) + dot(d1_b[rows, :], wt_ref[1], NN)
        base = b0_base // 512
        for a, ref in ((0, e0_b), (1, d1_b)):
            for v in range(gate // 512):
                part = ref[rows, v * 512 : (v + 1) * 512].astype(F32)
                vacc[base + a * (gate // 512) + v] += fold8(part)

    def phase_w(k):
        rows = pl.ds(pl.multiple_of(k * kw, kw), kw)
        nb = normed_b[rows, :]
        bgt = bg_b[rows, :]
        for j in range(gate // 256):
            cols = slice(j * 256, (j + 1) * 256)
            outer_acc[cols, :] += dot(h0_b[rows, cols], bgt, TN)
            inner_acc[0, cols, :] += dot(e0_b[rows, cols], nb, TN)
            inner_acc[1, cols, :] += dot(d1_b[rows, cols], nb, TN)

    def out_copies(b, slot):
        return (
            pltpu.make_async_copy(out_st.at[slot], out_hbm.at[b], out_sem.at[0, slot]),
            pltpu.make_async_copy(ig_st.at[slot], ig_hbm.at[b], out_sem.at[1, slot]),
        )

    def phase_d(b):
        slot = lax.rem(b, 2)

        @pl.when(b >= 2)
        def _():
            for cp in out_copies(b - 2, slot):
                cp.wait()

        n = counts[b]
        kn = keeps[b] * n
        o = pl.multiple_of(off_s[b], 16)
        ks = scale_of(b)
        pool = pool_ref[b]
        psum = jnp.zeros((8, width), F32)
        g1 = jnp.zeros((8, width), F32)
        s1 = jnp.zeros((8, width), F32)
        for r, rs in row_chunks + ([tail] if tail else []):
            x = load_rows(x_all, b, r, rs)
            c = load_rows(c_all, b, r, rs)
            unit, inv = norm(x)
            ids = row_ids(r, rs)
            valid = ids < n
            live = ids < kn
            og = c + jnp.where(valid, pool, 0.0)
            br = jnp.where(live, br_b[pl.ds(o + r, rs), :], 0.0)
            out = x + ks * (br + bias_out)
            out_st[slot, r : r + rs, :] = out
            ng = jnp.where(live, ng_b[pl.ds(o + r, rs), :], 0.0)
            t = ng * gain_one
            m1 = jnp.mean(t, axis=-1, keepdims=True)
            m2 = jnp.mean(t * unit, axis=-1, keepdims=True)
            ig_st[slot, r : r + rs, :] = og + inv * (t - m1 - unit * m2)
            ov = jnp.where(valid, out, 0.0)
            gu = ng * unit
            if rs % 8:
                z = jnp.zeros((8 - rs % 8, width), F32)
                ov = jnp.concatenate([ov, z], axis=0)
                gu = jnp.concatenate([gu, z], axis=0)
                ng = jnp.concatenate([ng, z], axis=0)
            psum = psum + fold8(ov)
            g1 = g1 + fold8(gu)
            s1 = s1 + fold8(ng)
        vacc[0] += g1
        vacc[1] += s1
        total = jnp.sum(psum, axis=0, keepdims=True)
        pooled_ref[b] = total / jnp.full((1, width), n.astype(F32), F32)
        for cp in out_copies(b, slot):
            cp.start()

    def group(g, b_start):
        b_end = gend_s[g]
        rows = grows_s[g]

        def loop(lo, hi, fn):
            def body(i, c):
                fn(i)
                return c

            lax.fori_loop(lo, hi, body, 0)

        loop(b_start, b_end, phase_in)
        zero_rows(normed_b, kw // 16, rows)
        zero_rows(bg_b, kw // 16, rows)
        tiles = (rows + tm - 1) // tm
        loop(0, tiles, phase_a)
        zero_rows(d1_b, tm // 16, rows)

        def do_b(b):
            n = counts[b]
            low = 0
            for m in classes:
                @pl.when((keeps[b] == 1) & (n > low) & (n <= m))
                def _(m=m):
                    phase_b(b, m)
                low = m

        loop(b_start, b_end, do_b)
        loop(0, tiles, phase_c)
        loop(0, (rows + kw - 1) // kw, phase_w)
        loop(b_start, b_end, phase_d)
        return b_end

    lax.fori_loop(0, last_group + 1, group, jnp.int32(0))
    for b in (images - 2, images - 1):
        for cp in out_copies(b, b % 2):
            cp.wait()
    vecg_ref[...] = jnp.sum(vacc[...], axis=1)


def run_block(counts, keeps, tokens, cot, pool, wt, outer, vec, sp, spt, sbias, *, rows_cap=1024, tm=128, kw=256, classes=(112, 160, 208)):
    images, patches, width = tokens.shape
    gate = outer.shape[0]
    pad = sp.shape[0]
    nvec = vec.shape[0]
    cap = rows_cap + 256
    cfg = (images, patches, width, gate, rows_cap, tm, kw, classes)
    smem = pl.BlockSpec(memory_space=pltpu.SMEM)
    vmem = pl.BlockSpec(memory_space=pltpu.VMEM)
    anyb = pl.BlockSpec(memory_space=pl.ANY)
    return pl.pallas_call(
        functools.partial(block_kernel, cfg),
        out_shape=(
            jax.ShapeDtypeStruct((images, patches, width), F32),
            jax.ShapeDtypeStruct((images, patches, width), F32),
            jax.ShapeDtypeStruct((images, 1, width), F32),
            jax.ShapeDtypeStruct((2, gate, width), F32),
            jax.ShapeDtypeStruct((gate, width), F32),
            jax.ShapeDtypeStruct((nvec, width), F32),
            jax.ShapeDtypeStruct((pad, pad), F32),
            jax.ShapeDtypeStruct((pad, 128), F32),
        ),
        in_specs=[smem, smem, anyb, anyb] + [vmem] * 7,
        out_specs=[anyb, anyb] + [vmem] * 6,
        scratch_shapes=[
            pltpu.SMEM((images,), jnp.int32),
            pltpu.SMEM((images,), jnp.int32),
            pltpu.SMEM((images,), jnp.int32),
            pltpu.VMEM((images, patches, width), BF),
            pltpu.VMEM((images, patches, width), BF),
            pltpu.VMEM((cap, width), BF),
            pltpu.VMEM((cap, width), BF),
        ]
        + [pltpu.VMEM((cap, gate), BF)] * 6
        + [
            pltpu.VMEM((cap, 256), F32),
            pltpu.VMEM((cap, width), F32),
            pltpu.VMEM((cap, width), F32),
            pltpu.VMEM((tm, gate), F32),
            pltpu.VMEM((pad, gate), F32),
            pltpu.VMEM((2, patches, width), F32),
            pltpu.VMEM((2, patches, width), F32),
            pltpu.VMEM((nvec, 8, width), F32),
            pltpu.SemaphoreType.DMA((2, images)),
            pltpu.SemaphoreType.DMA((2, 2)),
        ],
        compiler_params=pltpu.CompilerParams(vmem_limit_bytes=60 * 2**20),
        name="block",
    )(counts, keeps, tokens, cot, pool, wt, outer, vec, sp, spt, sbias)


STEP = 10
BETA_FIRST = 0.9
BETA_SECOND = 0.95
ADAM_EPS = 1e-08
DECAY_RATE = 0.05
RATE_MATRIX = 0.05
RATE_VECTOR = 0.8
CLIP_BOUND = 1.0
BOTH = ("dp", "fsdp")


def adam_step(weight, first, second, gradient, step_rate, weight_decay):
    first_new = BETA_FIRST * first + (1.0 - BETA_FIRST) * gradient
    second_new = BETA_SECOND * second + (1.0 - BETA_SECOND) * gradient * gradient
    first_hat = first_new / (1.0 - BETA_FIRST**STEP)
    second_hat = second_new / (1.0 - BETA_SECOND**STEP)
    weight_new = weight - step_rate * (
        first_hat / (jnp.sqrt(second_hat) + ADAM_EPS) + weight_decay * weight
    )
    return (weight_new, first_new, second_new)


def per_device(
    tokens,
    valid_mask,
    keep_mask,
    out_cotangent,
    pool_cotangent,
    inner_weight,
    outer_weight,
    vectors,
    spatial,
    inner_first,
    inner_second,
    outer_first,
    outer_second,
    vector_first,
    vector_second,
    spatial_first,
    spatial_second,
):
    images, patches, width = tokens.shape
    pad = (patches + 15) // 16 * 16
    wt = lax.all_gather(
        inner_weight.astype(BF).transpose(0, 2, 1), BOTH, axis=1, tiled=True
    )
    outer = lax.all_gather(outer_weight.astype(BF), BOTH, axis=0, tiled=True)
    vec = lax.all_gather(vectors.astype(BF), BOTH, axis=0, tiled=True)
    vec = vec.astype(F32).reshape(-1, width)
    counts = jnp.sum(valid_mask, axis=1)
    pool = (pool_cotangent.astype(F32) / counts.astype(F32)[:, None])[:, None, :]
    low = spatial[:patches].astype(BF)
    edge = ((0, pad - patches), (0, pad - patches))
    sp = jnp.pad(low, edge)
    spt = jnp.pad(low.T, edge)
    sbias = jnp.pad(spatial[patches][:, None], ((0, pad - patches), (0, 0)))
    output, input_grad, pooled, inner_g, outer_g, vec_g, sg, sbg = run_block(
        counts, keep_mask, tokens, out_cotangent, pool, wt, outer, vec, sp, spt, sbias
    )
    pooled = pooled.reshape(images, width)
    spatial_local = jnp.concatenate(
        [sg[:patches, :patches], jnp.sum(sbg[:patches], axis=1)[None, :]], axis=0
    )
    spatial_total = lax.psum(spatial_local, BOTH)
    vector_red = lax.psum_scatter(vec_g.reshape(-1), BOTH, scatter_dimension=0, tiled=True)
    inner_red = lax.psum_scatter(inner_g, BOTH, scatter_dimension=1, tiled=True)
    inner_red = inner_red.transpose(0, 2, 1)
    outer_red = lax.psum_scatter(outer_g, BOTH, scatter_dimension=0, tiled=True)
    shard_squares = (
        jnp.sum(inner_red * inner_red)
        + jnp.sum(outer_red * outer_red)
        + jnp.sum(vector_red * vector_red)
    )
    squares_total = lax.psum(shard_squares, BOTH)
    squares_total = squares_total + jnp.sum(spatial_total * spatial_total)
    grad_norm = jnp.sqrt(squares_total)
    clip_factor = CLIP_BOUND / jnp.maximum(grad_norm, CLIP_BOUND)
    inner_out = adam_step(
        inner_weight, inner_first, inner_second, inner_red * clip_factor, RATE_MATRIX, DECAY_RATE
    )
    outer_out = adam_step(
        outer_weight, outer_first, outer_second, outer_red * clip_factor, RATE_MATRIX, DECAY_RATE
    )
    vector_out = adam_step(
        vectors, vector_first, vector_second, vector_red * clip_factor, RATE_VECTOR, 0.0
    )
    row_index = jnp.arange(patches + 1)[:, None]
    spatial_rate = jnp.where(row_index < patches, RATE_MATRIX, RATE_VECTOR)
    spatial_decay = jnp.where(row_index < patches, DECAY_RATE, 0.0)
    spatial_out = adam_step(
        spatial,
        spatial_first,
        spatial_second,
        spatial_total * clip_factor,
        spatial_rate,
        spatial_decay,
    )
    return (
        (output, input_grad, pooled, grad_norm) + inner_out + outer_out + vector_out + spatial_out
    )


def solution(mesh):
    rows3 = P(BOTH, None, None)
    rows2 = P(BOTH, None)
    rows1 = P(BOTH)
    cols3 = P(None, None, BOTH)
    in_specs = (
        (rows3, rows2, rows1, rows3, rows2, cols3, rows2, rows1, P())
        + (cols3,) * 2
        + (rows2,) * 2
        + (rows1,) * 2
        + (P(),) * 2
    )
    out_specs = (
        (rows3, rows3, rows2, P()) + (cols3,) * 3 + (rows2,) * 3 + (rows1,) * 3 + (P(),) * 3
    )
    return jax.shard_map(
        per_device, mesh=mesh, in_specs=in_specs, out_specs=out_specs, check_vma=False
    )
```

```python
import functools
import jax
import jax.numpy as jnp
from jax import lax
from jax.experimental import pallas as pl
from jax.experimental.pallas import tpu as pltpu
from jax.sharding import PartitionSpec as P

NORM_EPS = 1e-05
DROP_RATE = 0.1
BF = jnp.bfloat16
F32 = jnp.float32
GELU_K = 0.7978845608
GELU_C = 0.044715
NN = (((1,), (0,)), ((), ()))
NT = (((1,), (1,)), ((), ()))
TN = (((0,), (0,)), ((), ()))


def dot(a, b, dims):
    return lax.dot_general(a, b, dims, preferred_element_type=F32)


def gelu_pair(v):
    u = v * v
    s = 0.5 * jnp.tanh(v * (GELU_K + (GELU_K * GELU_C) * u)) + 0.5
    h = v * s
    d = s + (h - h * s) * (2.0 * GELU_K + (6.0 * GELU_K * GELU_C) * u)
    return h, d


def fold8(x):
    rows = x.shape[0]
    total = x[0:8]
    for r in range(8, rows, 8):
        total = total + x[r : r + 8]
    return total


def lanes(x):
    total = x[:, 0:128]
    for c in range(128, x.shape[1], 128):
        total = total + x[:, c : c + 128]
    return total


def block_kernel(
    cfg,
    counts,
    keeps,
    tokens_hbm,
    cot_hbm,
    pool_ref,
    wt_ref,
    vec_ref,
    sp_ref,
    spt_ref,
    sbias_ref,
    out_hbm,
    ig_hbm,
    pooled_ref,
    grads_hbm,
    small_ref,
    acc,
    sg_ref,
    sbg_ref,
    off_s,
    gend_s,
    grows_s,
    x_all,
    c_all,
    normed_b,
    bg_b,
    h0_b,
    e0_b,
    mg_b,
    xm_b,
    u2_b,
    d1_b,
    stat_b,
    br_b,
    ng_b,
    h1_s,
    t_s,
    out_st,
    ig_st,
    vacc,
    in_sem,
    out_sem,
    grad_sem,
):
    images, patches, width, gate, rows_cap, tm, kw, classes = cfg
    nv = width // 512
    del nv
    cw = 256
    nj = gate // cw

    def vrow(base, j):
        start = base + j * cw
        return vec_ref[start // 512 : start // 512 + 1, start % 512 : start % 512 + cw]

    gain_one = vec_ref[0:1, :]
    shift_one = vec_ref[1:2, :]
    bias_out = vec_ref[2:3, :]
    g2_base, s2_base, b0_base, b1_base = 3 * width, 3 * width + gate, 3 * width + 2 * gate, 3 * width + 3 * gate

    def in_copies(b):
        return (
            pltpu.make_async_copy(tokens_hbm.at[b], x_all.at[b], in_sem.at[0, b]),
            pltpu.make_async_copy(cot_hbm.at[b], c_all.at[b], in_sem.at[1, b]),
        )

    for b in range(images):
        for cp in in_copies(b):
            cp.start()

    def plan(b, carry):
        group, row = carry
        need = keeps[b] * (((counts[b] + 15) // 16) * 16)
        over = (row + need > rows_cap).astype(jnp.int32)
        group = group + over
        row = jnp.where(over == 1, 0, row)
        off_s[b] = row
        row = row + need
        gend_s[group] = b + 1
        grows_s[group] = row
        return group, row

    last_group, _ = lax.fori_loop(0, images, plan, (jnp.int32(0), jnp.int32(0)))

    def zero_rows(ref, n_chunks, start):
        z = jnp.zeros((16, ref.shape[1]), ref.dtype)

        def body(i, c):
            ref[pl.ds(pl.multiple_of(start + i * 16, 16), 16), :] = z
            return c

        lax.fori_loop(0, n_chunks, body, 0)

    for ref in (normed_b, bg_b, h0_b, e0_b, mg_b, xm_b, u2_b, d1_b):
        zero_rows(ref, ref.shape[0] // 16, 0)
    vacc[...] = jnp.zeros_like(vacc)
    acc[...] = jnp.zeros_like(acc)
    sg_ref[...] = jnp.zeros_like(sg_ref)
    sbg_ref[...] = jnp.zeros_like(sbg_ref)
    stat_b[...] = jnp.zeros_like(stat_b)

    row_chunks = [(r, min(32, patches - r)) for r in range(0, patches // 16 * 16, 32)]
    row_chunks = []
    r = 0
    full = patches // 16 * 16
    while r < full:
        step = min(32, full - r)
        row_chunks.append((r, step))
        r += step
    tail = (full, patches - full) if full < patches else None

    def load_rows(ref, b, r, rs):
        return ref[b, r : r + rs, :].astype(F32)

    def norm(x):
        c = x - jnp.mean(x, axis=-1, keepdims=True)
        inv = lax.rsqrt(jnp.mean(c * c, axis=-1, keepdims=True) + NORM_EPS)
        return c * inv, inv

    def row_ids(r, rs):
        return lax.broadcasted_iota(jnp.int32, (rs, 1), 0) + r

    def scale_of(b):
        return keeps[b].astype(F32) * (1.0 / (1.0 - DROP_RATE))

    def phase_in(b):
        for cp in in_copies(b):
            cp.wait()

        @pl.when(keeps[b] == 1)
        def _():
            n = counts[b]
            o = pl.multiple_of(off_s[b], 16)
            ks = scale_of(b)
            pool = pool_ref[b]
            bsum = jnp.zeros((8, width), F32)
            for r, rs in row_chunks + ([tail] if tail else []):
                x = load_rows(x_all, b, r, rs)
                c = load_rows(c_all, b, r, rs)
                unit, _ = norm(x)
                normed = unit * gain_one + shift_one
                valid = row_ids(r, rs) < n
                og = c + jnp.where(valid, pool, 0.0)
                bg = (ks * og).astype(BF).astype(F32)
                bgm = jnp.where(valid, bg, 0.0)
                if rs % 16:
                    pad = 16 - rs
                    z = jnp.zeros((pad, width), F32)
                    normed = jnp.concatenate([normed, z], axis=0)
                    bg = jnp.concatenate([bg, z], axis=0)
                    bgm = jnp.concatenate([bgm, z], axis=0)
                    rs = 16
                bsum = bsum + fold8(bg)
                normed_b[pl.ds(o + r, rs), :] = normed.astype(BF)
                bg_b[pl.ds(o + r, rs), :] = bgm.astype(BF)
            vacc[2] += bsum

    def phase_a(t):
        r0 = pl.multiple_of(t * tm, tm)
        rows = pl.ds(r0, tm)
        nb = normed_b[rows, :]
        bgt = bg_b[rows, :]
        s1 = jnp.zeros((tm, 128), F32)
        for j in range(nj):
            cols = slice(j * cw, (j + 1) * cw)
            a1 = dot(nb, wt_ref[1, cols, :], NT) + vrow(b1_base, j)
            h1, d1 = gelu_pair(a1)
            h1_s[:, cols] = h1
            d1_b[rows, cols] = d1.astype(BF)
            s1 = s1 + lanes(h1)
        mean = jnp.sum(s1, axis=1, keepdims=True) * (1.0 / gate)
        q1 = jnp.zeros((tm, 128), F32)
        rs1 = jnp.zeros((tm, 128), F32)
        for j in range(nj):
            cols = slice(j * cw, (j + 1) * cw)
            a0 = dot(nb, wt_ref[0, cols, :], NT) + vrow(b0_base, j)
            h0, d0 = gelu_pair(a0)
            gg = dot(bgt, wt_ref[2, cols, :], NT)
            mg = gg * h0
            h0_b[rows, cols] = h0.astype(BF)
            mg_b[rows, cols] = mg.astype(BF)
            e0_b[rows, cols] = (gg * d0).astype(BF)
            rs1 = rs1 + lanes(mg)
            c = h1_s[:, cols] - mean
            q1 = q1 + lanes(c * c)
        inv = lax.rsqrt(jnp.sum(q1, axis=1, keepdims=True) * (1.0 / gate) + NORM_EPS)
        stat_b[rows, 0:128] = jnp.broadcast_to(inv, (tm, 128))
        stat_b[rows, 128:256] = rs1
        for j in range(nj):
            cols = slice(j * cw, (j + 1) * cw)
            u2 = (h1_s[:, cols] - mean) * inv
            u2_b[rows, cols] = u2.astype(BF)
            xm_b[rows, cols] = (u2 * vrow(g2_base, j) + vrow(s2_base, j)).astype(BF)

    def phase_b(b, m):
        n = counts[b]
        o = pl.multiple_of(off_s[b], 16)
        need = ((n + 15) // 16) * 16
        rows = pl.ds(o, m)
        rid = lax.broadcasted_iota(jnp.int32, (m, 1), 0)
        cid = lax.broadcasted_iota(jnp.int32, (m, m), 1)
        rid2 = lax.broadcasted_iota(jnp.int32, (m, m), 0)
        both = (cid < n) & (rid2 < n)
        sp = jnp.where(both, sp_ref[0:m, 0:m], 0.0).astype(BF)
        spt = jnp.where(both, spt_ref[0:m, 0:m], 0.0).astype(BF)
        sbias = sbias_ref[0:m, :]
        inside = rid < need
        inv = stat_b[rows, 0:1]
        tsum = jnp.zeros((m, 128), F32)
        tdot = jnp.zeros((m, 128), F32)
        sg = jnp.zeros((m, m), F32)
        for j in range(nj):
            cols = slice(j * cw, (j + 1) * cw)
            xm = xm_b[rows, cols]
            mg = mg_b[rows, cols]
            so = dot(sp, xm, NN) + sbias
            so = jnp.where(inside, so, 1.0)
            mix = dot(spt, mg, NN)
            sg = sg + dot(mg, xm, NT)
            h0_b[rows, cols] = (h0_b[rows, cols].astype(F32) * so).astype(BF)
            e0_b[rows, cols] = (e0_b[rows, cols].astype(F32) * so).astype(BF)
            u2 = u2_b[rows, cols].astype(F32)
            mu = mix * u2
            gain = vrow(g2_base, j)
            t = mix * gain
            t_s[0:m, cols] = t
            tsum = tsum + lanes(t)
            tdot = tdot + lanes(mu * gain)
            start = j * cw
            vi = start // 512
            lo = start % 512
            vacc[3 + vi, :, lo : lo + cw] += fold8(mu)
            vacc[3 + gate // 512 + vi, :, lo : lo + cw] += fold8(mix)
        sg_ref[0:m, 0:m] += jnp.where(both, sg, 0.0)
        sbg_ref[0:m, :] += jnp.where(rid < n, stat_b[rows, 128:256], 0.0)
        m1 = jnp.sum(tsum, axis=1, keepdims=True) * (1.0 / gate)
        m2 = jnp.sum(tdot, axis=1, keepdims=True) * (1.0 / gate)
        for j in range(nj):
            cols = slice(j * cw, (j + 1) * cw)
            u2 = u2_b[rows, cols].astype(F32)
            sec = inv * (t_s[0:m, cols] - m1 - u2 * m2)
            sec = jnp.where(inside, sec, 1.0)
            d1_b[rows, cols] = (d1_b[rows, cols].astype(F32) * sec).astype(BF)

    def phase_c(t):
        r0 = pl.multiple_of(t * tm, tm)
        rows = pl.ds(r0, tm)
        br_b[rows, :] = dot(h0_b[rows, :], wt_ref[2], NN)
        ng_b[rows, :] = dot(e0_b[rows, :], wt_ref[0], NN) + dot(d1_b[rows, :], wt_ref[1], NN)
        base = b0_base // 512
        for a, ref in ((0, e0_b), (1, d1_b)):
            for v in range(gate // 512):
                part = ref[rows, v * 512 : (v + 1) * 512].astype(F32)
                vacc[base + a * (gate // 512) + v] += fold8(part)

    def phase_w(k):
        rows = pl.ds(pl.multiple_of(k * kw, kw), kw)
        nb = normed_b[rows, :]
        bgt = bg_b[rows, :]
        for j in range(gate // 256):
            cols = slice(j * 256, (j + 1) * 256)
            acc[0, cols, :] += dot(e0_b[rows, cols], nb, TN)
            acc[1, cols, :] += dot(d1_b[rows, cols], nb, TN)
            acc[2, cols, :] += dot(h0_b[rows, cols], bgt, TN)

    def out_copies(b, slot):
        return (
            pltpu.make_async_copy(out_st.at[slot], out_hbm.at[b], out_sem.at[0, slot]),
            pltpu.make_async_copy(ig_st.at[slot], ig_hbm.at[b], out_sem.at[1, slot]),
        )

    def phase_d(b):
        slot = lax.rem(b, 2)

        @pl.when(b >= 2)
        def _():
            for cp in out_copies(b - 2, slot):
                cp.wait()

        n = counts[b]
        kn = keeps[b] * n
        o = pl.multiple_of(off_s[b], 16)
        ks = scale_of(b)
        pool = pool_ref[b]
        psum = jnp.zeros((8, width), F32)
        g1 = jnp.zeros((8, width), F32)
        s1 = jnp.zeros((8, width), F32)
        for r, rs in row_chunks + ([tail] if tail else []):
            x = load_rows(x_all, b, r, rs)
            c = load_rows(c_all, b, r, rs)
            unit, inv = norm(x)
            ids = row_ids(r, rs)
            valid = ids < n
            live = ids < kn
            og = c + jnp.where(valid, pool, 0.0)
            br = jnp.where(live, br_b[pl.ds(o + r, rs), :], 0.0)
            out = x + ks * (br + bias_out)
            out_st[slot, r : r + rs, :] = out
            ng = jnp.where(live, ng_b[pl.ds(o + r, rs), :], 0.0)
            t = ng * gain_one
            m1 = jnp.mean(t, axis=-1, keepdims=True)
            m2 = jnp.mean(t * unit, axis=-1, keepdims=True)
            ig_st[slot, r : r + rs, :] = og + inv * (t - m1 - unit * m2)
            ov = jnp.where(valid, out, 0.0)
            gu = ng * unit
            if rs % 8:
                z = jnp.zeros((8 - rs % 8, width), F32)
                ov = jnp.concatenate([ov, z], axis=0)
                gu = jnp.concatenate([gu, z], axis=0)
                ng = jnp.concatenate([ng, z], axis=0)
            psum = psum + fold8(ov)
            g1 = g1 + fold8(gu)
            s1 = s1 + fold8(ng)
        vacc[0] += g1
        vacc[1] += s1
        total = jnp.sum(psum, axis=0, keepdims=True)
        pooled_ref[b] = total / jnp.full((1, width), n.astype(F32), F32)
        for cp in out_copies(b, slot):
            cp.start()

    def group(g, b_start):
        b_end = gend_s[g]
        rows = grows_s[g]

        def loop(lo, hi, fn):
            def body(i, c):
                fn(i)
                return c

            lax.fori_loop(lo, hi, body, 0)

        loop(b_start, b_end, phase_in)
        zero_rows(normed_b, kw // 16, rows)
        zero_rows(bg_b, kw // 16, rows)
        tiles = (rows + tm - 1) // tm
        loop(0, tiles, phase_a)
        zero_rows(d1_b, tm // 16, rows)

        def do_b(b):
            n = counts[b]
            low = 0
            for m in classes:
                @pl.when((keeps[b] == 1) & (n > low) & (n <= m))
                def _(m=m):
                    phase_b(b, m)
                low = m

        loop(b_start, b_end, do_b)
        loop(0, tiles, phase_c)
        loop(0, (rows + kw - 1) // kw, phase_w)
        loop(b_start, b_end, phase_d)
        return b_end

    lax.fori_loop(0, last_group + 1, group, jnp.int32(0))
    for b in (images - 2, images - 1):
        for cp in out_copies(b, b % 2):
            cp.wait()
    half = gate // 2
    copies = []
    for i in range(6):
        q, lo = i // 2, (i % 2) * half
        buf = (normed_b, bg_b)[i % 2]
        if i >= 2:
            copies[i - 2].wait()
        buf[0:half, :] = acc[q, lo : lo + half, :].astype(BF)
        cp = pltpu.make_async_copy(
            buf.at[pl.ds(0, half)], grads_hbm.at[q, pl.ds(lo, half)], grad_sem.at[i]
        )
        cp.start()
        copies.append(cp)
    small_ref[...] = jnp.zeros_like(small_ref)
    sums = jnp.sum(vacc[...], axis=1)
    for v in range(sums.shape[0]):
        for h in range(width // 256):
            row = v * (width // 256) + h
            small_ref[row : row + 1, :] = sums[v : v + 1, h * 256 : (h + 1) * 256]
    sg_row = 32
    pad = sg_ref.shape[0]
    small_ref[sg_row : sg_row + pad, 0:pad] = sg_ref[...]
    bias = jnp.sum(sbg_ref[...], axis=1, keepdims=True)
    wide = jnp.where(
        lax.broadcasted_iota(jnp.int32, (pad, pad), 0) == lax.broadcasted_iota(jnp.int32, (pad, pad), 1),
        bias,
        0.0,
    )
    small_ref[sg_row + patches : sg_row + patches + 1, 0:pad] = jnp.sum(wide, axis=0, keepdims=True)
    for cp in copies[4:]:
        cp.wait()


def run_block(counts, keeps, tokens, cot, pool, wt, vec, sp, spt, sbias, *, rows_cap=1024, tm=128, kw=256, classes=(112, 160, 208)):
    images, patches, width = tokens.shape
    gate = wt.shape[1]
    pad = sp.shape[0]
    nvec = vec.shape[0]
    cap = rows_cap + 256
    cfg = (images, patches, width, gate, rows_cap, tm, kw, classes)
    smem = pl.BlockSpec(memory_space=pltpu.SMEM)
    vmem = pl.BlockSpec(memory_space=pltpu.VMEM)
    anyb = pl.BlockSpec(memory_space=pl.ANY)
    return pl.pallas_call(
        functools.partial(block_kernel, cfg),
        out_shape=(
            jax.ShapeDtypeStruct((images, patches, width), F32),
            jax.ShapeDtypeStruct((images, patches, width), F32),
            jax.ShapeDtypeStruct((images, 1, width), F32),
            jax.ShapeDtypeStruct((3, gate, width), BF),
            jax.ShapeDtypeStruct((256, 256), F32),
        ),
        in_specs=[smem, smem, anyb, anyb] + [vmem] * 6,
        out_specs=[anyb, anyb, vmem, anyb, vmem],
        scratch_shapes=[
            pltpu.VMEM((3, gate, width), F32),
            pltpu.VMEM((pad, pad), F32),
            pltpu.VMEM((pad, 128), F32),
            pltpu.SMEM((images,), jnp.int32),
            pltpu.SMEM((images,), jnp.int32),
            pltpu.SMEM((images,), jnp.int32),
            pltpu.VMEM((images, patches, width), BF),
            pltpu.VMEM((images, patches, width), BF),
            pltpu.VMEM((cap, width), BF),
            pltpu.VMEM((cap, width), BF),
        ]
        + [pltpu.VMEM((cap, gate), BF)] * 6
        + [
            pltpu.VMEM((cap, 256), F32),
            pltpu.VMEM((cap, width), F32),
            pltpu.VMEM((cap, width), F32),
            pltpu.VMEM((tm, gate), F32),
            pltpu.VMEM((pad, gate), F32),
            pltpu.VMEM((2, patches, width), F32),
            pltpu.VMEM((2, patches, width), F32),
            pltpu.VMEM((nvec, 8, width), F32),
            pltpu.SemaphoreType.DMA((2, images)),
            pltpu.SemaphoreType.DMA((2, 2)),
            pltpu.SemaphoreType.DMA((6,)),
        ],
        compiler_params=pltpu.CompilerParams(vmem_limit_bytes=60 * 2**20),
        name="block",
    )(counts, keeps, tokens, cot, pool, wt, vec, sp, spt, sbias)


MESH = pl.DeviceIdType.MESH


def place():
    d = lax.axis_index("dp")
    f = lax.axis_index("fsdp")
    return d % 2, d // 2, f // 2, f % 2


def device(x, y, z, c):
    return (y * 2 + x, z * 2 + c)


def greet_all():
    d = lax.axis_index("dp")
    f = lax.axis_index("fsdp")
    barrier = pltpu.get_barrier_semaphore()
    total = 32
    me = d * 8 + f

    def body(k, carry):
        peer = (me + k) % total
        pl.semaphore_signal(
            barrier, inc=1, device_id=(peer // 8, peer % 8), device_id_type=MESH
        )
        return carry

    lax.fori_loop(1, total, body, 0)
    pl.semaphore_wait(barrier, total - 1)


def gather_kernel(inner_ref, outer_ref, vec_ref, all_ref, vecs_ref, own, vown, send, recv, vsend, vrecv, lsem):
    x, y, z, c = place()
    own[0] = inner_ref[0].astype(BF)
    own[1] = inner_ref[1].astype(BF)
    own[2] = outer_ref[...].astype(BF)
    vown[...] = vec_ref[...].astype(BF).astype(F32)
    greet_all()
    me = (y * 2 + x) * 8 + z * 2 + c
    local = pltpu.make_async_copy(own, all_ref.at[:, y, x, z, c], lsem.at[0])
    local.start()
    vlocal = pltpu.make_async_copy(vown, vecs_ref.at[me], lsem.at[1])
    vlocal.start()

    px, py = jnp.where(c == 0, 1 - x, x), jnp.where(c == 0, y, 1 - y)
    rx, ry = jnp.where(c == 0, x, 1 - x), jnp.where(c == 0, 1 - y, y)
    dx, dy = 1 - x, 1 - y
    index = [0]

    def remote(src, dst, dev):
        k = index[0]
        index[0] += 1
        return pltpu.make_async_remote_copy(
            src_ref=src, dst_ref=dst, send_sem=send.at[k], recv_sem=recv.at[k],
            device_id=dev, device_id_type=MESH,
        )

    pnbr, rnbr, core = device(px, py, z, c), device(rx, ry, z, c), device(x, y, z, 1 - c)

    def line(q, ly, lx):
        return all_ref.at[q, ly, lx, :, c]

    def z_sends(q, src, by, bx):
        return [
            remote(src, all_ref.at[q, by, bx, z, c], device(x, y, (z + k) % 4, c)) for k in (1, 2, 3)
        ]

    def send_line(q, ly, lx, dev):
        return remote(line(q, ly, lx), line(q, ly, lx), dev)

    started = []

    def go(cps):
        for cp in cps:
            cp.start()
            started.append(cp)

    own2 = remote(own.at[2], all_ref.at[2, y, x, z, c], pnbr)
    go([own2])
    zs = {}
    for q in (0, 1):
        zs[q] = z_sends(q, own.at[q], y, x)
        go(zs[q])
    zs[2] = z_sends(2, own.at[2], y, x)
    go(zs[2])
    def vbody(k, carry):
        peer = (me + k) % 32
        pltpu.make_async_remote_copy(
            src_ref=vown, dst_ref=vecs_ref.at[me], send_sem=vsend, recv_sem=vrecv,
            device_id=(peer // 8, peer % 8), device_id_type=MESH,
        ).start()
        return carry
    lax.fori_loop(1, 32, vbody, 0)
    local.wait()
    vlocal.wait()
    own2.wait_recv()
    zp2 = z_sends(2, all_ref.at[2, py, px, z, c], py, px)
    go(zp2)
    lines_p, lines_r, lines_r2 = {}, {}, {}
    cores = []
    for q in (0, 1, 2):
        for cp in zs[q]:
            cp.wait_recv()
        if q < 2:
            lines_p[q] = send_line(q, y, x, pnbr)
            go([lines_p[q]])
        lines_r[q] = send_line(q, y, x, rnbr)
        cp = send_line(q, y, x, core)
        cores.append(cp)
        go([lines_r[q], cp])
    for q in (0, 1, 2):
        if q < 2:
            lines_p[q].wait_recv()
        else:
            for cp in zp2:
                cp.wait_recv()
        lines_r2[q] = send_line(q, py, px, rnbr)
        cp = send_line(q, py, px, core)
        cores.append(cp)
        go([lines_r2[q], cp])
    for q in (0, 1, 2):
        lines_r[q].wait_recv()
        cp = send_line(q, ry, rx, core)
        cores.append(cp)
        go([cp])
    for q in (0, 1, 2):
        lines_r2[q].wait_recv()
        cp = send_line(q, dy, dx, core)
        cores.append(cp)
        go([cp])
    for cp in cores:
        cp.wait_recv()
    for cp in started:
        cp.wait_send()
    allv = pltpu.make_async_copy(vecs_ref.at[pl.ds(0, 31)], vecs_ref.at[pl.ds(0, 31)], vrecv)
    allv.wait()
    pltpu.make_async_copy(vecs_ref.at[pl.ds(0, 31)], vecs_ref.at[pl.ds(0, 31)], vsend).wait()


NSEND = 33


def gather_all(inner, outer, vec, space=pl.ANY):
    rows, width = outer.shape
    vmem = pl.BlockSpec(memory_space=pltpu.VMEM)
    sp = pl.BlockSpec(memory_space=space)
    return pl.pallas_call(
        gather_kernel,
        out_shape=(
            jax.ShapeDtypeStruct((3, 2, 2, 4, 2, rows, width), BF),
            jax.ShapeDtypeStruct((32, 8, 128), F32),
        ),
        in_specs=[vmem] * 3,
        out_specs=[sp, sp],
        scratch_shapes=[
            pltpu.VMEM((3, rows, width), BF),
            pltpu.VMEM((8, 128), F32),
            pltpu.SemaphoreType.DMA((NSEND,)),
            pltpu.SemaphoreType.DMA((NSEND,)),
            pltpu.SemaphoreType.DMA,
            pltpu.SemaphoreType.DMA,
            pltpu.SemaphoreType.DMA((2,)),
        ],
        compiler_params=pltpu.CompilerParams(collective_id=0, has_side_effects=True, vmem_limit_bytes=40 * 2**20),
        name="gather",
    )(inner, outer, vec)


def reduce_kernel(
    g_hbm, small_ref, red_ref, tot_ref, norm_ref,
    acc, rc, rr, rp, rz, rz2, rb, stage, sbuf, sred, nbuf, nown,
    send, recv, lsem, s1s, s1r, s2s, s2r, ns, nr,
):
    x, y, z, c = place()
    me = (y * 2 + x) * 8 + z * 2 + c
    px, py = jnp.where(c == 0, 1 - x, x), jnp.where(c == 0, y, 1 - y)
    rx, ry = jnp.where(c == 0, x, 1 - x), jnp.where(c == 0, 1 - y, y)
    dx, dy = 1 - x, 1 - y
    pnbr, rnbr, core = device(px, py, z, c), device(rx, ry, z, c), device(x, y, z, 1 - c)
    lines = ((ry, rx), (dy, dx), (y, x), (py, px))
    loads = [pltpu.make_async_copy(g_hbm.at[q, :, :, :, c], acc.at[q], lsem.at[q]) for q in range(3)]
    for cp in loads:
        cp.start()
    greet_all()
    index = [0]
    started = []

    def remote(src, dst, dev):
        k = index[0]
        index[0] += 1
        cp = pltpu.make_async_remote_copy(
            src_ref=src, dst_ref=dst, send_sem=send.at[k], recv_sem=recv.at[k],
            device_id=dev, device_id_type=MESH,
        )
        cp.start()
        started.append(cp)
        return cp

    swaps = {}
    for i, (ly, lx) in enumerate(lines):
        for q in range(3):
            swaps[q, i] = None
    for i, (ly, lx) in enumerate(((dy, dx), (ry, rx), (py, px), (y, x))):
        for q in range(3):
            swaps[q, i] = remote(g_hbm.at[q, ly, lx, :, 1 - c], rc.at[q, ly, lx], core)

    def broadcast(src, dst_at, ssem, rsem):
        def body(k, carry):
            peer = (me + k) % 32
            pltpu.make_async_remote_copy(
                src_ref=src(peer), dst_ref=dst_at, send_sem=ssem, recv_sem=rsem,
                device_id=(peer // 8, peer % 8), device_id_type=MESH,
            ).start()
            return carry
        lax.fori_loop(1, 32, body, 0)

    def wait31(ref, sem):
        view = ref.at[pl.ds(0, 31)]
        pltpu.make_async_copy(view, view, sem).wait()

    broadcast(lambda p: small_ref.at[p], sbuf.at[me], s1s, s1r)
    for cp in loads:
        cp.wait()

    def add_line(q, ly, lx, ref):
        for b in range(4):
            acc[q, ly, lx, b] = (acc[q, ly, lx, b].astype(F32) + ref[b].astype(F32)).astype(BF)

    first = {}
    for q in range(3):
        swaps[q, 0].wait_recv()
        add_line(q, dy, dx, rc.at[q, dy, dx])
        first[q, 0] = remote(acc.at[q, dy, dx], rr.at[q, 0], rnbr)
    for i in (1, 2):
        for q in range(3):
            swaps[q, i].wait_recv()
    for q in range(3):
        add_line(q, ry, rx, rc.at[q, ry, rx])
        first[q, 1] = remote(acc.at[q, ry, rx], rr.at[q, 1], rnbr)
    for q in range(3):
        add_line(q, py, px, rc.at[q, py, px])
        swaps[q, 3].wait_recv()
        add_line(q, y, x, rc.at[q, y, x])
    second = {}
    for q in (2, 0, 1):
        first[q, 0].wait_recv()
        add_line(q, py, px, rr.at[q, 0])
        if q < 2:
            second[q] = remote(acc.at[q, py, px], rp.at[q], pnbr)
        else:
            second[q] = [
                remote(acc.at[q, py, px, (z + k) % 4], rz2.at[k - 1], device(x, y, (z + k) % 4, c)) for k in (1, 2, 3)
            ]
    own2 = None
    for q in (2, 0, 1):
        first[q, 1].wait_recv()
        add_line(q, y, x, rr.at[q, 1])
        if q == 2:
            own2 = [
                remote(acc.at[q, y, x, (z + k) % 4], rz.at[q, k - 1], device(x, y, (z + k) % 4, c)) for k in (1, 2, 3)
            ]
    third = {}
    for q in (0, 1):
        second[q].wait_recv()
        add_line(q, y, x, rp.at[q])
        third[q] = [
            remote(acc.at[q, y, x, (z + k) % 4], rz.at[q, k - 1], device(x, y, (z + k) % 4, c)) for k in (1, 2, 3)
        ]
    for cp in second[2]:
        cp.wait_recv()
    stage[...] = (
        acc[2, py, px, z].astype(F32) + rz2[0].astype(F32) + rz2[1].astype(F32) + rz2[2].astype(F32)
    ).astype(BF)
    last = remote(stage, rb, pnbr)
    sbuf[me] = small_ref[me]
    wait31(sbuf, s1r)
    total = sbuf[0]
    for k in range(1, 32):
        total = total + sbuf[k]
    sred[...] = total
    tot_ref[me] = total
    broadcast(lambda p: sred, tot_ref.at[me], s2s, s2r)
    sq = jnp.zeros((8, 128), F32)

    def fold(v):
        t = jnp.zeros((8, 128), F32)
        for r in range(0, v.shape[0], 8):
            for l in range(0, v.shape[1], 128):
                p = v[r : r + 8, l : l + 128]
                t = t + p * p
        return t

    sq = sq + fold(total)
    for cp in own2:
        cp.wait_recv()
    for q in (0, 1):
        for cp in third[q]:
            cp.wait_recv()
        v = (
            acc[q, y, x, z].astype(F32) + rz[q, 0].astype(F32) + rz[q, 1].astype(F32) + rz[q, 2].astype(F32)
        )
        red_ref[q] = v
        sq = sq + fold(v)
    last.wait_recv()
    v = (
        acc[2, y, x, z].astype(F32) + rz[2, 0].astype(F32) + rz[2, 1].astype(F32) + rz[2, 2].astype(F32)
    ) + rb[...].astype(F32)
    red_ref[2] = v
    sq = sq + fold(v)
    nown[...] = sq
    nbuf[me] = sq
    broadcast(lambda p: nown, nbuf.at[me], ns, nr)
    wait31(nbuf, nr)
    wait31(tot_ref, s2r)
    t = nbuf[0]
    for k in range(1, 32):
        t = t + nbuf[k]
    t = jnp.sum(jnp.sum(t, axis=0, keepdims=True), axis=1, keepdims=True)
    norm_ref[...] = jnp.broadcast_to(jnp.sqrt(t), (8, 128))
    for cp in started:
        cp.wait_send()
    wait31(sbuf, s1s)
    wait31(tot_ref, s2s)
    wait31(nbuf, ns)


NRED = 12 + 6 + 2 + 3 + 3 + 6 + 1


def reduce_all(g, small):
    rows, width = g.shape[-2:]
    vmem = pl.BlockSpec(memory_space=pltpu.VMEM)
    anyb = pl.BlockSpec(memory_space=pl.ANY)
    dma = pltpu.SemaphoreType.DMA
    blk = (rows, width)
    return pl.pallas_call(
        reduce_kernel,
        out_shape=(
            jax.ShapeDtypeStruct((3,) + blk, F32),
            jax.ShapeDtypeStruct(small.shape, F32),
            jax.ShapeDtypeStruct((8, 128), F32),
        ),
        in_specs=[anyb, vmem],
        out_specs=[vmem] * 3,
        scratch_shapes=[
            pltpu.VMEM((3, 2, 2, 4) + blk, BF),
            pltpu.VMEM((3, 2, 2, 4) + blk, BF),
            pltpu.VMEM((3, 2, 4) + blk, BF),
            pltpu.VMEM((2, 4) + blk, BF),
            pltpu.VMEM((3, 3) + blk, BF),
            pltpu.VMEM((3,) + blk, BF),
            pltpu.VMEM(blk, BF),
            pltpu.VMEM(blk, BF),
            pltpu.VMEM(small.shape, F32),
            pltpu.VMEM(small.shape[1:], F32),
            pltpu.VMEM((32, 8, 128), F32),
            pltpu.VMEM((8, 128), F32),
            dma((NRED,)), dma((NRED,)), dma((3,)),
            dma, dma, dma, dma, dma, dma,
        ],
        compiler_params=pltpu.CompilerParams(collective_id=1, has_side_effects=True, vmem_limit_bytes=40 * 2**20),
        name="reduce",
    )(g, small)


STEP = 10
BETA_FIRST = 0.9
BETA_SECOND = 0.95
ADAM_EPS = 1e-08
DECAY_RATE = 0.05
RATE_MATRIX = 0.05
RATE_VECTOR = 0.8
CLIP_BOUND = 1.0
BOTH = ("dp", "fsdp")
SPATIAL_ROW = 32


def adam_step(weight, first, second, gradient, step_rate, weight_decay):
    first_new = BETA_FIRST * first + (1.0 - BETA_FIRST) * gradient
    second_new = BETA_SECOND * second + (1.0 - BETA_SECOND) * gradient * gradient
    first_hat = first_new * (1.0 / (1.0 - BETA_FIRST**STEP))
    second_hat = second_new * (1.0 / (1.0 - BETA_SECOND**STEP))
    weight_new = weight - step_rate * (
        first_hat / (jnp.sqrt(second_hat) + ADAM_EPS) + weight_decay * weight
    )
    return (weight_new, first_new, second_new)


def adam_kernel(red, tot, norm, iw, i1, i2, ow, o1, o2, sw, s1, s2, *outs):
    clip = CLIP_BOUND / jnp.maximum(norm[0:1, 0:1], CLIP_BOUND)
    rows = ow.shape[0]
    for q in range(2):
        for r in range(0, rows, 8):
            cut = slice(r, r + 8)
            new = adam_step(
                iw[q, cut], i1[q, cut], i2[q, cut], red[q, cut] * clip, RATE_MATRIX, DECAY_RATE
            )
            for ref, val in zip(outs[0:3], new):
                ref[q, cut] = val
    for r in range(0, rows, 8):
        cut = slice(r, r + 8)
        new = adam_step(ow[cut], o1[cut], o2[cut], red[2, cut] * clip, RATE_MATRIX, DECAY_RATE)
        for ref, val in zip(outs[3:6], new):
            ref[cut] = val
    side, cols = sw.shape
    grad = tot[SPATIAL_ROW : SPATIAL_ROW + side, 0:cols] * clip
    last = lax.broadcasted_iota(jnp.int32, (side, 1), 0) == side - 1
    rate = jnp.where(last, RATE_VECTOR, RATE_MATRIX)
    decay = jnp.where(last, 0.0, DECAY_RATE)
    new = adam_step(sw[...], s1[...], s2[...], grad, rate, decay)
    for ref, val in zip(outs[6:9], new):
        ref[...] = val


def adam_all(red, tot, norm, inner, outer, spatial):
    vmem = pl.BlockSpec(memory_space=pltpu.VMEM)
    shape = lambda a: jax.ShapeDtypeStruct(a.shape, F32)
    return pl.pallas_call(
        adam_kernel,
        out_shape=tuple(shape(a) for a in inner + outer + spatial),
        in_specs=[vmem] * 12,
        out_specs=[vmem] * 9,
        compiler_params=pltpu.CompilerParams(vmem_limit_bytes=32 * 2**20),
        name="adam",
    )(red, tot, norm, *inner, *outer, *spatial)


def slow_gather(inner_t, outer_weight, vectors):
    wt = jnp.concatenate(
        [
            lax.all_gather(inner_t.astype(BF), BOTH, axis=1, tiled=True),
            lax.all_gather(outer_weight.astype(BF), BOTH, axis=0, tiled=True)[None],
        ],
        axis=0,
    )
    vec = lax.all_gather(vectors.astype(BF), BOTH, axis=0, tiled=True).astype(F32)
    return wt, vec


def slow_reduce(grads, small):
    red = lax.psum_scatter(grads.astype(F32), BOTH, scatter_dimension=1, tiled=True)
    tot = lax.psum(small, BOTH)
    squares = lax.psum(jnp.sum(red * red), BOTH) + jnp.sum(tot * tot)
    return red, tot, jnp.broadcast_to(jnp.sqrt(squares), (8, 128))


def per_device(
    fast,
    tokens,
    valid_mask,
    keep_mask,
    out_cotangent,
    pool_cotangent,
    inner_weight,
    outer_weight,
    vectors,
    spatial,
    inner_first,
    inner_second,
    outer_first,
    outer_second,
    vector_first,
    vector_second,
    spatial_first,
    spatial_second,
):
    images, patches, width = tokens.shape
    pad = (patches + 15) // 16 * 16
    own = vectors.shape[0]
    rows = outer_weight.shape[0]
    inner_t = tuple(a.transpose(0, 2, 1) for a in (inner_weight, inner_first, inner_second))
    if fast:
        wt, vec = gather_all(
            inner_t[0], outer_weight, jnp.pad(vectors, (0, 1024 - own)).reshape(8, 128)
        )
        wt = wt.reshape(3, 32 * rows, width)
        vec = vec.reshape(32, 1024)[:, :own]
    else:
        wt, vec = slow_gather(inner_t[0], outer_weight, vectors)
    vec = vec.reshape(-1, width)
    counts = jnp.sum(valid_mask, axis=1)
    pool = (pool_cotangent.astype(F32) / counts.astype(F32)[:, None])[:, None, :]
    low = spatial[:patches].astype(BF)
    edge = ((0, pad - patches), (0, pad - patches))
    sp = jnp.pad(low, edge)
    spt = jnp.pad(low.T, edge)
    sbias = jnp.pad(spatial[patches][:, None], ((0, pad - patches), (0, 0)))
    output, input_grad, pooled, grads, small = run_block(
        counts, keep_mask, tokens, out_cotangent, pool, wt, vec, sp, spt, sbias
    )
    pooled = pooled.reshape(images, width)
    if fast:
        red, tot, norm = reduce_all(
            grads.reshape(3, 2, 2, 4, 2, rows, width), small.reshape(32, 8, 256)
        )
        tot = tot.reshape(256, 256)
    else:
        red, tot, norm = slow_reduce(grads, small)
    new = adam_all(
        red,
        tot,
        norm,
        inner_t,
        (outer_weight, outer_first, outer_second),
        (spatial, spatial_first, spatial_second),
    )
    grad_norm = norm[0, 0]
    clip_factor = CLIP_BOUND / jnp.maximum(grad_norm, CLIP_BOUND)
    me = lax.axis_index("dp") * lax.axis_size("fsdp") + lax.axis_index("fsdp")
    flat = tot[: vec.size // 256].reshape(-1)
    vector_red = lax.dynamic_slice(flat, (me * own,), (own,))
    vector_out = adam_step(
        vectors, vector_first, vector_second, vector_red * clip_factor, RATE_VECTOR, 0.0
    )
    return (
        (output, input_grad, pooled, grad_norm)
        + tuple(a.transpose(0, 2, 1) for a in new[0:3])
        + tuple(new[3:6])
        + vector_out
        + tuple(new[6:9])
    )


def solution(mesh):
    fast = mesh.shape["dp"] == 4 and mesh.shape["fsdp"] == 8
    rows3 = P(BOTH, None, None)
    rows2 = P(BOTH, None)
    rows1 = P(BOTH)
    cols3 = P(None, None, BOTH)
    in_specs = (
        (rows3, rows2, rows1, rows3, rows2, cols3, rows2, rows1, P())
        + (cols3,) * 2
        + (rows2,) * 2
        + (rows1,) * 2
        + (P(),) * 2
    )
    out_specs = (
        (rows3, rows3, rows2, P()) + (cols3,) * 3 + (rows2,) * 3 + (rows1,) * 3 + (P(),) * 3
    )
    return jax.shard_map(
        functools.partial(per_device, fast),
        mesh=mesh,
        in_specs=in_specs,
        out_specs=out_specs,
        check_vma=False,
    )
```

```python
import functools

import jax
import jax.numpy as jnp
from jax import lax
from jax.experimental import pallas as pl
from jax.experimental.pallas import tpu as pltpu
from jax.sharding import PartitionSpec as P

NORM_EPS = 1e-05
DROP_RATE = 0.1
BF = jnp.bfloat16
F32 = jnp.float32
MESH = pl.DeviceIdType.MESH
GELU_K = 0.7978845608
GELU_C = 0.044715
NN = (((1,), (0,)), ((), ()))
NT = (((1,), (1,)), ((), ()))
TN = (((0,), (0,)), ((), ()))
LOT = 16
CUTS = 1


def dot(a, b, dims):
    return lax.dot_general(a, b, dims, preferred_element_type=F32)


def norm(x):
    c = x - jnp.mean(x, axis=-1, keepdims=True)
    inv = lax.rsqrt(jnp.mean(c * c, axis=-1, keepdims=True) + NORM_EPS)
    return c * inv, inv


def swap_matrix(images):
    side = LOT * images
    r = lax.broadcasted_iota(jnp.int32, (side, side), 0)
    s = lax.broadcasted_iota(jnp.int32, (side, side), 1)
    return jnp.where(s == (r % LOT) * images + r // LOT, 1.0, 0.0).astype(BF)


def unswap_matrix(images):
    side = LOT * images
    r = lax.broadcasted_iota(jnp.int32, (side, side), 0)
    s = lax.broadcasted_iota(jnp.int32, (side, side), 1)
    return jnp.where(s == (r % images) * LOT + r // images, 1.0, 0.0).astype(BF)


def place():
    d = lax.axis_index("dp")
    f = lax.axis_index("fsdp")
    return d % 2, d // 2, f // 2, f % 2


def device(x, y, z, c):
    return (y * 2 + x, z * 2 + c)


def greet_all():
    me = lax.axis_index("dp") * 8 + lax.axis_index("fsdp")
    barrier = pltpu.get_barrier_semaphore()

    def body(k, carry):
        peer = (me + k) % 32
        pl.semaphore_signal(
            barrier, inc=1, device_id=(peer // 8, peer % 8), device_id_type=MESH
        )
        return carry

    lax.fori_loop(1, 32, body, 0)
    pl.semaphore_wait(barrier, 31)


def gather_kernel(
    own_len,
    inner_ref, outer_ref, vec_ref, tokens_hbm, cot_hbm, mask_ref, keep_ref, pool_ref, spatial_ref,
    all_ref, vecs_ref, nm_ref, bg_ref, info_ref, poolc_ref, bsum_ref, sp_ref, spt_ref, sbias_ref,
    own, vown, vgot, wide, xblk, cblk, nrow, brow, send, recv, vsend, vrecv, lsem, isem,
):
    x, y, z, c = place()
    patches, images, width = tokens_hbm.shape
    own[0] = inner_ref[0].astype(BF)
    own[1] = inner_ref[1].astype(BF)
    own[2] = outer_ref[...].astype(BF)
    vown[...] = vec_ref[...].astype(BF).astype(F32)
    loads = [
        pltpu.make_async_copy(tokens_hbm, xblk, isem.at[0]),
        pltpu.make_async_copy(cot_hbm, cblk, isem.at[1]),
    ]
    for cp in loads:
        cp.start()
    greet_all()
    me = (y * 2 + x) * 8 + z * 2 + c
    local = pltpu.make_async_copy(own, all_ref.at[:, y, x, z, c], lsem)
    local.start()
    vgot[me] = vown[...]

    px, py = jnp.where(c == 0, 1 - x, x), jnp.where(c == 0, y, 1 - y)
    rx, ry = jnp.where(c == 0, x, 1 - x), jnp.where(c == 0, 1 - y, y)
    dx, dy = 1 - x, 1 - y
    index = [0]
    pnbr, rnbr, core = device(px, py, z, c), device(rx, ry, z, c), device(x, y, z, 1 - c)
    cut = outer_ref.shape[0] // CUTS
    started = []

    def remote(src, dst, dev):
        k = index[0]
        index[0] += 1
        cp = pltpu.make_async_remote_copy(
            src_ref=src, dst_ref=dst, send_sem=send.at[k], recv_sem=recv.at[k],
            device_id=dev, device_id_type=MESH,
        )
        cp.start()
        started.append(cp)
        return cp

    def span(s):
        return pl.ds(s * cut, cut)

    def block(q, s, by, bx):
        return all_ref.at[q, by, bx, z, c, span(s)]

    def z_sends(src, q, s, by, bx):
        return [remote(src, block(q, s, by, bx), device(x, y, (z + k) % 4, c)) for k in (1, 2, 3)]

    def send_line(q, s, ly, lx, dev):
        ref = all_ref.at[q, ly, lx, :, c, span(s)]
        return remote(ref, ref, dev)

    def vbody(k, carry):
        peer = (me + k) % 32
        pltpu.make_async_remote_copy(
            src_ref=vown, dst_ref=vgot.at[me], send_sem=vsend, recv_sem=vrecv,
            device_id=(peer // 8, peer % 8), device_id_type=MESH,
        ).start()
        return carry

    lax.fori_loop(1, 32, vbody, 0)
    cuts = [(q, s) for s in range(CUTS) for q in range(3)]
    zs = [None] * len(cuts)

    def start_z(k):
        if k < len(cuts):
            q, s = cuts[k]
            zs[k] = z_sends(own.at[q, span(s)], q, s, y, x)

    for k in range(WINDOW):
        start_z(k)
    local.wait()

    counts = jnp.sum(mask_ref[...], axis=1, keepdims=True)
    keeps = keep_ref[...]
    scale = keeps.astype(F32) * (1.0 / (1.0 - DROP_RATE))
    lane = lax.broadcasted_iota(jnp.int32, info_ref.shape, 1)
    info_ref[...] = jnp.where(lane == 0, counts, keeps)
    poolc = pool_ref[...].astype(F32) / counts.astype(F32)
    poolc_ref[...] = poolc
    side = spatial_ref.shape[1]
    wide[...] = jnp.zeros_like(wide)
    wide[0 : side + 1, 0:side] = spatial_ref[...]
    mat = wide[...]
    mat_t = mat.T
    span_a = lax.broadcasted_iota(jnp.int32, mat.shape, 0)
    span_b = lax.broadcasted_iota(jnp.int32, mat.shape, 1)
    sp_ref[...] = jnp.where(span_a < side, mat, 0.0).astype(BF)
    spt_ref[...] = jnp.where(span_b < side, mat_t, 0.0).astype(BF)
    sbias_ref[...] = mat_t[:, side : side + 1]
    bsum_ref[...] = jnp.zeros_like(bsum_ref)
    vecs_ref[...] = jnp.zeros_like(vecs_ref)

    def stack_vectors():
        view = vgot.at[pl.ds(0, 31)]
        pltpu.make_async_copy(view, view, vrecv).wait()
        per = width // 128
        for d in range(32):
            start = own_len * d
            shift = start % 128
            row = jnp.concatenate(
                [jnp.broadcast_to(vgot[d, i : i + 1, :], (8, 128)) for i in range(3)], axis=1
            )
            row = pltpu.roll(row, shift, 1) if shift else row
            for i in range(3):
                r = start // 128 + i
                if r * 128 < start + own_len:
                    at = (slice(r // per, r // per + 1), slice(r % per * 128, r % per * 128 + 128))
                    vecs_ref[at] += row[0:1, i * 128 : i * 128 + 128]

    swap = swap_matrix(images)

    def token_block(k, many):
        gain, shift = vecs_ref[0:1, :], vecs_ref[1:2, :]
        for p in range(many):
            patch = k * LOT + p
            xv = xblk[patch].astype(F32)
            unit, _ = norm(xv)
            nrow[p * images : (p + 1) * images, :] = (unit * gain + shift).astype(BF)
            live = jnp.where(counts > patch, 1.0, 0.0)
            og = cblk[patch].astype(F32) + live * poolc
            bg = (scale * og).astype(BF).astype(F32)
            bsum_ref[...] += bg
            brow[p * images : (p + 1) * images, :] = (live * bg).astype(BF)
        part = swap[:, 0 : many * images]
        for src, dst in ((nrow, nm_ref), (brow, bg_ref)):
            moved = dot(part, src[0 : many * images, :], NN).astype(BF)
            at = pl.ds(pl.multiple_of(k * LOT, LOT), LOT)
            dst[:, at, :] = moved.reshape(images, LOT, width)

    full = patches // LOT
    todo = list(range(full + (1 if patches % LOT else 0)))

    def some_tokens(many):
        for _ in range(many):
            if todo:
                k = todo.pop(0)
                token_block(k, LOT if k < full else patches % LOT)

    lines_p, lines_r, lines_r2, cores = {}, {}, {}, []

    def stage_two(k):
        q, s = cuts[k]
        for cp in zs[k]:
            cp.wait_recv()
        start_z(k + WINDOW)
        lines_p[k] = send_line(q, s, y, x, pnbr)
        lines_r[k] = send_line(q, s, y, x, rnbr)
        cores.append(send_line(q, s, y, x, core))

    def stage_three(k):
        q, s = cuts[k]
        lines_p[k].wait_recv()
        lines_r2[k] = send_line(q, s, py, px, rnbr)
        cores.append(send_line(q, s, py, px, core))

    def stage_four(k):
        q, s = cuts[k]
        lines_r[k].wait_recv()
        cores.append(send_line(q, s, ry, rx, core))

    def stage_five(k):
        q, s = cuts[k]
        lines_r2[k].wait_recv()
        cores.append(send_line(q, s, dy, dx, core))

    n = len(cuts)
    for t in range(n + 3):
        if t < n:
            stage_two(t)
        if 0 <= t - 1 < n:
            stage_three(t - 1)
            stage_four(t - 1)
        if 0 <= t - 2 < n:
            stage_five(t - 2)
        if t == 1:
            stack_vectors()
            for cp in loads:
                cp.wait()
        if t >= 1:
            some_tokens(2)
    some_tokens(len(todo))
    for cp in cores:
        cp.wait_recv()
    for cp in started:
        cp.wait_send()
    view = vgot.at[pl.ds(0, 31)]
    pltpu.make_async_copy(view, view, vsend).wait()


NSEND = 30 * CUTS
WINDOW = 3


def gather_all(own_len, inner, outer, vec, tokens, cot, mask, keep, pool, spatial):
    rows, width = outer.shape
    patches, images, _ = tokens.shape
    pad = -(-patches // LOT) * LOT
    vmem = pl.BlockSpec(memory_space=pltpu.VMEM)
    anyb = pl.BlockSpec(memory_space=pl.ANY)
    dma = pltpu.SemaphoreType.DMA
    shape = jax.ShapeDtypeStruct
    return pl.pallas_call(
        functools.partial(gather_kernel, own_len),
        out_shape=(
            shape((3, 2, 2, 4, 2, rows, width), BF),
            shape((16, width), F32),
            shape((images, pad, width), BF),
            shape((images, pad, width), BF),
            shape((images, 128), jnp.int32),
            shape((images, width), F32),
            shape((images, width), F32),
            shape((256, 256), BF),
            shape((256, 256), BF),
            shape((256, 1), F32),
        ),
        in_specs=[vmem] * 3 + [anyb] * 2 + [vmem] * 4,
        out_specs=[anyb] + [vmem] * 9,
        scratch_shapes=[
            pltpu.VMEM((3, rows, width), BF),
            pltpu.VMEM((8, 128), F32),
            pltpu.VMEM((32, 8, 128), F32),
            pltpu.VMEM((256, 256), F32),
            pltpu.VMEM((patches, images, width), BF),
            pltpu.VMEM((patches, images, width), BF),
            pltpu.VMEM((LOT * images, width), BF),
            pltpu.VMEM((LOT * images, width), BF),
            dma((NSEND,)), dma((NSEND,)), dma, dma, dma, dma((2,)),
        ],
        compiler_params=pltpu.CompilerParams(
            collective_id=0, has_side_effects=True, vmem_limit_bytes=60 * 2**20
        ),
        name="gather",
    )(inner, outer, vec, tokens, cot, mask, keep, pool, spatial)


def gelu_pair(v):
    u = v * v
    s = 0.5 * jnp.tanh(v * (GELU_K + (GELU_K * GELU_C) * u)) + 0.5
    h = v * s
    d = s + (h - h * s) * (2.0 * GELU_K + (6.0 * GELU_K * GELU_C) * u)
    return h, d


def fold8(x):
    total = x[0:8]
    for r in range(8, x.shape[0], 8):
        total = total + x[r : r + 8]
    return total


def lanes(x):
    total = x[:, 0:128]
    for c in range(128, x.shape[1], 128):
        total = total + x[:, c : c + 128]
    return total


def loop(lo, hi, fn):
    def body(i, c):
        fn(i)
        return c

    lax.fori_loop(lo, hi, body, 0)


def block_kernel(
    cfg,
    info_s,
    tokens_hbm, cot_hbm, nm_hbm, bg_hbm,
    info_ref, poolc_ref, bsum_ref, wt_ref, vec_ref, sp_ref, spt_ref, sbias_ref,
    out_hbm, ig_hbm, pooled_ref, grads_hbm, small_ref,
    acc, sg_ref, sbg_ref, off_s, gend_s, grows_s,
    wtt, nm_b, bg_b, h0_b, e0_b, mg_b, xm_b, u2_b, d1_b, stat_b, h1_s, t_s,
    xblk, cblk, br_s, ng_s, out_st, ig_st, vacc,
    pack_sem, in_sem, out_sem, grad_sem,
):
    images, patches, width, gate, rows_cap, tm, kw, classes = cfg
    cw = 256
    nj = gate // cw
    chunks = -(-patches // LOT)
    zero_row = nm_b.shape[0] - LOT
    g2_base, s2_base = 3 * width, 3 * width + gate
    b0_base, b1_base = 3 * width + 2 * gate, 3 * width + 3 * gate

    def vrow(base, j):
        start = base + j * cw
        return vec_ref[start // width : start // width + 1, start % width : start % width + cw]

    def count(b):
        return info_s[b, 0]

    def keep(b):
        return info_s[b, 1]

    def need_of(b):
        return keep(b) * ((count(b) + LOT - 1) // LOT)

    def plan(b, carry):
        group, row, first = carry
        need = need_of(b) * LOT
        over = row + need - first > rows_cap
        group = group + over.astype(jnp.int32)
        first = jnp.where(over, row, first)
        off_s[b] = row
        row = row + need
        gend_s[group] = b + 1
        grows_s[group] = row - first
        return group, row, first

    zero = jnp.int32(0)
    last_group, all_rows, _ = lax.fori_loop(0, images, plan, (zero, zero, zero))

    def pack(b, act):
        lots = need_of(b)
        o = off_s[b]
        done = jnp.int32(0)
        for size in (8, 4, 2, 1):
            @pl.when((lots & size) != 0)
            def _(size=size, done=done):
                src = pl.ds(pl.multiple_of(done * LOT, LOT), size * LOT)
                dst = pl.ds(pl.multiple_of(o + done * LOT, LOT), size * LOT)
                for i, (far, near) in enumerate(((nm_hbm, nm_b), (bg_hbm, bg_b))):
                    act(pltpu.make_async_copy(far.at[b, src], near.at[dst], pack_sem.at[i, b]))

            done = done + (lots & size)

    loop(0, images, lambda b: pack(b, lambda cp: cp.start()))

    full = patches // LOT
    rest = patches % LOT

    def load_lot(k, many, slot):
        at = pl.ds(k * LOT, many)
        return (
            pltpu.make_async_copy(tokens_hbm.at[at], xblk.at[slot, pl.ds(0, many)], in_sem.at[0, slot]),
            pltpu.make_async_copy(cot_hbm.at[at], cblk.at[slot, pl.ds(0, many)], in_sem.at[1, slot]),
        )

    for k in (0, 1):
        for cp in load_lot(k, LOT, k):
            cp.start()

    for q in range(3):
        for j in range(nj):
            wtt[q, :, j * cw : (j + 1) * cw] = wt_ref[q, j * cw : (j + 1) * cw, :].T

    def zero_rows(ref, n_chunks, start):
        z = jnp.zeros((LOT, ref.shape[1]), ref.dtype)

        def body(i):
            ref[pl.ds(pl.multiple_of(start + i * LOT, LOT), LOT), :] = z

        loop(0, n_chunks, body)

    for ref in (mg_b, xm_b, u2_b):
        zero_rows(ref, ref.shape[0] // LOT, 0)
    for ref in (nm_b, bg_b):
        zero_rows(ref, tm // LOT, all_rows)
    z = jnp.zeros((LOT, width), BF)
    nm_b[zero_row : zero_row + LOT, :] = z
    bg_b[zero_row : zero_row + LOT, :] = z
    vacc[...] = jnp.zeros_like(vacc)
    acc[...] = jnp.zeros_like(acc)
    sg_ref[...] = jnp.zeros_like(sg_ref)
    sbg_ref[...] = jnp.zeros_like(sbg_ref)
    loop(0, images, lambda b: pack(b, lambda cp: cp.wait()))

    def phase_a(t, gs):
        r0 = pl.multiple_of(t * tm, tm)
        rows = pl.ds(r0, tm)
        here = pl.ds(pl.multiple_of(gs + r0, LOT), tm)
        nb = nm_b[here, :]
        bgt = bg_b[here, :]
        s1 = jnp.zeros((tm, 128), F32)
        for j in range(nj):
            cols = slice(j * cw, (j + 1) * cw)
            a1 = dot(nb, wtt[1, :, cols], NN) + vrow(b1_base, j)
            h1, d1 = gelu_pair(a1)
            h1_s[:, cols] = h1
            d1_b[rows, cols] = d1.astype(BF)
            s1 = s1 + lanes(h1)
        mean = jnp.sum(s1, axis=1, keepdims=True) * (1.0 / gate)
        q1 = jnp.zeros((tm, 128), F32)
        rs1 = jnp.zeros((tm, 128), F32)
        for j in range(nj):
            cols = slice(j * cw, (j + 1) * cw)
            a0 = dot(nb, wtt[0, :, cols], NN) + vrow(b0_base, j)
            h0, d0 = gelu_pair(a0)
            gg = dot(bgt, wtt[2, :, cols], NN)
            mg = gg * h0
            h0_b[rows, cols] = h0.astype(BF)
            mg_b[rows, cols] = mg.astype(BF)
            e0_b[rows, cols] = (gg * d0).astype(BF)
            rs1 = rs1 + lanes(mg)
            c = h1_s[:, cols] - mean
            q1 = q1 + lanes(c * c)
        inv = lax.rsqrt(jnp.sum(q1, axis=1, keepdims=True) * (1.0 / gate) + NORM_EPS)
        stat_b[rows, 0:128] = jnp.broadcast_to(inv, (tm, 128))
        stat_b[rows, 128:256] = rs1
        for j in range(nj):
            cols = slice(j * cw, (j + 1) * cw)
            u2 = (h1_s[:, cols] - mean) * inv
            u2_b[rows, cols] = u2.astype(BF)
            xm_b[rows, cols] = (u2 * vrow(g2_base, j) + vrow(s2_base, j)).astype(BF)

    def phase_b(b, m, gs):
        n = count(b)
        o = pl.multiple_of(off_s[b] - gs, LOT)
        rows = pl.ds(o, m)
        rid = lax.broadcasted_iota(jnp.int32, (m, 1), 0)
        cid = lax.broadcasted_iota(jnp.int32, (m, m), 1)
        rid2 = lax.broadcasted_iota(jnp.int32, (m, m), 0)
        both = (cid < n) & (rid2 < n)
        sp = jnp.where(both, sp_ref[0:m, 0:m], 0.0).astype(BF)
        spt = jnp.where(both, spt_ref[0:m, 0:m], 0.0).astype(BF)
        sbias = sbias_ref[0:m, :]
        valid = rid < n
        fill = jnp.where(rid < need_of(b) * LOT, 0.0, 1.0)
        inv = stat_b[rows, 0:1]
        tsum = jnp.zeros((m, 128), F32)
        tdot = jnp.zeros((m, 128), F32)
        sg = jnp.zeros((m, m), F32)
        for j in range(nj):
            cols = slice(j * cw, (j + 1) * cw)
            xm = xm_b[rows, cols]
            mg = mg_b[rows, cols]
            so = dot(sp, xm, NN) + sbias
            so = jnp.where(valid, so, fill)
            mix = dot(spt, mg, NN)
            sg = sg + dot(mg, xm, NT)
            h0_b[rows, cols] = (h0_b[rows, cols].astype(F32) * so).astype(BF)
            e0_b[rows, cols] = (e0_b[rows, cols].astype(F32) * so).astype(BF)
            u2 = u2_b[rows, cols].astype(F32)
            mu = mix * u2
            gain = vrow(g2_base, j)
            t = mix * gain
            t_s[0:m, cols] = t
            tsum = tsum + lanes(t)
            tdot = tdot + lanes(mu * gain)
            vi, lo = j * cw // width, j * cw % width
            vacc[g2_base // width + vi, :, lo : lo + cw] += fold8(mu)
            vacc[s2_base // width + vi, :, lo : lo + cw] += fold8(mix)
        sg_ref[0:m, 0:m] += jnp.where(both, sg, 0.0)
        sbg_ref[0:m, :] += jnp.where(valid, stat_b[rows, 128:256], 0.0)
        m1 = jnp.sum(tsum, axis=1, keepdims=True) * (1.0 / gate)
        m2 = jnp.sum(tdot, axis=1, keepdims=True) * (1.0 / gate)
        for j in range(nj):
            cols = slice(j * cw, (j + 1) * cw)
            u2 = u2_b[rows, cols].astype(F32)
            sec = inv * (t_s[0:m, cols] - m1 - u2 * m2)
            sec = jnp.where(valid, sec, fill)
            d1_b[rows, cols] = (d1_b[rows, cols].astype(F32) * sec).astype(BF)

    def phase_w(k, gs):
        r0 = pl.multiple_of(k * kw, kw)
        rows = pl.ds(r0, kw)
        here = pl.ds(pl.multiple_of(gs + r0, LOT), kw)
        nb = nm_b[here, :]
        bgt = bg_b[here, :]
        for j in range(gate // 256):
            cols = slice(j * 256, (j + 1) * 256)
            acc[0, cols, :] += dot(e0_b[rows, cols], nb, TN)
            acc[1, cols, :] += dot(d1_b[rows, cols], nb, TN)
            acc[2, cols, :] += dot(h0_b[rows, cols], bgt, TN)

    def phase_c(t, gs, group_rows):
        r0 = pl.multiple_of(t * tm, tm)
        rows = pl.ds(r0, tm)
        here = pl.ds(pl.multiple_of(gs + r0, LOT), tm)
        mine = lax.broadcasted_iota(jnp.int32, (tm, 1), 0) < group_rows - r0
        br = dot(h0_b[rows, :], wt_ref[2], NN)
        bg_b[here, :] = jnp.where(mine, br, bg_b[here, :].astype(F32)).astype(BF)
        ng = dot(e0_b[rows, :], wt_ref[0], NN) + dot(d1_b[rows, :], wt_ref[1], NN)
        nm_b[here, :] = jnp.where(mine, ng, nm_b[here, :].astype(F32)).astype(BF)
        for base, ref in ((b0_base // width, e0_b), (b1_base // width, d1_b)):
            for v in range(gate // width):
                vacc[base + v] += fold8(ref[rows, v * width : (v + 1) * width].astype(F32))

    def group(g, carry):
        b_start, gs = carry
        b_end = gend_s[g]
        rows = grows_s[g]
        tiles = (rows + tm - 1) // tm
        loop(0, tiles, lambda t: phase_a(t, gs))

        def do_b(b):
            low = 0
            for m in classes:
                @pl.when((keep(b) == 1) & (count(b) > low) & (count(b) <= m))
                def _(m=m):
                    phase_b(b, m, gs)

                low = m

        loop(b_start, b_end, do_b)
        tail = (tiles * tm - rows) // LOT
        for ref in (h0_b, e0_b, d1_b):
            zero_rows(ref, tail, rows)
        loop(0, (rows + kw - 1) // kw, lambda k: phase_w(k, gs))
        loop(0, tiles, lambda t: phase_c(t, gs, rows))
        return b_end, gs + rows

    lax.fori_loop(0, last_group + 1, group, (zero, zero))

    half = gate // 2
    grad_out = []
    per = gate // width
    for i in range(6):
        q, lo = i // 2, (i % 2) * half
        buf = (h1_s, t_s)[0]
        del buf
        stage = (mg_b, xm_b)[i % 2]
        if i >= 2:
            for cp in grad_out[i - 2]:
                cp.wait()
        cps = []
        for v in range(per):
            third = half // per
            cut = slice(v * width, (v + 1) * width)
            stage[0:third, cut] = acc[q, lo + v * third : lo + (v + 1) * third, :].astype(BF)
            cps.append(
                pltpu.make_async_copy(
                    stage.at[pl.ds(0, third), pl.ds(v * width, width)],
                    grads_hbm.at[q, pl.ds(lo + v * third, third)],
                    grad_sem.at[i, v],
                )
            )
        for cp in cps:
            cp.start()
        grad_out.append(cps)

    counts = info_ref[:, 0:1]
    live_counts = counts * info_ref[:, 1:2]
    scale = info_ref[:, 1:2].astype(F32) * (1.0 / (1.0 - DROP_RATE))
    poolc = poolc_ref[...]
    gain_one, bias_out = vec_ref[0:1, :], vec_ref[2:3, :]
    back = unswap_matrix(images)

    def store_lot(k, many, slot):
        at = pl.ds(k * LOT, many)
        return (
            pltpu.make_async_copy(out_st.at[slot, pl.ds(0, many)], out_hbm.at[at], out_sem.at[0, slot]),
            pltpu.make_async_copy(ig_st.at[slot, pl.ds(0, many)], ig_hbm.at[at], out_sem.at[1, slot]),
        )

    pooled_ref[...] = jnp.zeros_like(pooled_ref)

    def lot(k, many, slot):
        for cp in load_lot(k, many, slot):
            cp.wait()
        parts = [[], []]
        for b in range(images):
            there = k < need_of(b)
            row = pl.multiple_of(jnp.where(there, off_s[b] + k * LOT, zero_row), LOT)
            parts[0].append(bg_b[pl.ds(row, LOT), :])
            parts[1].append(nm_b[pl.ds(row, LOT), :])
        mat = back[0 : many * images, :]
        br_s[0 : many * images, :] = dot(mat, jnp.concatenate(parts[0], axis=0), NN)
        ng_s[0 : many * images, :] = dot(mat, jnp.concatenate(parts[1], axis=0), NN)
        psum = jnp.zeros((images, width), F32)
        g1 = jnp.zeros((images, width), F32)
        s1 = jnp.zeros((images, width), F32)
        for p in range(many):
            patch = k * LOT + p
            x = xblk[slot, p].astype(F32)
            unit, inv = norm(x)
            live = jnp.where(counts > patch, 1.0, 0.0)
            og = cblk[slot, p].astype(F32) + live * poolc
            cut = slice(p * images, (p + 1) * images)
            out = x + scale * (br_s[cut, :] + bias_out)
            out_st[slot, p] = out
            psum = psum + live * out
            ng = ng_s[cut, :]
            t = ng * gain_one
            m1 = jnp.mean(t, axis=-1, keepdims=True)
            m2 = jnp.mean(t * unit, axis=-1, keepdims=True)
            ig_st[slot, p] = og + inv * (t - m1 - unit * m2)
            g1 = g1 + ng * unit
            s1 = s1 + ng
        pooled_ref[...] += psum
        vacc[0] += fold8(g1)
        vacc[1] += fold8(s1)
        for cp in store_lot(k, many, slot):
            cp.start()

    def lots(k):
        slot = lax.rem(k, 2)

        @pl.when(k >= 2)
        def _():
            for cp in store_lot(k - 2, LOT, slot):
                cp.wait()

        lot(k, LOT, slot)

        @pl.when(k + 2 < full)
        def _():
            for cp in load_lot(k + 2, LOT, slot):
                cp.start()

        if rest:
            @pl.when(k + 2 == full)
            def _():
                for cp in load_lot(full, rest, full % 2):
                    cp.start()

    loop(0, full, lots)
    if rest:
        for cp in store_lot(full - 2, LOT, full % 2):
            cp.wait()
        lot(full, rest, full % 2)
    pooled_ref[...] = pooled_ref[...] / counts.astype(F32)

    vacc[2] += fold8(bsum_ref[...])
    small_ref[...] = jnp.zeros_like(small_ref)
    sums = jnp.sum(vacc[...], axis=1)
    for v in range(sums.shape[0]):
        for h in range(width // 256):
            row = v * (width // 256) + h
            small_ref[row : row + 1, :] = sums[v : v + 1, h * 256 : (h + 1) * 256]
    pad = sg_ref.shape[0]
    small_ref[SPATIAL_ROW : SPATIAL_ROW + pad, 0:pad] = sg_ref[...]
    bias = jnp.sum(sbg_ref[...], axis=1, keepdims=True)
    eye = lax.broadcasted_iota(jnp.int32, (pad, pad), 0) == lax.broadcasted_iota(jnp.int32, (pad, pad), 1)
    bias_row = jnp.sum(jnp.where(eye, bias, 0.0), axis=0, keepdims=True)
    small_ref[SPATIAL_ROW + patches : SPATIAL_ROW + patches + 1, 0:pad] = bias_row
    for cps in grad_out[4:]:
        for cp in cps:
            cp.wait()
    if rest:
        for cp in store_lot(full - 1, LOT, (full - 1) % 2) + store_lot(full, rest, full % 2):
            cp.wait()
    else:
        for k in (full - 2, full - 1):
            for cp in store_lot(k, LOT, k % 2):
                cp.wait()


SPATIAL_ROW = 32


def run_block(
    tokens, cot, nm, bg, info, poolc, bsum, wt, vec, sp, spt, sbias,
    *, rows_cap=1024, tm=256, kw=256, classes=(112, 160, 208),
):
    patches, images, width = tokens.shape
    gate = wt.shape[1]
    pad = -(-patches // LOT) * LOT
    classes = tuple(m for m in classes if m < pad) + (pad,)
    cap = rows_cap + pad + 48
    cap = -(-cap // tm) * tm
    long = images * pad + tm + LOT
    cfg = (images, patches, width, gate, rows_cap, tm, kw, classes)
    smem = pl.BlockSpec(memory_space=pltpu.SMEM)
    vmem = pl.BlockSpec(memory_space=pltpu.VMEM)
    anyb = pl.BlockSpec(memory_space=pl.ANY)
    dma = pltpu.SemaphoreType.DMA
    shape = jax.ShapeDtypeStruct
    nvec = 3 + 4 * gate // width
    return pl.pallas_call(
        functools.partial(block_kernel, cfg),
        out_shape=(
            shape((patches, images, width), F32),
            shape((patches, images, width), F32),
            shape((images, width), F32),
            shape((3, gate, width), BF),
            shape((256, 256), F32),
        ),
        in_specs=[smem] + [anyb] * 4 + [vmem] * 8,
        out_specs=[anyb, anyb, vmem, anyb, vmem],
        scratch_shapes=[
            pltpu.VMEM((3, gate, width), F32),
            pltpu.VMEM((pad, pad), F32),
            pltpu.VMEM((pad, 128), F32),
            pltpu.SMEM((images,), jnp.int32),
            pltpu.SMEM((images,), jnp.int32),
            pltpu.SMEM((images,), jnp.int32),
            pltpu.VMEM((3, width, gate), BF),
            pltpu.VMEM((long, width), BF),
            pltpu.VMEM((long, width), BF),
        ]
        + [pltpu.VMEM((cap, gate), BF)] * 6
        + [
            pltpu.VMEM((cap, 256), F32),
            pltpu.VMEM((tm, gate), F32),
            pltpu.VMEM((pad, gate), F32),
            pltpu.VMEM((2, LOT, images, width), BF),
            pltpu.VMEM((2, LOT, images, width), BF),
            pltpu.VMEM((LOT * images, width), F32),
            pltpu.VMEM((LOT * images, width), F32),
            pltpu.VMEM((2, LOT, images, width), F32),
            pltpu.VMEM((2, LOT, images, width), F32),
            pltpu.VMEM((nvec, 8, width), F32),
            dma((2, images)),
            dma((2, 2)),
            dma((2, 2)),
            dma((6, gate // width)),
        ],
        compiler_params=pltpu.CompilerParams(vmem_limit_bytes=60 * 2**20),
        name="block",
    )(info, tokens, cot, nm, bg, info, poolc, bsum, wt, vec, sp, spt, sbias)


def reduce_kernel(
    g_hbm, small_ref, red_ref, tot_ref, norm_ref,
    acc, rc, rr, rp, rz, rz2, rb, stage, sbuf, sred, nbuf, nown,
    send, recv, lsem, s1s, s1r, s2s, s2r, ns, nr,
):
    x, y, z, c = place()
    me = (y * 2 + x) * 8 + z * 2 + c
    px, py = jnp.where(c == 0, 1 - x, x), jnp.where(c == 0, y, 1 - y)
    rx, ry = jnp.where(c == 0, x, 1 - x), jnp.where(c == 0, 1 - y, y)
    dx, dy = 1 - x, 1 - y
    pnbr, rnbr, core = device(px, py, z, c), device(rx, ry, z, c), device(x, y, z, 1 - c)
    lines = ((ry, rx), (dy, dx), (y, x), (py, px))
    loads = [pltpu.make_async_copy(g_hbm.at[q, :, :, :, c], acc.at[q], lsem.at[q]) for q in range(3)]
    for cp in loads:
        cp.start()
    greet_all()
    index = [0]
    started = []

    def remote(src, dst, dev):
        k = index[0]
        index[0] += 1
        cp = pltpu.make_async_remote_copy(
            src_ref=src, dst_ref=dst, send_sem=send.at[k], recv_sem=recv.at[k],
            device_id=dev, device_id_type=MESH,
        )
        cp.start()
        started.append(cp)
        return cp

    swaps = {}
    for i, (ly, lx) in enumerate(lines):
        for q in range(3):
            swaps[q, i] = None
    for i, (ly, lx) in enumerate(((dy, dx), (ry, rx), (py, px), (y, x))):
        for q in range(3):
            swaps[q, i] = remote(g_hbm.at[q, ly, lx, :, 1 - c], rc.at[q, ly, lx], core)

    def broadcast(src, dst_at, ssem, rsem):
        def body(k, carry):
            peer = (me + k) % 32
            pltpu.make_async_remote_copy(
                src_ref=src(peer), dst_ref=dst_at, send_sem=ssem, recv_sem=rsem,
                device_id=(peer // 8, peer % 8), device_id_type=MESH,
            ).start()
            return carry
        lax.fori_loop(1, 32, body, 0)

    def wait31(ref, sem):
        view = ref.at[pl.ds(0, 31)]
        pltpu.make_async_copy(view, view, sem).wait()

    broadcast(lambda p: small_ref.at[p], sbuf.at[me], s1s, s1r)
    for cp in loads:
        cp.wait()

    def add_line(q, ly, lx, ref):
        for b in range(4):
            acc[q, ly, lx, b] = (acc[q, ly, lx, b].astype(F32) + ref[b].astype(F32)).astype(BF)

    first = {}
    for q in range(3):
        swaps[q, 0].wait_recv()
        add_line(q, dy, dx, rc.at[q, dy, dx])
        first[q, 0] = remote(acc.at[q, dy, dx], rr.at[q, 0], rnbr)
    for i in (1, 2):
        for q in range(3):
            swaps[q, i].wait_recv()
    for q in range(3):
        add_line(q, ry, rx, rc.at[q, ry, rx])
        first[q, 1] = remote(acc.at[q, ry, rx], rr.at[q, 1], rnbr)
    for q in range(3):
        add_line(q, py, px, rc.at[q, py, px])
        swaps[q, 3].wait_recv()
        add_line(q, y, x, rc.at[q, y, x])
    second = {}
    for q in (2, 0, 1):
        first[q, 0].wait_recv()
        add_line(q, py, px, rr.at[q, 0])
        if q < 2:
            second[q] = remote(acc.at[q, py, px], rp.at[q], pnbr)
        else:
            second[q] = [
                remote(acc.at[q, py, px, (z + k) % 4], rz2.at[k - 1], device(x, y, (z + k) % 4, c)) for k in (1, 2, 3)
            ]
    own2 = None
    for q in (2, 0, 1):
        first[q, 1].wait_recv()
        add_line(q, y, x, rr.at[q, 1])
        if q == 2:
            own2 = [
                remote(acc.at[q, y, x, (z + k) % 4], rz.at[q, k - 1], device(x, y, (z + k) % 4, c)) for k in (1, 2, 3)
            ]
    third = {}
    for q in (0, 1):
        second[q].wait_recv()
        add_line(q, y, x, rp.at[q])
        third[q] = [
            remote(acc.at[q, y, x, (z + k) % 4], rz.at[q, k - 1], device(x, y, (z + k) % 4, c)) for k in (1, 2, 3)
        ]
    for cp in second[2]:
        cp.wait_recv()
    stage[...] = (
        acc[2, py, px, z].astype(F32) + rz2[0].astype(F32) + rz2[1].astype(F32) + rz2[2].astype(F32)
    ).astype(BF)
    last = remote(stage, rb, pnbr)
    sbuf[me] = small_ref[me]
    wait31(sbuf, s1r)
    total = sbuf[0]
    for k in range(1, 32):
        total = total + sbuf[k]
    sred[...] = total
    tot_ref[me] = total
    broadcast(lambda p: sred, tot_ref.at[me], s2s, s2r)
    sq = jnp.zeros((8, 128), F32)

    def fold(v):
        t = jnp.zeros((8, 128), F32)
        for r in range(0, v.shape[0], 8):
            for l in range(0, v.shape[1], 128):
                p = v[r : r + 8, l : l + 128]
                t = t + p * p
        return t

    sq = sq + fold(total)
    for cp in own2:
        cp.wait_recv()
    for q in (0, 1):
        for cp in third[q]:
            cp.wait_recv()
        v = (
            acc[q, y, x, z].astype(F32) + rz[q, 0].astype(F32) + rz[q, 1].astype(F32) + rz[q, 2].astype(F32)
        )
        red_ref[q] = v
        sq = sq + fold(v)
    last.wait_recv()
    v = (
        acc[2, y, x, z].astype(F32) + rz[2, 0].astype(F32) + rz[2, 1].astype(F32) + rz[2, 2].astype(F32)
    ) + rb[...].astype(F32)
    red_ref[2] = v
    sq = sq + fold(v)
    nown[...] = sq
    nbuf[me] = sq
    broadcast(lambda p: nown, nbuf.at[me], ns, nr)
    wait31(nbuf, nr)
    wait31(tot_ref, s2r)
    t = nbuf[0]
    for k in range(1, 32):
        t = t + nbuf[k]
    t = jnp.sum(jnp.sum(t, axis=0, keepdims=True), axis=1, keepdims=True)
    norm_ref[...] = jnp.broadcast_to(jnp.sqrt(t), (8, 128))
    for cp in started:
        cp.wait_send()
    wait31(sbuf, s1s)
    wait31(tot_ref, s2s)
    wait31(nbuf, ns)


NRED = 12 + 6 + 2 + 3 + 3 + 6 + 1


def reduce_all(g, small):
    rows, width = g.shape[-2:]
    vmem = pl.BlockSpec(memory_space=pltpu.VMEM)
    anyb = pl.BlockSpec(memory_space=pl.ANY)
    dma = pltpu.SemaphoreType.DMA
    blk = (rows, width)
    return pl.pallas_call(
        reduce_kernel,
        out_shape=(
            jax.ShapeDtypeStruct((3,) + blk, F32),
            jax.ShapeDtypeStruct(small.shape, F32),
            jax.ShapeDtypeStruct((8, 128), F32),
        ),
        in_specs=[anyb, vmem],
        out_specs=[vmem] * 3,
        scratch_shapes=[
            pltpu.VMEM((3, 2, 2, 4) + blk, BF),
            pltpu.VMEM((3, 2, 2, 4) + blk, BF),
            pltpu.VMEM((3, 2, 4) + blk, BF),
            pltpu.VMEM((2, 4) + blk, BF),
            pltpu.VMEM((3, 3) + blk, BF),
            pltpu.VMEM((3,) + blk, BF),
            pltpu.VMEM(blk, BF),
            pltpu.VMEM(blk, BF),
            pltpu.VMEM(small.shape, F32),
            pltpu.VMEM(small.shape[1:], F32),
            pltpu.VMEM((32, 8, 128), F32),
            pltpu.VMEM((8, 128), F32),
            dma((NRED,)), dma((NRED,)), dma((3,)),
            dma, dma, dma, dma, dma, dma,
        ],
        compiler_params=pltpu.CompilerParams(collective_id=1, has_side_effects=True, vmem_limit_bytes=60 * 2**20),
        name="reduce",
    )(g, small)


STEP = 10
BETA_FIRST = 0.9
BETA_SECOND = 0.95
ADAM_EPS = 1e-08
DECAY_RATE = 0.05
RATE_MATRIX = 0.05
RATE_VECTOR = 0.8
CLIP_BOUND = 1.0
BOTH = ("dp", "fsdp")


def adam_step(weight, first, second, gradient, step_rate, weight_decay):
    first_new = BETA_FIRST * first + (1.0 - BETA_FIRST) * gradient
    second_new = BETA_SECOND * second + (1.0 - BETA_SECOND) * gradient * gradient
    first_hat = first_new * (1.0 / (1.0 - BETA_FIRST**STEP))
    second_hat = second_new * (1.0 / (1.0 - BETA_SECOND**STEP))
    weight_new = weight - step_rate * (
        first_hat / (jnp.sqrt(second_hat) + ADAM_EPS) + weight_decay * weight
    )
    return (weight_new, first_new, second_new)


def adam_kernel(red, tot, norm, iw, i1, i2, ow, o1, o2, sw, s1, s2, *outs):
    clip = CLIP_BOUND / jnp.maximum(norm[0:1, 0:1], CLIP_BOUND)
    rows = ow.shape[0]
    for q in range(2):
        for r in range(0, rows, 8):
            cut = slice(r, r + 8)
            new = adam_step(
                iw[q, cut], i1[q, cut], i2[q, cut], red[q, cut] * clip, RATE_MATRIX, DECAY_RATE
            )
            for ref, val in zip(outs[0:3], new):
                ref[q, cut] = val
    for r in range(0, rows, 8):
        cut = slice(r, r + 8)
        new = adam_step(ow[cut], o1[cut], o2[cut], red[2, cut] * clip, RATE_MATRIX, DECAY_RATE)
        for ref, val in zip(outs[3:6], new):
            ref[cut] = val
    side, cols = sw.shape
    grad = tot[SPATIAL_ROW : SPATIAL_ROW + side, 0:cols] * clip
    last = lax.broadcasted_iota(jnp.int32, (side, 1), 0) == side - 1
    rate = jnp.where(last, RATE_VECTOR, RATE_MATRIX)
    decay = jnp.where(last, 0.0, DECAY_RATE)
    new = adam_step(sw[...], s1[...], s2[...], grad, rate, decay)
    for ref, val in zip(outs[6:9], new):
        ref[...] = val


def adam_all(red, tot, norm, inner, outer, spatial):
    vmem = pl.BlockSpec(memory_space=pltpu.VMEM)
    shape = lambda a: jax.ShapeDtypeStruct(a.shape, F32)
    return pl.pallas_call(
        adam_kernel,
        out_shape=tuple(shape(a) for a in inner + outer + spatial),
        in_specs=[vmem] * 12,
        out_specs=[vmem] * 9,
        compiler_params=pltpu.CompilerParams(vmem_limit_bytes=32 * 2**20),
        name="adam",
    )(red, tot, norm, *inner, *outer, *spatial)


def slow_prepare(inner_t, outer_weight, vectors, tokens, cot, mask, keep, pool_cot, spatial):
    patches, images, width = tokens.shape
    pad = -(-patches // LOT) * LOT
    wt = jnp.concatenate(
        [
            lax.all_gather(inner_t.astype(BF), BOTH, axis=1, tiled=True),
            lax.all_gather(outer_weight.astype(BF), BOTH, axis=0, tiled=True)[None],
        ],
        axis=0,
    )
    vec = lax.all_gather(vectors.astype(BF), BOTH, axis=0, tiled=True).astype(F32)
    vec = vec.reshape(-1, width)
    counts = jnp.sum(mask, axis=1)
    info = jnp.zeros((images, 128), jnp.int32).at[:, 0].set(counts).at[:, 1].set(keep)
    poolc = pool_cot.astype(F32) / counts.astype(F32)[:, None]
    unit, _ = norm(tokens.astype(F32))
    edge = ((0, 0), (0, pad - patches), (0, 0))
    nm = (unit * vec[0] + vec[1]).astype(BF)
    live = mask.astype(F32).T[:, :, None]
    scale = keep.astype(F32) * (1.0 / (1.0 - DROP_RATE))
    bg = (scale[:, None] * (cot.astype(F32) + live * poolc)).astype(BF)
    bsum = jnp.sum(bg, axis=0, dtype=F32)
    nm = jnp.pad(nm.transpose(1, 0, 2), edge)
    bg = jnp.pad((bg * live.astype(BF)).transpose(1, 0, 2), edge)
    low = spatial[:patches].astype(BF)
    square = ((0, 256 - patches), (0, 256 - patches))
    sbias = jnp.pad(spatial[patches][:, None], ((0, 256 - patches), (0, 0)))
    return wt, vec, nm, bg, info, poolc, bsum, jnp.pad(low, square), jnp.pad(low.T, square), sbias


def slow_reduce(grads, small):
    red = lax.psum_scatter(grads.astype(F32), BOTH, scatter_dimension=1, tiled=True)
    tot = lax.psum(small, BOTH)
    squares = lax.psum(jnp.sum(red * red), BOTH) + jnp.sum(tot * tot)
    return red, tot, jnp.broadcast_to(jnp.sqrt(squares), (8, 128))


def per_device(
    fast,
    tokens,
    valid_mask,
    keep_mask,
    out_cotangent,
    pool_cotangent,
    inner_weight,
    outer_weight,
    vectors,
    spatial,
    inner_first,
    inner_second,
    outer_first,
    outer_second,
    vector_first,
    vector_second,
    spatial_first,
    spatial_second,
):
    own = vectors.shape[0]
    rows, width = outer_weight.shape
    inner_t = tuple(a.transpose(0, 2, 1) for a in (inner_weight, inner_first, inner_second))
    tokens = tokens.transpose(1, 0, 2)
    cot = out_cotangent.transpose(1, 0, 2)
    if fast:
        wt, *ready = gather_all(
            own,
            inner_t[0],
            outer_weight,
            jnp.pad(vectors, (0, 1024 - own)).reshape(8, 128),
            tokens,
            cot,
            valid_mask,
            keep_mask[:, None],
            pool_cotangent,
            spatial,
        )
        wt = wt.reshape(3, 32 * rows, width)
    else:
        wt, *ready = slow_prepare(
            inner_t[0], outer_weight, vectors, tokens, cot, valid_mask, keep_mask, pool_cotangent, spatial
        )
    vec, nm, bg, info, poolc, bsum, sp, spt, sbias = ready
    output, input_grad, pooled, grads, small = run_block(
        tokens, cot, nm, bg, info, poolc, bsum, wt, vec, sp, spt, sbias
    )
    output = output.transpose(1, 0, 2)
    input_grad = input_grad.transpose(1, 0, 2)
    if fast:
        red, tot, norm = reduce_all(
            grads.reshape(3, 2, 2, 4, 2, rows, width), small.reshape(32, 8, 256)
        )
        tot = tot.reshape(256, 256)
    else:
        red, tot, norm = slow_reduce(grads, small)
    new = adam_all(
        red,
        tot,
        norm,
        inner_t,
        (outer_weight, outer_first, outer_second),
        (spatial, spatial_first, spatial_second),
    )
    grad_norm = norm[0, 0]
    clip_factor = CLIP_BOUND / jnp.maximum(grad_norm, CLIP_BOUND)
    me = lax.axis_index("dp") * lax.axis_size("fsdp") + lax.axis_index("fsdp")
    total_vec = own * lax.axis_size("dp") * lax.axis_size("fsdp")
    flat = tot[: total_vec // 256].reshape(-1)
    vector_red = lax.dynamic_slice(flat, (me * own,), (own,))
    vector_out = adam_step(
        vectors, vector_first, vector_second, vector_red * clip_factor, RATE_VECTOR, 0.0
    )
    return (
        (output, input_grad, pooled, grad_norm)
        + tuple(a.transpose(0, 2, 1) for a in new[0:3])
        + tuple(new[3:6])
        + vector_out
        + tuple(new[6:9])
    )


def solution(mesh):
    fast = mesh.shape["dp"] == 4 and mesh.shape["fsdp"] == 8
    rows3 = P(BOTH, None, None)
    rows2 = P(BOTH, None)
    rows1 = P(BOTH)
    cols3 = P(None, None, BOTH)
    in_specs = (
        (rows3, rows2, rows1, rows3, rows2, cols3, rows2, rows1, P())
        + (cols3,) * 2
        + (rows2,) * 2
        + (rows1,) * 2
        + (P(),) * 2
    )
    out_specs = (
        (rows3, rows3, rows2, P()) + (cols3,) * 3 + (rows2,) * 3 + (rows1,) * 3 + (P(),) * 3
    )
    return jax.shard_map(
        functools.partial(per_device, fast),
        mesh=mesh,
        in_specs=in_specs,
        out_specs=out_specs,
        check_vma=False,
    )
```

```python
import functools

import jax
import jax.numpy as jnp
from jax import lax
from jax.experimental import pallas as pl
from jax.experimental.pallas import tpu as pltpu
from jax.sharding import PartitionSpec as P

NORM_EPS = 1e-05
DROP_RATE = 0.1
BF = jnp.bfloat16
F32 = jnp.float32
MESH = pl.DeviceIdType.MESH
GELU_K = 0.7978845608
GELU_C = 0.044715
NN = (((1,), (0,)), ((), ()))
NT = (((1,), (1,)), ((), ()))
TN = (((0,), (0,)), ((), ()))
LOT = 16
CUTS = 3


def dot(a, b, dims):
    return lax.dot_general(a, b, dims, preferred_element_type=F32)


def norm(x):
    c = x - jnp.mean(x, axis=-1, keepdims=True)
    inv = lax.rsqrt(jnp.mean(c * c, axis=-1, keepdims=True) + NORM_EPS)
    return c * inv, inv


def swap_matrix(images):
    side = LOT * images
    r = lax.broadcasted_iota(jnp.int32, (side, side), 0)
    s = lax.broadcasted_iota(jnp.int32, (side, side), 1)
    return jnp.where(s == (r % LOT) * images + r // LOT, 1.0, 0.0).astype(BF)


def unswap_matrix(images):
    side = LOT * images
    r = lax.broadcasted_iota(jnp.int32, (side, side), 0)
    s = lax.broadcasted_iota(jnp.int32, (side, side), 1)
    return jnp.where(s == (r % images) * LOT + r // images, 1.0, 0.0).astype(BF)


def place():
    d = lax.axis_index("dp")
    f = lax.axis_index("fsdp")
    return d % 2, d // 2, f // 2, f % 2


def device(x, y, z, c):
    return (y * 2 + x, z * 2 + c)


def greet_partners():
    x, y, z, c = place()
    barrier = pltpu.get_barrier_semaphore()
    peers = [device(1 - x, y, z, c), device(x, 1 - y, z, c), device(x, y, z, 1 - c)]
    peers += [device(x, y, (z + k) % 4, c) for k in (1, 2, 3)]
    for peer in peers:
        pl.semaphore_signal(barrier, inc=1, device_id=peer, device_id_type=MESH)
    pl.semaphore_wait(barrier, len(peers))


def gather_kernel(
    own_len,
    inner_ref, outer_ref, vec_ref, tokens_hbm, cot_hbm, mask_ref, keep_ref, pool_ref, spatial_ref,
    all_ref, vecs_ref, nm_ref, bg_ref, info_ref, poolc_ref, bsum_ref, sp_ref, spt_ref, sbias_ref,
    own, vown, vgot, wide, xblk, cblk, nrow, brow, nm_v, bg_v, send, recv, lsem, isem, osem,
):
    x, y, z, c = place()
    patches, images, width = tokens_hbm.shape
    own[0] = inner_ref[0].astype(BF)
    own[1] = inner_ref[1].astype(BF)
    own[2] = outer_ref[...].astype(BF)
    vown[...] = vec_ref[...].astype(BF).astype(F32)
    loads = [
        pltpu.make_async_copy(tokens_hbm, xblk, isem.at[0]),
        pltpu.make_async_copy(cot_hbm, cblk, isem.at[1]),
    ]
    for cp in loads:
        cp.start()
    greet_partners()
    local = pltpu.make_async_copy(own, all_ref.at[:, y, x, z, c], lsem)
    local.start()
    vgot[y, x, z, c] = vown[...]

    px, py = jnp.where(c == 0, 1 - x, x), jnp.where(c == 0, y, 1 - y)
    rx, ry = jnp.where(c == 0, x, 1 - x), jnp.where(c == 0, 1 - y, y)
    dx, dy = 1 - x, 1 - y
    index = [0]
    pnbr, rnbr, core = device(px, py, z, c), device(rx, ry, z, c), device(x, y, z, 1 - c)
    cut = outer_ref.shape[0] // CUTS
    started = []

    def remote(src, dst, dev):
        k = index[0]
        index[0] += 1
        cp = pltpu.make_async_remote_copy(
            src_ref=src, dst_ref=dst, send_sem=send.at[k], recv_sem=recv.at[k],
            device_id=dev, device_id_type=MESH,
        )
        cp.start()
        started.append(cp)
        return cp

    def span(s):
        return pl.ds(s * cut, cut)

    def block(q, s, by, bx):
        if q == 3:
            return vgot.at[by, bx, z, c]
        return all_ref.at[q, by, bx, z, c, span(s)]

    def z_sends(src, q, s, by, bx):
        return [remote(src, block(q, s, by, bx), device(x, y, (z + k) % 4, c)) for k in (1, 2, 3)]

    def send_line(q, s, ly, lx, dev):
        ref = vgot.at[ly, lx, :, c] if q == 3 else all_ref.at[q, ly, lx, :, c, span(s)]
        return remote(ref, ref, dev)

    cuts = [(3, 0)] + [(q, s) for s in range(CUTS) for q in range(3)]
    zs = [None] * len(cuts)

    def start_z(k):
        if k < len(cuts):
            q, s = cuts[k]
            src = vown if q == 3 else own.at[q, span(s)]
            zs[k] = z_sends(src, q, s, y, x)

    for k in range(WINDOW):
        start_z(k)
    local.wait()

    counts = jnp.sum(mask_ref[...], axis=1, keepdims=True)
    keeps = jnp.zeros((images, 1), jnp.int32)
    image = lax.broadcasted_iota(jnp.int32, (images, 1), 0)
    for b in range(images):
        keeps = jnp.where(image == b, keep_ref[b], keeps)
    scale = keeps.astype(F32) * (1.0 / (1.0 - DROP_RATE))
    lane = lax.broadcasted_iota(jnp.int32, info_ref.shape, 1)
    info_ref[...] = jnp.where(lane == 0, counts, keeps)
    poolc = pool_ref[...].astype(F32) / counts.astype(F32)
    poolc_ref[...] = poolc
    side = spatial_ref.shape[1]
    wide[...] = jnp.zeros_like(wide)
    wide[0 : side + 1, 0:side] = spatial_ref[...]
    mat = wide[...]
    mat_t = mat.T
    span_a = lax.broadcasted_iota(jnp.int32, mat.shape, 0)
    span_b = lax.broadcasted_iota(jnp.int32, mat.shape, 1)
    sp_ref[...] = jnp.where(span_a < side, mat, 0.0).astype(BF)
    spt_ref[...] = jnp.where(span_b < side, mat_t, 0.0).astype(BF)
    sbias_ref[...] = mat_t[:, side : side + 1]
    bsum_ref[...] = jnp.zeros_like(bsum_ref)
    vecs_ref[...] = jnp.zeros_like(vecs_ref)

    def stack_vectors():
        per = width // 128
        for d in range(32):
            start = own_len * d
            shift = start % 128
            blk = vgot[d // 16, d // 8 % 2, d // 2 % 4, d % 2]
            row = jnp.concatenate(
                [jnp.broadcast_to(blk[i : i + 1, :], (8, 128)) for i in range(3)], axis=1
            )
            row = pltpu.roll(row, shift, 1) if shift else row
            for i in range(3):
                r = start // 128 + i
                if r * 128 < start + own_len:
                    at = (slice(r // per, r // per + 1), slice(r % per * 128, r % per * 128 + 128))
                    vecs_ref[at] += row[0:1, i * 128 : i * 128 + 128]

    swap = swap_matrix(images)

    def token_block(k, many):
        gain, shift = vecs_ref[0:1, :], vecs_ref[1:2, :]
        for p in range(many):
            patch = k * LOT + p
            xv = xblk[patch].astype(F32)
            unit, _ = norm(xv)
            nrow[p * images : (p + 1) * images, :] = (unit * gain + shift).astype(BF)
            live = jnp.where(counts > patch, 1.0, 0.0)
            og = cblk[patch].astype(F32) + live * poolc
            bg = (scale * og).astype(BF).astype(F32)
            bsum_ref[...] += bg
            brow[p * images : (p + 1) * images, :] = (live * bg).astype(BF)
        part = swap[:, 0 : many * images]
        for src, dst in ((nrow, nm_v), (brow, bg_v)):
            moved = dot(part, src[0 : many * images, :], NN).astype(BF)
            at = pl.ds(pl.multiple_of(k * LOT, LOT), LOT)
            dst[:, at, :] = moved.reshape(images, LOT, width)

    full = patches // LOT
    todo = list(range(full + (1 if patches % LOT else 0)))

    stores = []
    pad = nm_v.shape[1]
    marks = [pad // (2 * LOT) * LOT, pad]

    def some_tokens(many):
        for _ in range(many):
            if not todo:
                return
            k = todo.pop(0)
            token_block(k, LOT if k < full else patches % LOT)
            end = (k + 1) * LOT
            if end in marks:
                at = pl.ds(0, end) if end == marks[0] else pl.ds(marks[0], end - marks[0])
                for src, dst in ((nm_v, nm_ref), (bg_v, bg_ref)):
                    cp = pltpu.make_async_copy(src.at[:, at], dst.at[:, at], osem.at[len(stores)])
                    cp.start()
                    stores.append(cp)

    lines_p, lines_r, lines_r2, cores = {}, {}, {}, {}

    def swap_core(k, cp):
        cores.setdefault(k, []).append(cp)


    def stage_two(k):
        q, s = cuts[k]
        for cp in zs[k]:
            cp.wait_recv()
        start_z(k + WINDOW)
        lines_p[k] = send_line(q, s, y, x, pnbr)
        lines_r[k] = send_line(q, s, y, x, rnbr)
        swap_core(k, send_line(q, s, y, x, core))

    def stage_three(k):
        q, s = cuts[k]
        lines_p[k].wait_recv()
        lines_r2[k] = send_line(q, s, py, px, rnbr)
        swap_core(k, send_line(q, s, py, px, core))

    def stage_four(k):
        q, s = cuts[k]
        lines_r[k].wait_recv()
        swap_core(k, send_line(q, s, ry, rx, core))

    def stage_five(k):
        q, s = cuts[k]
        lines_r2[k].wait_recv()
        swap_core(k, send_line(q, s, dy, dx, core))

    n = len(cuts)
    for t in range(n + LAG_FIVE):
        if t < n:
            stage_two(t)
        if 0 <= t - LAG_THREE < n:
            stage_three(t - LAG_THREE)
            stage_four(t - LAG_THREE)
        if 0 <= t - LAG_FIVE < n:
            stage_five(t - LAG_FIVE)
        if t == LAG_FIVE + 1:
            for cp in cores[0]:
                cp.wait_recv()
            stack_vectors()
            for cp in loads:
                cp.wait()
        if t > LAG_FIVE:
            some_tokens(-(-13 // (n - 1)))
    some_tokens(len(todo))
    for k in range(1, n):
        for cp in cores[k]:
            cp.wait_recv()
    for cp in started:
        cp.wait_send()
    for cp in stores:
        cp.wait()


NSEND = 10 * (3 * CUTS + 1)
LAG_THREE = 3
LAG_FIVE = 6
WINDOW = 4


def gather_all(own_len, inner, outer, vec, tokens, cot, mask, keep, pool, spatial):
    rows, width = outer.shape
    patches, images, _ = tokens.shape
    pad = -(-patches // LOT) * LOT
    vmem = pl.BlockSpec(memory_space=pltpu.VMEM)
    smem = pl.BlockSpec(memory_space=pltpu.SMEM)
    anyb = pl.BlockSpec(memory_space=pl.ANY)
    dma = pltpu.SemaphoreType.DMA
    shape = jax.ShapeDtypeStruct
    return pl.pallas_call(
        functools.partial(gather_kernel, own_len),
        out_shape=(
            shape((3, 2, 2, 4, 2, rows, width), BF),
            shape((16, width), F32),
            shape((images, pad, width), BF),
            shape((images, pad, width), BF),
            shape((images, 128), jnp.int32),
            shape((images, width), F32),
            shape((images, width), F32),
            shape((256, 256), BF),
            shape((256, 256), BF),
            shape((256, 1), F32),
        ),
        in_specs=[vmem] * 3 + [anyb] * 2 + [vmem, smem, vmem, vmem],
        out_specs=[anyb, vmem, anyb, anyb] + [vmem] * 6,
        scratch_shapes=[
            pltpu.VMEM((3, rows, width), BF),
            pltpu.VMEM((8, 128), F32),
            pltpu.VMEM((2, 2, 4, 2, 8, 128), F32),
            pltpu.VMEM((256, 256), F32),
            pltpu.VMEM((patches, images, width), BF),
            pltpu.VMEM((patches, images, width), BF),
            pltpu.VMEM((LOT * images, width), BF),
            pltpu.VMEM((LOT * images, width), BF),
            pltpu.VMEM((images, pad, width), BF),
            pltpu.VMEM((images, pad, width), BF),
            dma((NSEND,)), dma((NSEND,)), dma, dma((2,)), dma((4,)),
        ],
        compiler_params=pltpu.CompilerParams(
            collective_id=0, has_side_effects=True, vmem_limit_bytes=60 * 2**20
        ),
        name="gather",
    )(inner, outer, vec, tokens, cot, mask, keep, pool, spatial)


def gelu_pair(v):
    u = v * v
    s = 0.5 * jnp.tanh(v * (GELU_K + (GELU_K * GELU_C) * u)) + 0.5
    h = v * s
    d = s + (h - h * s) * (2.0 * GELU_K + (6.0 * GELU_K * GELU_C) * u)
    return h, d


def fold8(x):
    total = x[0:8]
    for r in range(8, x.shape[0], 8):
        total = total + x[r : r + 8]
    return total


def lanes(x):
    total = x[:, 0:128]
    for c in range(128, x.shape[1], 128):
        total = total + x[:, c : c + 128]
    return total


def loop(lo, hi, fn):
    def body(i, c):
        fn(i)
        return c

    lax.fori_loop(lo, hi, body, 0)


def block_kernel(
    cfg,
    info_s,
    tokens_hbm, cot_hbm, nm_hbm, bg_hbm,
    info_ref, poolc_ref, bsum_ref, wt_ref, vec_ref, sp_ref, spt_ref, sbias_ref,
    out_hbm, ig_hbm, pooled_ref, grads_hbm, small_ref,
    acc, sg_ref, sbg_ref, off_s, gend_s, grows_s,
    wtt, nm_b, bg_b, h0_b, e0_b, mg_b, xm_b, u2_b, d1_b, stat_b, h1_s, t_s,
    xblk, cblk, br_s, ng_s, out_st, ig_st, vacc,
    pack_sem, in_sem, out_sem, grad_sem,
):
    images, patches, width, gate, rows_cap, tm, kw, classes = cfg
    cw = 256
    nj = gate // cw
    chunks = -(-patches // LOT)
    zero_row = nm_b.shape[0] - LOT
    g2_base, s2_base = 3 * width, 3 * width + gate
    b0_base, b1_base = 3 * width + 2 * gate, 3 * width + 3 * gate

    def vrow(base, j):
        start = base + j * cw
        return vec_ref[start // width : start // width + 1, start % width : start % width + cw]

    def count(b):
        return info_s[b, 0]

    def keep(b):
        return info_s[b, 1]

    def need_of(b):
        return keep(b) * ((count(b) + LOT - 1) // LOT)

    def plan(b, carry):
        group, row, first = carry
        need = need_of(b) * LOT
        over = row + need - first > rows_cap
        group = group + over.astype(jnp.int32)
        first = jnp.where(over, row, first)
        off_s[b] = row
        row = row + need
        gend_s[group] = b + 1
        grows_s[group] = row - first
        return group, row, first

    zero = jnp.int32(0)
    last_group, all_rows, _ = lax.fori_loop(0, images, plan, (zero, zero, zero))

    def pack(b, act):
        lots = need_of(b)
        o = off_s[b]
        done = jnp.int32(0)
        for size in (8, 4, 2, 1):
            @pl.when((lots & size) != 0)
            def _(size=size, done=done):
                src = pl.ds(pl.multiple_of(done * LOT, LOT), size * LOT)
                dst = pl.ds(pl.multiple_of(o + done * LOT, LOT), size * LOT)
                for i, (far, near) in enumerate(((nm_hbm, nm_b), (bg_hbm, bg_b))):
                    act(pltpu.make_async_copy(far.at[b, src], near.at[dst], pack_sem.at[i, b]))

            done = done + (lots & size)

    loop(0, images, lambda b: pack(b, lambda cp: cp.start()))

    full = patches // LOT
    rest = patches % LOT

    def load_lot(k, many, slot):
        at = pl.ds(k * LOT, many)
        return (
            pltpu.make_async_copy(tokens_hbm.at[at], xblk.at[slot, pl.ds(0, many)], in_sem.at[0, slot]),
            pltpu.make_async_copy(cot_hbm.at[at], cblk.at[slot, pl.ds(0, many)], in_sem.at[1, slot]),
        )

    for k in (0, 1):
        for cp in load_lot(k, LOT, k):
            cp.start()

    for q in range(3):
        for j in range(nj):
            wtt[q, :, j * cw : (j + 1) * cw] = wt_ref[q, j * cw : (j + 1) * cw, :].T

    def zero_rows(ref, n_chunks, start):
        z = jnp.zeros((LOT, ref.shape[1]), ref.dtype)

        def body(i):
            ref[pl.ds(pl.multiple_of(start + i * LOT, LOT), LOT), :] = z

        loop(0, n_chunks, body)

    for ref in (mg_b, xm_b, u2_b):
        zero_rows(ref, ref.shape[0] // LOT, 0)
    for ref in (nm_b, bg_b):
        zero_rows(ref, tm // LOT, all_rows)
    z = jnp.zeros((LOT, width), BF)
    nm_b[zero_row : zero_row + LOT, :] = z
    bg_b[zero_row : zero_row + LOT, :] = z
    vacc[...] = jnp.zeros_like(vacc)
    acc[...] = jnp.zeros_like(acc)
    sg_ref[...] = jnp.zeros_like(sg_ref)
    sbg_ref[...] = jnp.zeros_like(sbg_ref)
    loop(0, images, lambda b: pack(b, lambda cp: cp.wait()))

    def phase_a(t, gs):
        r0 = pl.multiple_of(t * tm, tm)
        rows = pl.ds(r0, tm)
        here = pl.ds(pl.multiple_of(gs + r0, LOT), tm)
        nb = nm_b[here, :]
        bgt = bg_b[here, :]
        s1 = jnp.zeros((tm, 128), F32)
        for j in range(nj):
            cols = slice(j * cw, (j + 1) * cw)
            a1 = dot(nb, wtt[1, :, cols], NN) + vrow(b1_base, j)
            h1, d1 = gelu_pair(a1)
            h1_s[:, cols] = h1
            d1_b[rows, cols] = d1.astype(BF)
            s1 = s1 + lanes(h1)
        mean = jnp.sum(s1, axis=1, keepdims=True) * (1.0 / gate)
        q1 = jnp.zeros((tm, 128), F32)
        for j in range(nj):
            cols = slice(j * cw, (j + 1) * cw)
            a0 = dot(nb, wtt[0, :, cols], NN) + vrow(b0_base, j)
            h0, d0 = gelu_pair(a0)
            gg = dot(bgt, wtt[2, :, cols], NN)
            mg = gg * h0
            h0_b[rows, cols] = h0.astype(BF)
            mg_b[rows, cols] = mg.astype(BF)
            e0_b[rows, cols] = (gg * d0).astype(BF)
            c = h1_s[:, cols] - mean
            q1 = q1 + lanes(c * c)
        inv = lax.rsqrt(jnp.sum(q1, axis=1, keepdims=True) * (1.0 / gate) + NORM_EPS)
        stat_b[rows, :] = jnp.broadcast_to(inv, (tm, 128))
        for j in range(nj):
            cols = slice(j * cw, (j + 1) * cw)
            u2 = (h1_s[:, cols] - mean) * inv
            u2_b[rows, cols] = u2.astype(BF)
            xm_b[rows, cols] = (u2 * vrow(g2_base, j) + vrow(s2_base, j)).astype(BF)

    def phase_b(b, m, gs):
        n = count(b)
        o = pl.multiple_of(off_s[b] - gs, LOT)
        rows = pl.ds(o, m)
        rid = lax.broadcasted_iota(jnp.int32, (m, 1), 0)
        cid = lax.broadcasted_iota(jnp.int32, (m, m), 1)
        rid2 = lax.broadcasted_iota(jnp.int32, (m, m), 0)
        both = (cid < n) & (rid2 < n)
        sp = jnp.where(both, sp_ref[0:m, 0:m], 0.0).astype(BF)
        spt = jnp.where(both, spt_ref[0:m, 0:m], 0.0).astype(BF)
        valid = rid < n
        fill = jnp.where(rid < need_of(b) * LOT, 0.0, 1.0)
        sbias = jnp.where(valid, sbias_ref[0:m, :], fill)
        inv = jnp.where(valid, stat_b[rows, 0:1], 0.0)
        ones = jnp.ones((LOT, gate), BF)
        tsum = jnp.zeros((m, 128), F32)
        tdot = jnp.zeros((m, 128), F32)
        xm_ones = jnp.concatenate([xm_b[rows, :], ones], axis=0)
        sg = dot(mg_b[rows, :], xm_ones, NT)
        sg_ref[0:m, 0:m] += jnp.where(both, sg[:, 0:m], 0.0)
        sbg_ref[0:m, 0:1] += jnp.where(valid, sg[:, m : m + 1], 0.0)
        for j in range(nj):
            cols = slice(j * cw, (j + 1) * cw)
            xm = xm_b[rows, cols]
            mg = mg_b[rows, cols]
            so = (dot(sp, xm, NN) + sbias).astype(BF)
            mix = dot(spt, mg, NN)
            h0_b[rows, cols] = h0_b[rows, cols] * so
            e0_b[rows, cols] = e0_b[rows, cols] * so
            u2 = u2_b[rows, cols].astype(F32)
            mu = mix * u2
            gain = vrow(g2_base, j)
            t = mix * gain
            t_s[0:m, cols] = t
            tsum = tsum + lanes(t)
            tdot = tdot + lanes(mu * gain)
            vi, lo = j * cw // width, j * cw % width
            vacc[g2_base // width + vi, :, lo : lo + cw] += fold8(mu)
            vacc[s2_base // width + vi, :, lo : lo + cw] += fold8(mix)
        m1 = jnp.sum(tsum, axis=1, keepdims=True) * (1.0 / gate)
        m2 = jnp.sum(tdot, axis=1, keepdims=True) * (1.0 / gate)
        base, slope = fill - inv * m1, inv * m2
        for j in range(nj):
            cols = slice(j * cw, (j + 1) * cw)
            u2 = u2_b[rows, cols].astype(F32)
            sec = (inv * t_s[0:m, cols] + (base - u2 * slope)).astype(BF)
            d1_b[rows, cols] = d1_b[rows, cols] * sec

    def phase_w(k, gs):
        r0 = pl.multiple_of(k * kw, kw)
        rows = pl.ds(r0, kw)
        here = pl.ds(pl.multiple_of(gs + r0, LOT), kw)
        nb = nm_b[here, :]
        bgt = bg_b[here, :]
        for j in range(gate // 256):
            cols = slice(j * 256, (j + 1) * 256)
            acc[0, cols, :] += dot(e0_b[rows, cols], nb, TN)
            acc[1, cols, :] += dot(d1_b[rows, cols], nb, TN)
            acc[2, cols, :] += dot(h0_b[rows, cols], bgt, TN)

    def phase_c(t, gs, group_rows):
        r0 = pl.multiple_of(t * tm, tm)
        rows = pl.ds(r0, tm)
        here = pl.ds(pl.multiple_of(gs + r0, LOT), tm)
        mine = lax.broadcasted_iota(jnp.int32, (tm, 1), 0) < group_rows - r0
        br = dot(h0_b[rows, :], wt_ref[2], NN)
        bg_b[here, :] = jnp.where(mine, br, bg_b[here, :].astype(F32)).astype(BF)
        ng = dot(e0_b[rows, :], wt_ref[0], NN) + dot(d1_b[rows, :], wt_ref[1], NN)
        nm_b[here, :] = jnp.where(mine, ng, nm_b[here, :].astype(F32)).astype(BF)
        for base, ref in ((b0_base // width, e0_b), (b1_base // width, d1_b)):
            for v in range(gate // width):
                vacc[base + v] += fold8(ref[rows, v * width : (v + 1) * width].astype(F32))

    def group(g, carry):
        b_start, gs = carry
        b_end = gend_s[g]
        rows = grows_s[g]
        tiles = (rows + tm - 1) // tm
        loop(0, tiles, lambda t: phase_a(t, gs))

        def do_b(b):
            low = 0
            for m in classes:
                @pl.when((keep(b) == 1) & (count(b) > low) & (count(b) <= m))
                def _(m=m):
                    phase_b(b, m, gs)

                low = m

        loop(b_start, b_end, do_b)
        tail = (tiles * tm - rows) // LOT
        for ref in (h0_b, e0_b, d1_b):
            zero_rows(ref, tail, rows)
        loop(0, (rows + kw - 1) // kw, lambda k: phase_w(k, gs))
        loop(0, tiles, lambda t: phase_c(t, gs, rows))
        return b_end, gs + rows

    lax.fori_loop(0, last_group + 1, group, (zero, zero))

    half = gate // 2
    grad_out = []
    per = gate // width
    for i in range(6):
        q, lo = i // 2, (i % 2) * half
        buf = (h1_s, t_s)[0]
        del buf
        stage = (mg_b, xm_b)[i % 2]
        if i >= 2:
            for cp in grad_out[i - 2]:
                cp.wait()
        cps = []
        for v in range(per):
            third = half // per
            cut = slice(v * width, (v + 1) * width)
            stage[0:third, cut] = acc[q, lo + v * third : lo + (v + 1) * third, :].astype(BF)
            cps.append(
                pltpu.make_async_copy(
                    stage.at[pl.ds(0, third), pl.ds(v * width, width)],
                    grads_hbm.at[q, pl.ds(lo + v * third, third)],
                    grad_sem.at[i, v],
                )
            )
        for cp in cps:
            cp.start()
        grad_out.append(cps)

    counts = info_ref[:, 0:1]
    live_counts = counts * info_ref[:, 1:2]
    scale = info_ref[:, 1:2].astype(F32) * (1.0 / (1.0 - DROP_RATE))
    poolc = poolc_ref[...]
    gain_one, bias_out = vec_ref[0:1, :], vec_ref[2:3, :]
    back = unswap_matrix(images)

    def store_lot(k, many, slot):
        at = pl.ds(k * LOT, many)
        return (
            pltpu.make_async_copy(out_st.at[slot, pl.ds(0, many)], out_hbm.at[at], out_sem.at[0, slot]),
            pltpu.make_async_copy(ig_st.at[slot, pl.ds(0, many)], ig_hbm.at[at], out_sem.at[1, slot]),
        )

    pooled_ref[...] = jnp.zeros_like(pooled_ref)

    def lot(k, many, slot):
        for cp in load_lot(k, many, slot):
            cp.wait()
        parts = [[], []]
        for b in range(images):
            there = k < need_of(b)
            row = pl.multiple_of(jnp.where(there, off_s[b] + k * LOT, zero_row), LOT)
            parts[0].append(bg_b[pl.ds(row, LOT), :])
            parts[1].append(nm_b[pl.ds(row, LOT), :])
        mat = back[0 : many * images, :]
        br_s[0 : many * images, :] = dot(mat, jnp.concatenate(parts[0], axis=0), NN)
        ng_s[0 : many * images, :] = dot(mat, jnp.concatenate(parts[1], axis=0), NN)
        psum = jnp.zeros((images, width), F32)
        g1 = jnp.zeros((images, width), F32)
        s1 = jnp.zeros((images, width), F32)
        for p in range(many):
            patch = k * LOT + p
            x = xblk[slot, p].astype(F32)
            unit, inv = norm(x)
            live = jnp.where(counts > patch, 1.0, 0.0)
            og = cblk[slot, p].astype(F32) + live * poolc
            cut = slice(p * images, (p + 1) * images)
            out = x + scale * (br_s[cut, :] + bias_out)
            out_st[slot, p] = out
            psum = psum + live * out
            ng = ng_s[cut, :]
            t = ng * gain_one
            m1 = jnp.mean(t, axis=-1, keepdims=True)
            m2 = jnp.mean(t * unit, axis=-1, keepdims=True)
            ig_st[slot, p] = og + inv * (t - m1 - unit * m2)
            g1 = g1 + ng * unit
            s1 = s1 + ng
        pooled_ref[...] += psum
        vacc[0] += fold8(g1)
        vacc[1] += fold8(s1)
        for cp in store_lot(k, many, slot):
            cp.start()

    def lots(k):
        slot = lax.rem(k, 2)

        @pl.when(k >= 2)
        def _():
            for cp in store_lot(k - 2, LOT, slot):
                cp.wait()

        lot(k, LOT, slot)

        @pl.when(k + 2 < full)
        def _():
            for cp in load_lot(k + 2, LOT, slot):
                cp.start()

        if rest:
            @pl.when(k + 2 == full)
            def _():
                for cp in load_lot(full, rest, full % 2):
                    cp.start()

    loop(0, full, lots)
    if rest:
        for cp in store_lot(full - 2, LOT, full % 2):
            cp.wait()
        lot(full, rest, full % 2)
    pooled_ref[...] = pooled_ref[...] / counts.astype(F32)

    vacc[2] += fold8(bsum_ref[...])
    small_ref[...] = jnp.zeros_like(small_ref)
    sums = jnp.sum(vacc[...], axis=1)
    for v in range(sums.shape[0]):
        for h in range(width // 256):
            row = v * (width // 256) + h
            small_ref[row : row + 1, :] = sums[v : v + 1, h * 256 : (h + 1) * 256]
    pad = sg_ref.shape[0]
    small_ref[SPATIAL_ROW : SPATIAL_ROW + pad, 0:pad] = sg_ref[...]
    bias = sbg_ref[:, 0:1]
    eye = lax.broadcasted_iota(jnp.int32, (pad, pad), 0) == lax.broadcasted_iota(jnp.int32, (pad, pad), 1)
    bias_row = jnp.sum(jnp.where(eye, bias, 0.0), axis=0, keepdims=True)
    small_ref[SPATIAL_ROW + patches : SPATIAL_ROW + patches + 1, 0:pad] = bias_row
    for cps in grad_out[4:]:
        for cp in cps:
            cp.wait()
    if rest:
        for cp in store_lot(full - 1, LOT, (full - 1) % 2) + store_lot(full, rest, full % 2):
            cp.wait()
    else:
        for k in (full - 2, full - 1):
            for cp in store_lot(k, LOT, k % 2):
                cp.wait()


SPATIAL_ROW = 32


def run_block(
    tokens, cot, nm, bg, info, poolc, bsum, wt, vec, sp, spt, sbias,
    *, rows_cap=1024, tm=256, kw=256, classes=(96, 144, 208),
):
    patches, images, width = tokens.shape
    gate = wt.shape[1]
    pad = -(-patches // LOT) * LOT
    classes = tuple(m for m in classes if m < pad) + (pad,)
    cap = rows_cap + pad + 48
    cap = -(-cap // tm) * tm
    long = images * pad + tm + LOT
    cfg = (images, patches, width, gate, rows_cap, tm, kw, classes)
    smem = pl.BlockSpec(memory_space=pltpu.SMEM)
    vmem = pl.BlockSpec(memory_space=pltpu.VMEM)
    anyb = pl.BlockSpec(memory_space=pl.ANY)
    dma = pltpu.SemaphoreType.DMA
    shape = jax.ShapeDtypeStruct
    nvec = 3 + 4 * gate // width
    return pl.pallas_call(
        functools.partial(block_kernel, cfg),
        out_shape=(
            shape((patches, images, width), F32),
            shape((patches, images, width), F32),
            shape((images, width), F32),
            shape((3, gate, width), BF),
            shape((256, 256), F32),
        ),
        in_specs=[smem] + [anyb] * 4 + [vmem] * 8,
        out_specs=[anyb, anyb, vmem, anyb, vmem],
        scratch_shapes=[
            pltpu.VMEM((3, gate, width), F32),
            pltpu.VMEM((pad, pad), F32),
            pltpu.VMEM((pad, 128), F32),
            pltpu.SMEM((images,), jnp.int32),
            pltpu.SMEM((images,), jnp.int32),
            pltpu.SMEM((images,), jnp.int32),
            pltpu.VMEM((3, width, gate), BF),
            pltpu.VMEM((long, width), BF),
            pltpu.VMEM((long, width), BF),
        ]
        + [pltpu.VMEM((cap, gate), BF)] * 6
        + [
            pltpu.VMEM((cap, 128), F32),
            pltpu.VMEM((tm, gate), F32),
            pltpu.VMEM((pad, gate), F32),
            pltpu.VMEM((2, LOT, images, width), BF),
            pltpu.VMEM((2, LOT, images, width), BF),
            pltpu.VMEM((LOT * images, width), F32),
            pltpu.VMEM((LOT * images, width), F32),
            pltpu.VMEM((2, LOT, images, width), F32),
            pltpu.VMEM((2, LOT, images, width), F32),
            pltpu.VMEM((nvec, 8, width), F32),
            dma((2, images)),
            dma((2, 2)),
            dma((2, 2)),
            dma((6, gate // width)),
        ],
        compiler_params=pltpu.CompilerParams(vmem_limit_bytes=60 * 2**20),
        name="block",
    )(info, tokens, cot, nm, bg, info, poolc, bsum, wt, vec, sp, spt, sbias)


def reduce_kernel(
    g_hbm, small_ref, red_ref, tot_ref, norm_ref,
    acc, rc, rr, rp, rz, sacc, src, srr, srp, srz, nbuf, mbuf, nown, mown,
    send, recv, lsem,
):
    x, y, z, c = place()
    px, py = jnp.where(c == 0, 1 - x, x), jnp.where(c == 0, y, 1 - y)
    rx, ry = jnp.where(c == 0, x, 1 - x), jnp.where(c == 0, 1 - y, y)
    dx, dy = 1 - x, 1 - y
    pnbr, rnbr, core = device(px, py, z, c), device(rx, ry, z, c), device(x, y, z, 1 - c)
    loads = [pltpu.make_async_copy(g_hbm.at[q, :, :, :, c], acc.at[q], lsem.at[q]) for q in range(3)]
    for cp in loads:
        cp.start()
    column = [device(x, y, (z + k) % 4, c) for k in (1, 2, 3)]
    column += [device(x, y, (z + k) % 4, 1 - c) for k in (0, 1, 2, 3)]
    plane = [device(dx, y, z, c), device(x, dy, z, c), device(dx, dy, z, c)]
    barrier = pltpu.get_barrier_semaphore()
    for peer in column + plane:
        pl.semaphore_signal(barrier, inc=1, device_id=peer, device_id_type=MESH)
    pl.semaphore_wait(barrier, len(column + plane))
    index = [0]
    started = []

    def remote(src_ref, dst_ref, dev):
        k = index[0]
        index[0] += 1
        cp = pltpu.make_async_remote_copy(
            src_ref=src_ref, dst_ref=dst_ref, send_sem=send.at[k], recv_sem=recv.at[k],
            device_id=dev, device_id_type=MESH,
        )
        cp.start()
        started.append(cp)
        return cp

    cut = acc.shape[4] // RCUTS
    cuts = [(3, 0)] + [(q, s) for s in range(RCUTS) for q in range(3)]

    def views(k):
        q, s = cuts[k]
        if q == 3:
            return (
                F32, lambda *i: sacc.at[i], lambda *i: src.at[i], lambda *i: srr.at[i],
                lambda *i: srp.at[i], lambda *i: srz.at[i],
            )
        at = pl.ds(s * cut, cut)

        def of(ref, dims):
            def view(*i):
                rest = (slice(None),) * (dims - len(i))
                return ref.at[(q,) + i + rest + (at,)]

            return view

        return BF, of(acc, 3), of(rc, 3), of(rr, 2), of(rp, 1), of(rz, 1)

    def plus(kind, a, b):
        a[...] = (a[...].astype(F32) + b[...].astype(F32)).astype(kind)

    swaps, r_in, p_in, z_in = {}, {}, {}, {}
    scopy = pltpu.make_async_copy(small_ref.at[:, :, :, c], sacc, lsem.at[3])
    scopy.start()
    for k, (q, s) in enumerate(cuts):
        if q == 3:
            swaps[k] = remote(small_ref.at[:, :, :, 1 - c], src, core)
        else:
            at = pl.ds(s * cut, cut)
            swaps[k] = remote(g_hbm.at[q, :, :, :, 1 - c, at], rc.at[q, :, :, :, at], core)

    def stage_two(k):
        kind, a, b, r, p, zz = views(k)
        if k == 0:
            scopy.wait()
        elif k <= 3:
            loads[cuts[k][0]].wait()
        swaps[k].wait_recv()
        for ly in range(2):
            for lx in range(2):
                for lz in range(4):
                    plus(kind, a(ly, lx, lz), b(ly, lx, lz))
        r_in[k] = [remote(a(dy, dx), r(0), rnbr), remote(a(ry, rx), r(1), rnbr)]

    def stage_three(k):
        kind, a, b, r, p, zz = views(k)
        for cp in r_in[k]:
            cp.wait_recv()
        for lz in range(4):
            plus(kind, a(py, px, lz), r(0, lz))
        p_in[k] = remote(a(py, px), p(), pnbr)
        for lz in range(4):
            plus(kind, a(y, x, lz), r(1, lz))

    def stage_four(k):
        kind, a, b, r, p, zz = views(k)
        p_in[k].wait_recv()
        for lz in range(4):
            plus(kind, a(y, x, lz), p(lz))
        z_in[k] = [
            remote(a(y, x, (z + j) % 4), zz(j - 1), device(x, y, (z + j) % 4, c)) for j in (1, 2, 3)
        ]

    def fold(v):
        t = jnp.zeros((8, 128), F32)
        for r in range(0, v.shape[0], 8):
            for l in range(0, v.shape[1], 128):
                part = v[r : r + 8, l : l + 128]
                t = t + part * part
        return t

    squares = [jnp.zeros((8, 128), F32)]
    tots = []

    def stage_five(k):
        kind, a, b, r, p, zz = views(k)
        for cp in z_in[k]:
            cp.wait_recv()
        v = (a(y, x, z)[...].astype(F32) + zz(0)[...].astype(F32)) + (
            zz(1)[...].astype(F32) + zz(2)[...].astype(F32)
        )
        squares[0] = squares[0] + fold(v)
        q, s = cuts[k]
        if q == 3:
            tot_ref[y, x, z, c] = v
            mine = tot_ref.at[y, x, z, c]
            tots.append([remote(mine, mine, dev) for dev in column])
        else:
            red_ref[q, s * cut : (s + 1) * cut] = v

    n = len(cuts)
    for t in range(n + 3 * RLAG):
        if t < n:
            stage_two(t)
        if 0 <= t - RLAG < n:
            stage_three(t - RLAG)
        if 0 <= t - 2 * RLAG < n:
            stage_four(t - 2 * RLAG)
        if 0 <= t - 3 * RLAG < n:
            stage_five(t - 3 * RLAG)
        if t == n:
            for cp in tots[0]:
                cp.wait_recv()
            lines = tot_ref.at[y, x]
            tots.append([remote(lines, lines, dev) for dev in plane])
    nown[...] = squares[0]
    sent = [remote(nown, nbuf.at[z * 2 + c], dev) for dev in column]
    nbuf[z * 2 + c] = squares[0]
    for cp in sent:
        cp.wait_recv()
    total = nbuf[0]
    for i in range(1, 8):
        total = total + nbuf[i]
    mown[...] = total
    sent = [remote(mown, mbuf.at[y * 2 + x], dev) for dev in plane]
    mbuf[y * 2 + x] = total
    for cp in sent:
        cp.wait_recv()
    total = mbuf[0]
    for i in range(1, 4):
        total = total + mbuf[i]
    total = jnp.sum(jnp.sum(total, axis=0, keepdims=True), axis=1, keepdims=True)
    norm_ref[...] = jnp.broadcast_to(jnp.sqrt(total), norm_ref.shape)
    for cp in tots[1]:
        cp.wait_recv()
    for cp in started:
        cp.wait_send()


RCUTS = 3
RLAG = 2
NRED = 7 * (3 * RCUTS + 1) + 20


def reduce_all(g, small):
    rows, width = g.shape[-2:]
    vmem = pl.BlockSpec(memory_space=pltpu.VMEM)
    anyb = pl.BlockSpec(memory_space=pl.ANY)
    dma = pltpu.SemaphoreType.DMA
    blk, sblk = (rows, width), small.shape[-2:]
    return pl.pallas_call(
        reduce_kernel,
        out_shape=(
            jax.ShapeDtypeStruct((3,) + blk, F32),
            jax.ShapeDtypeStruct(small.shape, F32),
            jax.ShapeDtypeStruct((8, 128), F32),
        ),
        in_specs=[anyb, vmem],
        out_specs=[vmem] * 3,
        scratch_shapes=[
            pltpu.VMEM((3, 2, 2, 4) + blk, BF),
            pltpu.VMEM((3, 2, 2, 4) + blk, BF),
            pltpu.VMEM((3, 2, 4) + blk, BF),
            pltpu.VMEM((3, 4) + blk, BF),
            pltpu.VMEM((3, 3) + blk, BF),
            pltpu.VMEM((2, 2, 4) + sblk, F32),
            pltpu.VMEM((2, 2, 4) + sblk, F32),
            pltpu.VMEM((2, 4) + sblk, F32),
            pltpu.VMEM((4,) + sblk, F32),
            pltpu.VMEM((3,) + sblk, F32),
            pltpu.VMEM((8, 8, 128), F32),
            pltpu.VMEM((4, 8, 128), F32),
            pltpu.VMEM((8, 128), F32),
            pltpu.VMEM((8, 128), F32),
            dma((NRED,)), dma((NRED,)), dma((4,)),
        ],
        compiler_params=pltpu.CompilerParams(
            collective_id=1, has_side_effects=True, vmem_limit_bytes=60 * 2**20
        ),
        name="reduce",
    )(g, small)


STEP = 10
BETA_FIRST = 0.9
BETA_SECOND = 0.95
ADAM_EPS = 1e-08
DECAY_RATE = 0.05
RATE_MATRIX = 0.05
RATE_VECTOR = 0.8
CLIP_BOUND = 1.0
BOTH = ("dp", "fsdp")


def adam_step(weight, first, second, gradient, step_rate, weight_decay):
    first_new = BETA_FIRST * first + (1.0 - BETA_FIRST) * gradient
    second_new = BETA_SECOND * second + (1.0 - BETA_SECOND) * gradient * gradient
    first_hat = first_new * (1.0 / (1.0 - BETA_FIRST**STEP))
    second_hat = second_new * (1.0 / (1.0 - BETA_SECOND**STEP))
    weight_new = weight - step_rate * (
        first_hat / (jnp.sqrt(second_hat) + ADAM_EPS) + weight_decay * weight
    )
    return (weight_new, first_new, second_new)


def adam_kernel(red, tot, norm, iw, i1, i2, ow, o1, o2, sw, s1, s2, *outs):
    clip = CLIP_BOUND / jnp.maximum(norm[0:1, 0:1], CLIP_BOUND)
    rows = ow.shape[0]
    for q in range(2):
        for r in range(0, rows, 8):
            cut = slice(r, r + 8)
            new = adam_step(
                iw[q, cut], i1[q, cut], i2[q, cut], red[q, cut] * clip, RATE_MATRIX, DECAY_RATE
            )
            for ref, val in zip(outs[0:3], new):
                ref[q, cut] = val
    for r in range(0, rows, 8):
        cut = slice(r, r + 8)
        new = adam_step(ow[cut], o1[cut], o2[cut], red[2, cut] * clip, RATE_MATRIX, DECAY_RATE)
        for ref, val in zip(outs[3:6], new):
            ref[cut] = val
    side, cols = sw.shape
    grad = tot[SPATIAL_ROW : SPATIAL_ROW + side, 0:cols] * clip
    last = lax.broadcasted_iota(jnp.int32, (side, 1), 0) == side - 1
    rate = jnp.where(last, RATE_VECTOR, RATE_MATRIX)
    decay = jnp.where(last, 0.0, DECAY_RATE)
    new = adam_step(sw[...], s1[...], s2[...], grad, rate, decay)
    for ref, val in zip(outs[6:9], new):
        ref[...] = val


def adam_all(red, tot, norm, inner, outer, spatial):
    vmem = pl.BlockSpec(memory_space=pltpu.VMEM)
    shape = lambda a: jax.ShapeDtypeStruct(a.shape, F32)
    return pl.pallas_call(
        adam_kernel,
        out_shape=tuple(shape(a) for a in inner + outer + spatial),
        in_specs=[vmem] * 12,
        out_specs=[vmem] * 9,
        compiler_params=pltpu.CompilerParams(vmem_limit_bytes=60 * 2**20),
        name="adam",
    )(red, tot, norm, *inner, *outer, *spatial)


def slow_prepare(inner_t, outer_weight, vectors, tokens, cot, mask, keep, pool_cot, spatial):
    patches, images, width = tokens.shape
    pad = -(-patches // LOT) * LOT
    wt = jnp.concatenate(
        [
            lax.all_gather(inner_t.astype(BF), BOTH, axis=1, tiled=True),
            lax.all_gather(outer_weight.astype(BF), BOTH, axis=0, tiled=True)[None],
        ],
        axis=0,
    )
    vec = lax.all_gather(vectors.astype(BF), BOTH, axis=0, tiled=True).astype(F32)
    vec = vec.reshape(-1, width)
    counts = jnp.sum(mask, axis=1)
    info = jnp.zeros((images, 128), jnp.int32).at[:, 0].set(counts).at[:, 1].set(keep)
    poolc = pool_cot.astype(F32) / counts.astype(F32)[:, None]
    unit, _ = norm(tokens.astype(F32))
    edge = ((0, 0), (0, pad - patches), (0, 0))
    nm = (unit * vec[0] + vec[1]).astype(BF)
    live = mask.astype(F32).T[:, :, None]
    scale = keep.astype(F32) * (1.0 / (1.0 - DROP_RATE))
    bg = (scale[:, None] * (cot.astype(F32) + live * poolc)).astype(BF)
    bsum = jnp.sum(bg, axis=0, dtype=F32)
    nm = jnp.pad(nm.transpose(1, 0, 2), edge)
    bg = jnp.pad((bg * live.astype(BF)).transpose(1, 0, 2), edge)
    low = spatial[:patches].astype(BF)
    square = ((0, 256 - patches), (0, 256 - patches))
    sbias = jnp.pad(spatial[patches][:, None], ((0, 256 - patches), (0, 0)))
    return wt, vec, nm, bg, info, poolc, bsum, jnp.pad(low, square), jnp.pad(low.T, square), sbias


def slow_reduce(grads, small):
    red = lax.psum_scatter(grads.astype(F32), BOTH, scatter_dimension=1, tiled=True)
    tot = lax.psum(small, BOTH)
    squares = lax.psum(jnp.sum(red * red), BOTH) + jnp.sum(tot * tot)
    return red, tot, jnp.broadcast_to(jnp.sqrt(squares), (8, 128))


def per_device(
    fast,
    tokens,
    valid_mask,
    keep_mask,
    out_cotangent,
    pool_cotangent,
    inner_weight,
    outer_weight,
    vectors,
    spatial,
    inner_first,
    inner_second,
    outer_first,
    outer_second,
    vector_first,
    vector_second,
    spatial_first,
    spatial_second,
):
    own = vectors.shape[0]
    rows, width = outer_weight.shape
    inner_t = tuple(a.transpose(0, 2, 1) for a in (inner_weight, inner_first, inner_second))
    tokens = tokens.transpose(1, 0, 2)
    cot = out_cotangent.transpose(1, 0, 2)
    if fast:
        wt, *ready = gather_all(
            own,
            inner_t[0],
            outer_weight,
            jnp.pad(vectors, (0, 1024 - own)).reshape(8, 128),
            tokens,
            cot,
            valid_mask,
            keep_mask,
            pool_cotangent,
            spatial,
        )
        wt = wt.reshape(3, 32 * rows, width)
    else:
        wt, *ready = slow_prepare(
            inner_t[0], outer_weight, vectors, tokens, cot, valid_mask, keep_mask, pool_cotangent, spatial
        )
    vec, nm, bg, info, poolc, bsum, sp, spt, sbias = ready
    output, input_grad, pooled, grads, small = run_block(
        tokens, cot, nm, bg, info, poolc, bsum, wt, vec, sp, spt, sbias
    )
    output = output.transpose(1, 0, 2)
    input_grad = input_grad.transpose(1, 0, 2)
    if fast:
        red, tot, norm = reduce_all(
            grads.reshape(3, 2, 2, 4, 2, rows, width), small.reshape(2, 2, 4, 2, 8, 256)
        )
        tot = tot.reshape(256, 256)
    else:
        red, tot, norm = slow_reduce(grads, small)
    new = adam_all(
        red,
        tot,
        norm,
        inner_t,
        (outer_weight, outer_first, outer_second),
        (spatial, spatial_first, spatial_second),
    )
    grad_norm = norm[0, 0]
    clip_factor = CLIP_BOUND / jnp.maximum(grad_norm, CLIP_BOUND)
    me = lax.axis_index("dp") * lax.axis_size("fsdp") + lax.axis_index("fsdp")
    total_vec = own * lax.axis_size("dp") * lax.axis_size("fsdp")
    flat = tot[: total_vec // 256].reshape(-1)
    vector_red = lax.dynamic_slice(flat, (me * own,), (own,))
    vector_out = adam_step(
        vectors, vector_first, vector_second, vector_red * clip_factor, RATE_VECTOR, 0.0
    )
    return (
        (output, input_grad, pooled, grad_norm)
        + tuple(a.transpose(0, 2, 1) for a in new[0:3])
        + tuple(new[3:6])
        + vector_out
        + tuple(new[6:9])
    )


def solution(mesh):
    fast = mesh.shape["dp"] == 4 and mesh.shape["fsdp"] == 8
    rows3 = P(BOTH, None, None)
    rows2 = P(BOTH, None)
    rows1 = P(BOTH)
    cols3 = P(None, None, BOTH)
    in_specs = (
        (rows3, rows2, rows1, rows3, rows2, cols3, rows2, rows1, P())
        + (cols3,) * 2
        + (rows2,) * 2
        + (rows1,) * 2
        + (P(),) * 2
    )
    out_specs = (
        (rows3, rows3, rows2, P()) + (cols3,) * 3 + (rows2,) * 3 + (rows1,) * 3 + (P(),) * 3
    )
    return jax.shard_map(
        functools.partial(per_device, fast),
        mesh=mesh,
        in_specs=in_specs,
        out_specs=out_specs,
        check_vma=False,
    )
```

```python
import functools

import jax
import jax.numpy as jnp
from jax import lax
from jax.experimental import pallas as pl
from jax.experimental.pallas import tpu as pltpu
from jax.sharding import PartitionSpec as P

NORM_EPS = 1e-05
DROP_RATE = 0.1
BF = jnp.bfloat16
F32 = jnp.float32
MESH = pl.DeviceIdType.MESH
GELU_K = 0.7978845608
GELU_C = 0.044715
NN = (((1,), (0,)), ((), ()))
NT = (((1,), (1,)), ((), ()))
TN = (((0,), (0,)), ((), ()))
LOT = 16
CUTS = 3


def dot(a, b, dims):
    return lax.dot_general(a, b, dims, preferred_element_type=F32)


def norm(x):
    c = x - jnp.mean(x, axis=-1, keepdims=True)
    inv = lax.rsqrt(jnp.mean(c * c, axis=-1, keepdims=True) + NORM_EPS)
    return c * inv, inv


def swap_matrix(images):
    side = LOT * images
    r = lax.broadcasted_iota(jnp.int32, (side, side), 0)
    s = lax.broadcasted_iota(jnp.int32, (side, side), 1)
    return jnp.where(s == (r % LOT) * images + r // LOT, 1.0, 0.0).astype(BF)


def unswap_matrix(images):
    side = LOT * images
    r = lax.broadcasted_iota(jnp.int32, (side, side), 0)
    s = lax.broadcasted_iota(jnp.int32, (side, side), 1)
    return jnp.where(s == (r % images) * LOT + r // images, 1.0, 0.0).astype(BF)


def place():
    d = lax.axis_index("dp")
    f = lax.axis_index("fsdp")
    return d % 2, d // 2, f // 2, f % 2


def device(x, y, z, c):
    return (y * 2 + x, z * 2 + c)


def greet_partners():
    x, y, z, c = place()
    barrier = pltpu.get_barrier_semaphore()
    peers = [device(1 - x, y, z, c), device(x, 1 - y, z, c), device(x, y, z, 1 - c)]
    peers += [device(x, y, (z + k) % 4, c) for k in (1, 2, 3)]
    for peer in peers:
        pl.semaphore_signal(barrier, inc=1, device_id=peer, device_id_type=MESH)
    pl.semaphore_wait(barrier, len(peers))


def gather_kernel(
    own_len,
    inner_ref, outer_ref, vec_ref, tokens_hbm, cot_hbm, mask_ref, keep_ref, pool_ref, spatial_ref,
    all_ref, vecs_ref, nm_ref, bg_ref, info_ref, poolc_ref, bsum_ref, sp_ref, spt_ref, sbias_ref,
    own, vown, vgot, wide, xblk, cblk, nrow, brow, nm_v, bg_v, send, recv, lsem, isem, osem,
):
    x, y, z, c = place()
    patches, images, width = tokens_hbm.shape
    own[0] = inner_ref[0].astype(BF)
    own[1] = inner_ref[1].astype(BF)
    own[2] = outer_ref[...].astype(BF)
    vown[...] = vec_ref[...].astype(BF).astype(F32)
    loads = [
        pltpu.make_async_copy(tokens_hbm, xblk, isem.at[0]),
        pltpu.make_async_copy(cot_hbm, cblk, isem.at[1]),
    ]
    for cp in loads:
        cp.start()
    greet_partners()
    local = pltpu.make_async_copy(own, all_ref.at[:, y, x, z, c], lsem)
    local.start()
    vgot[y, x, z, c] = vown[...]

    px, py = jnp.where(c == 0, 1 - x, x), jnp.where(c == 0, y, 1 - y)
    rx, ry = jnp.where(c == 0, x, 1 - x), jnp.where(c == 0, 1 - y, y)
    dx, dy = 1 - x, 1 - y
    index = [0]
    pnbr, rnbr, core = device(px, py, z, c), device(rx, ry, z, c), device(x, y, z, 1 - c)
    cut = outer_ref.shape[0] // CUTS
    started = []

    def remote(src, dst, dev):
        k = index[0]
        index[0] += 1
        cp = pltpu.make_async_remote_copy(
            src_ref=src, dst_ref=dst, send_sem=send.at[k], recv_sem=recv.at[k],
            device_id=dev, device_id_type=MESH,
        )
        cp.start()
        started.append(cp)
        return cp

    def span(s):
        return pl.ds(s * cut, cut)

    def block(q, s, by, bx):
        if q == 3:
            return vgot.at[by, bx, z, c]
        return all_ref.at[q, by, bx, z, c, span(s)]

    def z_sends(src, q, s, by, bx):
        return [remote(src, block(q, s, by, bx), device(x, y, (z + k) % 4, c)) for k in (1, 2, 3)]

    def send_line(q, s, ly, lx, dev):
        ref = vgot.at[ly, lx, :, c] if q == 3 else all_ref.at[q, ly, lx, :, c, span(s)]
        return remote(ref, ref, dev)

    cuts = [(3, 0)] + [(q, s) for s in range(CUTS) for q in range(3)]
    zs = [None] * len(cuts)

    def start_z(k):
        if k < len(cuts):
            q, s = cuts[k]
            src = vown if q == 3 else own.at[q, span(s)]
            zs[k] = z_sends(src, q, s, y, x)

    for k in range(WINDOW):
        start_z(k)
    local.wait()

    counts = jnp.sum(mask_ref[...], axis=1, keepdims=True)
    keeps = jnp.zeros((images, 1), jnp.int32)
    image = lax.broadcasted_iota(jnp.int32, (images, 1), 0)
    for b in range(images):
        keeps = jnp.where(image == b, keep_ref[b], keeps)
    scale = keeps.astype(F32) * (1.0 / (1.0 - DROP_RATE))
    lane = lax.broadcasted_iota(jnp.int32, info_ref.shape, 1)
    info_ref[...] = jnp.where(lane == 0, counts, keeps)
    poolc = pool_ref[...].astype(F32) / counts.astype(F32)
    poolc_ref[...] = poolc
    side = spatial_ref.shape[1]
    wide[...] = jnp.zeros_like(wide)
    wide[0 : side + 1, 0:side] = spatial_ref[...]
    mat = wide[...]
    mat_t = mat.T
    span_a = lax.broadcasted_iota(jnp.int32, mat.shape, 0)
    span_b = lax.broadcasted_iota(jnp.int32, mat.shape, 1)
    sp_ref[...] = jnp.where(span_a < side, mat, 0.0).astype(BF)
    spt_ref[...] = jnp.where(span_b < side, mat_t, 0.0).astype(BF)
    sbias_ref[...] = mat_t[:, side : side + 1]
    bsum_ref[...] = jnp.zeros_like(bsum_ref)
    vecs_ref[...] = jnp.zeros_like(vecs_ref)

    def stack_vectors():
        per = width // 128
        for d in range(32):
            start = own_len * d
            shift = start % 128
            blk = vgot[d // 16, d // 8 % 2, d // 2 % 4, d % 2]
            row = jnp.concatenate(
                [jnp.broadcast_to(blk[i : i + 1, :], (8, 128)) for i in range(3)], axis=1
            )
            row = pltpu.roll(row, shift, 1) if shift else row
            for i in range(3):
                r = start // 128 + i
                if r * 128 < start + own_len:
                    at = (slice(r // per, r // per + 1), slice(r % per * 128, r % per * 128 + 128))
                    vecs_ref[at] += row[0:1, i * 128 : i * 128 + 128]

    swap = swap_matrix(images)

    def token_block(k, many):
        gain, shift = vecs_ref[0:1, :], vecs_ref[1:2, :]
        for p in range(many):
            patch = k * LOT + p
            xv = xblk[patch].astype(F32)
            unit, _ = norm(xv)
            nrow[p * images : (p + 1) * images, :] = (unit * gain + shift).astype(BF)
            live = jnp.where(counts > patch, 1.0, 0.0)
            og = cblk[patch].astype(F32) + live * poolc
            bg = (scale * og).astype(BF).astype(F32)
            bsum_ref[...] += bg
            brow[p * images : (p + 1) * images, :] = (live * bg).astype(BF)
        part = swap[:, 0 : many * images]
        for src, dst in ((nrow, nm_v), (brow, bg_v)):
            moved = dot(part, src[0 : many * images, :], NN).astype(BF)
            at = pl.ds(pl.multiple_of(k * LOT, LOT), LOT)
            dst[:, at, :] = moved.reshape(images, LOT, width)

    full = patches // LOT
    todo = list(range(full + (1 if patches % LOT else 0)))

    stores = []
    pad = nm_v.shape[1]
    marks = [pad // (2 * LOT) * LOT, pad]

    def some_tokens(many):
        for _ in range(many):
            if not todo:
                return
            k = todo.pop(0)
            token_block(k, LOT if k < full else patches % LOT)
            end = (k + 1) * LOT
            if end in marks:
                at = pl.ds(0, end) if end == marks[0] else pl.ds(marks[0], end - marks[0])
                for src, dst in ((nm_v, nm_ref), (bg_v, bg_ref)):
                    cp = pltpu.make_async_copy(src.at[:, at], dst.at[:, at], osem.at[len(stores)])
                    cp.start()
                    stores.append(cp)

    lines_p, lines_r, lines_r2, cores = {}, {}, {}, {}

    def swap_core(k, cp):
        cores.setdefault(k, []).append(cp)


    def stage_two(k):
        q, s = cuts[k]
        for cp in zs[k]:
            cp.wait_recv()
        start_z(k + WINDOW)
        lines_p[k] = send_line(q, s, y, x, pnbr)
        lines_r[k] = send_line(q, s, y, x, rnbr)
        swap_core(k, send_line(q, s, y, x, core))

    def stage_three(k):
        q, s = cuts[k]
        lines_p[k].wait_recv()
        lines_r2[k] = send_line(q, s, py, px, rnbr)
        swap_core(k, send_line(q, s, py, px, core))

    def stage_four(k):
        q, s = cuts[k]
        lines_r[k].wait_recv()
        swap_core(k, send_line(q, s, ry, rx, core))

    def stage_five(k):
        q, s = cuts[k]
        lines_r2[k].wait_recv()
        swap_core(k, send_line(q, s, dy, dx, core))

    n = len(cuts)
    for t in range(n + LAG_FIVE):
        if t < n:
            stage_two(t)
        if 0 <= t - LAG_THREE < n:
            stage_three(t - LAG_THREE)
            stage_four(t - LAG_THREE)
        if 0 <= t - LAG_FIVE < n:
            stage_five(t - LAG_FIVE)
        if t == LAG_FIVE + 1:
            for cp in cores[0]:
                cp.wait_recv()
            stack_vectors()
            for cp in loads:
                cp.wait()
        if t > LAG_FIVE:
            some_tokens(-(-13 // (n - 1)))
    some_tokens(len(todo))
    for k in range(1, n):
        for cp in cores[k]:
            cp.wait_recv()
    for cp in started:
        cp.wait_send()
    for cp in stores:
        cp.wait()


NSEND = 10 * (3 * CUTS + 1)
LAG_THREE = 3
LAG_FIVE = 6
WINDOW = 4


def gather_all(own_len, inner, outer, vec, tokens, cot, mask, keep, pool, spatial):
    rows, width = outer.shape
    patches, images, _ = tokens.shape
    pad = -(-patches // LOT) * LOT
    vmem = pl.BlockSpec(memory_space=pltpu.VMEM)
    smem = pl.BlockSpec(memory_space=pltpu.SMEM)
    anyb = pl.BlockSpec(memory_space=pl.ANY)
    dma = pltpu.SemaphoreType.DMA
    shape = jax.ShapeDtypeStruct
    return pl.pallas_call(
        functools.partial(gather_kernel, own_len),
        out_shape=(
            shape((3, 2, 2, 4, 2, rows, width), BF),
            shape((16, width), F32),
            shape((images, pad, width), BF),
            shape((images, pad, width), BF),
            shape((images, 128), jnp.int32),
            shape((images, width), F32),
            shape((images, width), F32),
            shape((256, 256), BF),
            shape((256, 256), BF),
            shape((256, 1), F32),
        ),
        in_specs=[vmem] * 3 + [anyb] * 2 + [vmem, smem, vmem, vmem],
        out_specs=[anyb, vmem, anyb, anyb] + [vmem] * 6,
        scratch_shapes=[
            pltpu.VMEM((3, rows, width), BF),
            pltpu.VMEM((8, 128), F32),
            pltpu.VMEM((2, 2, 4, 2, 8, 128), F32),
            pltpu.VMEM((256, 256), F32),
            pltpu.VMEM((patches, images, width), BF),
            pltpu.VMEM((patches, images, width), BF),
            pltpu.VMEM((LOT * images, width), BF),
            pltpu.VMEM((LOT * images, width), BF),
            pltpu.VMEM((images, pad, width), BF),
            pltpu.VMEM((images, pad, width), BF),
            dma((NSEND,)), dma((NSEND,)), dma, dma((2,)), dma((4,)),
        ],
        compiler_params=pltpu.CompilerParams(
            collective_id=0, has_side_effects=True, vmem_limit_bytes=60 * 2**20
        ),
        name="gather",
    )(inner, outer, vec, tokens, cot, mask, keep, pool, spatial)


def gelu_pair(v):
    u = v * v
    s = 0.5 * jnp.tanh(v * (GELU_K + (GELU_K * GELU_C) * u)) + 0.5
    h = v * s
    d = s + (h - h * s) * (2.0 * GELU_K + (6.0 * GELU_K * GELU_C) * u)
    return h, d


def fold8(x):
    total = x[0:8]
    for r in range(8, x.shape[0], 8):
        total = total + x[r : r + 8]
    return total


def lanes(x):
    total = x[:, 0:128]
    for c in range(128, x.shape[1], 128):
        total = total + x[:, c : c + 128]
    return total


def loop(lo, hi, fn):
    def body(i, c):
        fn(i)
        return c

    lax.fori_loop(lo, hi, body, 0)


def block_kernel(
    cfg,
    info_s,
    tokens_hbm, cot_hbm, nm_hbm, bg_hbm,
    info_ref, poolc_ref, bsum_ref, wt_hbm, vec_ref, sp_ref, spt_ref, sbias_ref,
    out_hbm, ig_hbm, pooled_ref, grads_hbm, small_ref,
    acc, sg_ref, sbg_ref, off_s, gend_s, grows_s,
    wt_ref, wtt, nm_b, bg_b, h0_b, e0_b, mg_b, xm_b, u2_b, d1_b, stat_b, h1_s, t_s,
    xblk, cblk, br_s, ng_s, out_st, ig_st, vacc,
    wt_sem, pack_sem, in_sem, out_sem, grad_sem,
):
    images, patches, width, gate, rows_cap, tm, classes = cfg
    cw = 256
    nj = gate // cw
    chunks = -(-patches // LOT)
    zero_row = nm_b.shape[0] - LOT
    g2_base, s2_base = 3 * width, 3 * width + gate
    b0_base, b1_base = 3 * width + 2 * gate, 3 * width + 3 * gate

    def vrow(base, j):
        start = base + j * cw
        return vec_ref[start // width : start // width + 1, start % width : start % width + cw]

    def count(b):
        return info_s[b, 0]

    def keep(b):
        return info_s[b, 1]

    def need_of(b):
        return keep(b) * ((count(b) + LOT - 1) // LOT)

    wt_loads = [pltpu.make_async_copy(wt_hbm.at[q], wt_ref.at[q], wt_sem.at[q]) for q in range(3)]
    for q in (1, 0, 2):
        wt_loads[q].start()

    def plan(b, carry):
        group, row, first = carry
        need = need_of(b) * LOT
        over = row + need - first > rows_cap
        group = group + over.astype(jnp.int32)
        first = jnp.where(over, row, first)
        off_s[b] = row
        row = row + need
        gend_s[group] = b + 1
        grows_s[group] = row - first
        return group, row, first

    zero = jnp.int32(0)
    last_group, all_rows, _ = lax.fori_loop(0, images, plan, (zero, zero, zero))

    def pack(b, act):
        lots = need_of(b)
        o = off_s[b]
        done = jnp.int32(0)
        for size in (8, 4, 2, 1):
            @pl.when((lots & size) != 0)
            def _(size=size, done=done):
                src = pl.ds(pl.multiple_of(done * LOT, LOT), size * LOT)
                dst = pl.ds(pl.multiple_of(o + done * LOT, LOT), size * LOT)
                for i, (far, near) in enumerate(((nm_hbm, nm_b), (bg_hbm, bg_b))):
                    act(pltpu.make_async_copy(far.at[b, src], near.at[dst], pack_sem.at[i, b]))

            done = done + (lots & size)

    loop(0, images, lambda b: pack(b, lambda cp: cp.start()))

    full = patches // LOT
    rest = patches % LOT

    def load_lot(k, many, slot):
        at = pl.ds(k * LOT, many)
        return (
            pltpu.make_async_copy(tokens_hbm.at[at], xblk.at[slot, pl.ds(0, many)], in_sem.at[0, slot]),
            pltpu.make_async_copy(cot_hbm.at[at], cblk.at[slot, pl.ds(0, many)], in_sem.at[1, slot]),
        )

    for k in (0, 1):
        for cp in load_lot(k, LOT, k):
            cp.start()

    def zero_rows(ref, n_chunks, start):
        z = jnp.zeros((LOT, ref.shape[1]), ref.dtype)

        def body(i):
            ref[pl.ds(pl.multiple_of(start + i * LOT, LOT), LOT), :] = z

        loop(0, n_chunks, body)

    for ref in (mg_b, xm_b, u2_b):
        zero_rows(ref, ref.shape[0] // LOT, 0)
    for ref in (nm_b, bg_b):
        zero_rows(ref, tm // LOT, all_rows)
    z = jnp.zeros((LOT, width), BF)
    nm_b[zero_row : zero_row + LOT, :] = z
    bg_b[zero_row : zero_row + LOT, :] = z
    vacc[...] = jnp.zeros_like(vacc)
    acc[...] = jnp.zeros_like(acc)
    sg_ref[...] = jnp.zeros_like(sg_ref)
    sbg_ref[...] = jnp.zeros_like(sbg_ref)
    for q in (1, 0, 2):
        wt_loads[q].wait()
        for j in range(nj):
            wtt[q, :, j * cw : (j + 1) * cw] = wt_ref[q, j * cw : (j + 1) * cw, :].T
    loop(0, images, lambda b: pack(b, lambda cp: cp.wait()))

    def phase_a(t, gs):
        r0 = pl.multiple_of(t * tm, tm)
        rows = pl.ds(r0, tm)
        here = pl.ds(pl.multiple_of(gs + r0, LOT), tm)
        nb = nm_b[here, :]
        bgt = bg_b[here, :]
        s1 = jnp.zeros((tm, 128), F32)
        for j in range(nj):
            cols = slice(j * cw, (j + 1) * cw)
            a1 = dot(nb, wtt[1, :, cols], NN) + vrow(b1_base, j)
            h1, d1 = gelu_pair(a1)
            h1_s[:, cols] = h1
            d1_b[rows, cols] = d1.astype(BF)
            s1 = s1 + lanes(h1)
        mean = jnp.sum(s1, axis=1, keepdims=True) * (1.0 / gate)
        q1 = jnp.zeros((tm, 128), F32)
        for j in range(nj):
            cols = slice(j * cw, (j + 1) * cw)
            a0 = dot(nb, wtt[0, :, cols], NN) + vrow(b0_base, j)
            h0, d0 = gelu_pair(a0)
            gg = dot(bgt, wtt[2, :, cols], NN)
            mg = gg * h0
            h0_b[rows, cols] = h0.astype(BF)
            mg_b[rows, cols] = mg.astype(BF)
            e0_b[rows, cols] = (gg * d0).astype(BF)
            c = h1_s[:, cols] - mean
            q1 = q1 + lanes(c * c)
        inv = lax.rsqrt(jnp.sum(q1, axis=1, keepdims=True) * (1.0 / gate) + NORM_EPS)
        stat_b[rows, :] = jnp.broadcast_to(inv, (tm, 128))
        for j in range(nj):
            cols = slice(j * cw, (j + 1) * cw)
            u2 = (h1_s[:, cols] - mean) * inv
            u2_b[rows, cols] = u2.astype(BF)
            xm_b[rows, cols] = (u2 * vrow(g2_base, j) + vrow(s2_base, j)).astype(BF)

    def phase_b(b, m, gs):
        n = count(b)
        o = pl.multiple_of(off_s[b] - gs, LOT)
        rows = pl.ds(o, m)
        rid = lax.broadcasted_iota(jnp.int32, (m, 1), 0)
        cid = lax.broadcasted_iota(jnp.int32, (m, m), 1)
        rid2 = lax.broadcasted_iota(jnp.int32, (m, m), 0)
        both = (cid < n) & (rid2 < n)
        sp = jnp.where(both, sp_ref[0:m, 0:m], 0.0).astype(BF)
        spt = jnp.where(both, spt_ref[0:m, 0:m], 0.0).astype(BF)
        valid = rid < n
        fill = jnp.where(rid < need_of(b) * LOT, 0.0, 1.0)
        sbias = jnp.where(valid, sbias_ref[0:m, :], fill)
        inv = jnp.where(valid, stat_b[rows, 0:1], 0.0)
        ones = jnp.ones((LOT, gate), BF)
        tsum = jnp.zeros((m, 128), F32)
        tdot = jnp.zeros((m, 128), F32)
        xm_ones = jnp.concatenate([xm_b[rows, :], ones], axis=0)
        sg = dot(mg_b[rows, :], xm_ones, NT)
        sg_ref[0:m, 0:m] += jnp.where(both, sg[:, 0:m], 0.0)
        sbg_ref[0:m, 0:1] += jnp.where(valid, sg[:, m : m + 1], 0.0)
        for j in range(nj):
            cols = slice(j * cw, (j + 1) * cw)
            xm = xm_b[rows, cols]
            mg = mg_b[rows, cols]
            so = (dot(sp, xm, NN) + sbias).astype(BF)
            mix = dot(spt, mg, NN)
            h0_b[rows, cols] = h0_b[rows, cols] * so
            e0_b[rows, cols] = e0_b[rows, cols] * so
            u2 = u2_b[rows, cols].astype(F32)
            mu = mix * u2
            gain = vrow(g2_base, j)
            t = mix * gain
            t_s[0:m, cols] = t
            tsum = tsum + lanes(t)
            tdot = tdot + lanes(mu * gain)
            vi, lo = j * cw // width, j * cw % width
            vacc[g2_base // width + vi, :, lo : lo + cw] += fold8(mu)
            vacc[s2_base // width + vi, :, lo : lo + cw] += fold8(mix)
        m1 = jnp.sum(tsum, axis=1, keepdims=True) * (1.0 / gate)
        m2 = jnp.sum(tdot, axis=1, keepdims=True) * (1.0 / gate)
        base, slope = fill - inv * m1, inv * m2
        for j in range(nj):
            cols = slice(j * cw, (j + 1) * cw)
            u2 = u2_b[rows, cols].astype(F32)
            sec = (inv * t_s[0:m, cols] + (base - u2 * slope)).astype(BF)
            d1_b[rows, cols] = d1_b[rows, cols] * sec

    def phase_c(t, gs, group_rows):
        r0 = pl.multiple_of(t * tm, tm)
        rows = pl.ds(r0, tm)
        here = pl.ds(pl.multiple_of(gs + r0, LOT), tm)
        nb = nm_b[here, :]
        bgt = bg_b[here, :]
        mine = lax.broadcasted_iota(jnp.int32, (tm, 1), 0) < group_rows - r0
        br = dot(h0_b[rows, :], wt_ref[2], NN)
        bg_b[here, :] = jnp.where(mine, br, bgt.astype(F32)).astype(BF)
        ng = dot(e0_b[rows, :], wt_ref[0], NN) + dot(d1_b[rows, :], wt_ref[1], NN)
        nm_b[here, :] = jnp.where(mine, ng, nb.astype(F32)).astype(BF)
        for j in range(nj):
            cols = slice(j * cw, (j + 1) * cw)
            vi, lo = j * cw // width, j * cw % width
            e0, d1 = e0_b[rows, cols], d1_b[rows, cols]
            acc[0, cols, :] += dot(e0, nb, TN)
            acc[1, cols, :] += dot(d1, nb, TN)
            acc[2, cols, :] += dot(h0_b[rows, cols], bgt, TN)
            vacc[b0_base // width + vi, :, lo : lo + cw] += fold8(e0.astype(F32))
            vacc[b1_base // width + vi, :, lo : lo + cw] += fold8(d1.astype(F32))

    def group(g, carry):
        b_start, gs = carry
        b_end = gend_s[g]
        rows = grows_s[g]
        tiles = (rows + tm - 1) // tm
        loop(0, tiles, lambda t: phase_a(t, gs))

        def do_b(b):
            low = 0
            for m in classes:
                @pl.when((keep(b) == 1) & (count(b) > low) & (count(b) <= m))
                def _(m=m):
                    phase_b(b, m, gs)

                low = m

        loop(b_start, b_end, do_b)
        tail = (tiles * tm - rows) // LOT
        for ref in (h0_b, e0_b, d1_b):
            zero_rows(ref, tail, rows)
        loop(0, tiles, lambda t: phase_c(t, gs, rows))
        return b_end, gs + rows

    lax.fori_loop(0, last_group + 1, group, (zero, zero))

    half = gate // 2
    grad_out = []
    per = gate // width
    for i in range(6):
        q, lo = i // 2, (i % 2) * half
        buf = (h1_s, t_s)[0]
        del buf
        stage = (mg_b, xm_b)[i % 2]
        if i >= 2:
            for cp in grad_out[i - 2]:
                cp.wait()
        cps = []
        for v in range(per):
            third = half // per
            cut = slice(v * width, (v + 1) * width)
            stage[0:third, cut] = acc[q, lo + v * third : lo + (v + 1) * third, :].astype(BF)
            cps.append(
                pltpu.make_async_copy(
                    stage.at[pl.ds(0, third), pl.ds(v * width, width)],
                    grads_hbm.at[q, pl.ds(lo + v * third, third)],
                    grad_sem.at[i, v],
                )
            )
        for cp in cps:
            cp.start()
        grad_out.append(cps)

    counts = info_ref[:, 0:1]
    live_counts = counts * info_ref[:, 1:2]
    scale = info_ref[:, 1:2].astype(F32) * (1.0 / (1.0 - DROP_RATE))
    poolc = poolc_ref[...]
    gain_one, bias_out = vec_ref[0:1, :], vec_ref[2:3, :]
    back = unswap_matrix(images)

    def store_lot(k, many, slot):
        at = pl.ds(k * LOT, many)
        return (
            pltpu.make_async_copy(out_st.at[slot, pl.ds(0, many)], out_hbm.at[at], out_sem.at[0, slot]),
            pltpu.make_async_copy(ig_st.at[slot, pl.ds(0, many)], ig_hbm.at[at], out_sem.at[1, slot]),
        )

    pooled_ref[...] = jnp.zeros_like(pooled_ref)

    def lot(k, many, slot):
        for cp in load_lot(k, many, slot):
            cp.wait()
        parts = [[], []]
        for b in range(images):
            there = k < need_of(b)
            row = pl.multiple_of(jnp.where(there, off_s[b] + k * LOT, zero_row), LOT)
            parts[0].append(bg_b[pl.ds(row, LOT), :])
            parts[1].append(nm_b[pl.ds(row, LOT), :])
        mat = back[0 : many * images, :]
        br_s[0 : many * images, :] = dot(mat, jnp.concatenate(parts[0], axis=0), NN)
        ng_s[0 : many * images, :] = dot(mat, jnp.concatenate(parts[1], axis=0), NN)
        psum = jnp.zeros((images, width), F32)
        g1 = jnp.zeros((images, width), F32)
        s1 = jnp.zeros((images, width), F32)
        for p in range(many):
            patch = k * LOT + p
            x = xblk[slot, p].astype(F32)
            unit, inv = norm(x)
            live = jnp.where(counts > patch, 1.0, 0.0)
            og = cblk[slot, p].astype(F32) + live * poolc
            cut = slice(p * images, (p + 1) * images)
            out = x + scale * (br_s[cut, :] + bias_out)
            out_st[slot, p] = out
            psum = psum + live * out
            ng = ng_s[cut, :]
            t = ng * gain_one
            m1 = jnp.mean(t, axis=-1, keepdims=True)
            m2 = jnp.mean(t * unit, axis=-1, keepdims=True)
            ig_st[slot, p] = og + inv * (t - m1 - unit * m2)
            g1 = g1 + ng * unit
            s1 = s1 + ng
        pooled_ref[...] += psum
        vacc[0] += fold8(g1)
        vacc[1] += fold8(s1)
        for cp in store_lot(k, many, slot):
            cp.start()

    def lots(k):
        slot = lax.rem(k, 2)

        @pl.when(k >= 2)
        def _():
            for cp in store_lot(k - 2, LOT, slot):
                cp.wait()

        lot(k, LOT, slot)

        @pl.when(k + 2 < full)
        def _():
            for cp in load_lot(k + 2, LOT, slot):
                cp.start()

        if rest:
            @pl.when(k + 2 == full)
            def _():
                for cp in load_lot(full, rest, full % 2):
                    cp.start()

    loop(0, full, lots)
    if rest:
        for cp in store_lot(full - 2, LOT, full % 2):
            cp.wait()
        lot(full, rest, full % 2)
    pooled_ref[...] = pooled_ref[...] / counts.astype(F32)

    vacc[2] += fold8(bsum_ref[...])
    small_ref[...] = jnp.zeros_like(small_ref)
    sums = jnp.sum(vacc[...], axis=1)
    for v in range(sums.shape[0]):
        for h in range(width // 256):
            row = v * (width // 256) + h
            small_ref[row : row + 1, :] = sums[v : v + 1, h * 256 : (h + 1) * 256]
    pad = sg_ref.shape[0]
    small_ref[SPATIAL_ROW : SPATIAL_ROW + pad, 0:pad] = sg_ref[...]
    bias = sbg_ref[:, 0:1]
    eye = lax.broadcasted_iota(jnp.int32, (pad, pad), 0) == lax.broadcasted_iota(jnp.int32, (pad, pad), 1)
    bias_row = jnp.sum(jnp.where(eye, bias, 0.0), axis=0, keepdims=True)
    small_ref[SPATIAL_ROW + patches : SPATIAL_ROW + patches + 1, 0:pad] = bias_row
    for cps in grad_out[4:]:
        for cp in cps:
            cp.wait()
    if rest:
        for cp in store_lot(full - 1, LOT, (full - 1) % 2) + store_lot(full, rest, full % 2):
            cp.wait()
    else:
        for k in (full - 2, full - 1):
            for cp in store_lot(k, LOT, k % 2):
                cp.wait()


SPATIAL_ROW = 32


def run_block(
    tokens, cot, nm, bg, info, poolc, bsum, wt, vec, sp, spt, sbias,
    *, rows_cap=1024, tm=256, classes=(96, 144, 208),
):
    patches, images, width = tokens.shape
    gate = wt.shape[1]
    pad = -(-patches // LOT) * LOT
    classes = tuple(m for m in classes if m < pad) + (pad,)
    cap = rows_cap + pad + 48
    cap = -(-cap // tm) * tm
    long = images * pad + tm + LOT
    cfg = (images, patches, width, gate, rows_cap, tm, classes)
    smem = pl.BlockSpec(memory_space=pltpu.SMEM)
    vmem = pl.BlockSpec(memory_space=pltpu.VMEM)
    anyb = pl.BlockSpec(memory_space=pl.ANY)
    dma = pltpu.SemaphoreType.DMA
    shape = jax.ShapeDtypeStruct
    nvec = 3 + 4 * gate // width
    return pl.pallas_call(
        functools.partial(block_kernel, cfg),
        out_shape=(
            shape((patches, images, width), F32),
            shape((patches, images, width), F32),
            shape((images, width), F32),
            shape((3, gate, width), BF),
            shape((256, 256), F32),
        ),
        in_specs=[smem] + [anyb] * 4 + [vmem] * 3 + [anyb] + [vmem] * 4,
        out_specs=[anyb, anyb, vmem, anyb, vmem],
        scratch_shapes=[
            pltpu.VMEM((3, gate, width), F32),
            pltpu.VMEM((pad, pad), F32),
            pltpu.VMEM((pad, 128), F32),
            pltpu.SMEM((images,), jnp.int32),
            pltpu.SMEM((images,), jnp.int32),
            pltpu.SMEM((images,), jnp.int32),
            pltpu.VMEM((3, gate, width), BF),
            pltpu.VMEM((3, width, gate), BF),
            pltpu.VMEM((long, width), BF),
            pltpu.VMEM((long, width), BF),
        ]
        + [pltpu.VMEM((cap, gate), BF)] * 6
        + [
            pltpu.VMEM((cap, 128), F32),
            pltpu.VMEM((tm, gate), F32),
            pltpu.VMEM((pad, gate), F32),
            pltpu.VMEM((2, LOT, images, width), BF),
            pltpu.VMEM((2, LOT, images, width), BF),
            pltpu.VMEM((LOT * images, width), F32),
            pltpu.VMEM((LOT * images, width), F32),
            pltpu.VMEM((2, LOT, images, width), F32),
            pltpu.VMEM((2, LOT, images, width), F32),
            pltpu.VMEM((nvec, 8, width), F32),
            dma((3,)),
            dma((2, images)),
            dma((2, 2)),
            dma((2, 2)),
            dma((6, gate // width)),
        ],
        compiler_params=pltpu.CompilerParams(vmem_limit_bytes=60 * 2**20),
        name="block",
    )(info, tokens, cot, nm, bg, info, poolc, bsum, wt, vec, sp, spt, sbias)


def reduce_kernel(
    g_hbm, small_ref, red_ref, tot_ref, norm_ref,
    acc, rc, rr, rp, rz, sacc, src, srr, srp, srz, nbuf, mbuf, nown, mown,
    send, recv, lsem,
):
    x, y, z, c = place()
    px, py = jnp.where(c == 0, 1 - x, x), jnp.where(c == 0, y, 1 - y)
    rx, ry = jnp.where(c == 0, x, 1 - x), jnp.where(c == 0, 1 - y, y)
    dx, dy = 1 - x, 1 - y
    pnbr, rnbr, core = device(px, py, z, c), device(rx, ry, z, c), device(x, y, z, 1 - c)
    loads = [pltpu.make_async_copy(g_hbm.at[q, :, :, :, c], acc.at[q], lsem.at[q]) for q in range(3)]
    for cp in loads:
        cp.start()
    column = [device(x, y, (z + k) % 4, c) for k in (1, 2, 3)]
    column += [device(x, y, (z + k) % 4, 1 - c) for k in (0, 1, 2, 3)]
    plane = [device(dx, y, z, c), device(x, dy, z, c), device(dx, dy, z, c)]
    barrier = pltpu.get_barrier_semaphore()
    for peer in column + plane:
        pl.semaphore_signal(barrier, inc=1, device_id=peer, device_id_type=MESH)
    pl.semaphore_wait(barrier, len(column + plane))
    index = [0]
    started = []

    def remote(src_ref, dst_ref, dev):
        k = index[0]
        index[0] += 1
        cp = pltpu.make_async_remote_copy(
            src_ref=src_ref, dst_ref=dst_ref, send_sem=send.at[k], recv_sem=recv.at[k],
            device_id=dev, device_id_type=MESH,
        )
        cp.start()
        started.append(cp)
        return cp

    cut = acc.shape[4] // RCUTS
    cuts = [(3, 0)] + [(q, s) for s in range(RCUTS) for q in range(3)]

    def views(k):
        q, s = cuts[k]
        if q == 3:
            return (
                F32, lambda *i: sacc.at[i], lambda *i: src.at[i], lambda *i: srr.at[i],
                lambda *i: srp.at[i], lambda *i: srz.at[i],
            )
        at = pl.ds(s * cut, cut)

        def of(ref, dims):
            def view(*i):
                rest = (slice(None),) * (dims - len(i))
                return ref.at[(q,) + i + rest + (at,)]

            return view

        return BF, of(acc, 3), of(rc, 3), of(rr, 2), of(rp, 1), of(rz, 1)

    def plus(kind, a, b):
        a[...] = (a[...].astype(F32) + b[...].astype(F32)).astype(kind)

    swaps, r_in, p_in, z_in = {}, {}, {}, {}
    scopy = pltpu.make_async_copy(small_ref.at[:, :, :, c], sacc, lsem.at[3])
    scopy.start()
    for k, (q, s) in enumerate(cuts):
        if q == 3:
            swaps[k] = remote(small_ref.at[:, :, :, 1 - c], src, core)
        else:
            at = pl.ds(s * cut, cut)
            swaps[k] = remote(g_hbm.at[q, :, :, :, 1 - c, at], rc.at[q, :, :, :, at], core)

    def stage_two(k):
        kind, a, b, r, p, zz = views(k)
        if k == 0:
            scopy.wait()
        elif k <= 3:
            loads[cuts[k][0]].wait()
        swaps[k].wait_recv()
        for ly in range(2):
            for lx in range(2):
                for lz in range(4):
                    plus(kind, a(ly, lx, lz), b(ly, lx, lz))
        r_in[k] = [remote(a(dy, dx), r(0), rnbr), remote(a(ry, rx), r(1), rnbr)]

    def stage_three(k):
        kind, a, b, r, p, zz = views(k)
        for cp in r_in[k]:
            cp.wait_recv()
        for lz in range(4):
            plus(kind, a(py, px, lz), r(0, lz))
        p_in[k] = remote(a(py, px), p(), pnbr)
        for lz in range(4):
            plus(kind, a(y, x, lz), r(1, lz))

    def stage_four(k):
        kind, a, b, r, p, zz = views(k)
        p_in[k].wait_recv()
        for lz in range(4):
            plus(kind, a(y, x, lz), p(lz))
        z_in[k] = [
            remote(a(y, x, (z + j) % 4), zz(j - 1), device(x, y, (z + j) % 4, c)) for j in (1, 2, 3)
        ]

    def fold(v):
        t = jnp.zeros((8, 128), F32)
        for r in range(0, v.shape[0], 8):
            for l in range(0, v.shape[1], 128):
                part = v[r : r + 8, l : l + 128]
                t = t + part * part
        return t

    squares = [jnp.zeros((8, 128), F32)]
    tots = []

    def stage_five(k):
        kind, a, b, r, p, zz = views(k)
        for cp in z_in[k]:
            cp.wait_recv()
        v = (a(y, x, z)[...].astype(F32) + zz(0)[...].astype(F32)) + (
            zz(1)[...].astype(F32) + zz(2)[...].astype(F32)
        )
        squares[0] = squares[0] + fold(v)
        q, s = cuts[k]
        if q == 3:
            tot_ref[y, x, z, c] = v
            mine = tot_ref.at[y, x, z, c]
            tots.append([remote(mine, mine, dev) for dev in column])
        else:
            red_ref[q, s * cut : (s + 1) * cut] = v

    n = len(cuts)
    for t in range(n + 3 * RLAG):
        if t < n:
            stage_two(t)
        if 0 <= t - RLAG < n:
            stage_three(t - RLAG)
        if 0 <= t - 2 * RLAG < n:
            stage_four(t - 2 * RLAG)
        if 0 <= t - 3 * RLAG < n:
            stage_five(t - 3 * RLAG)
        if t == n:
            for cp in tots[0]:
                cp.wait_recv()
            lines = tot_ref.at[y, x]
            tots.append([remote(lines, lines, dev) for dev in plane])
    nown[...] = squares[0]
    sent = [remote(nown, nbuf.at[z * 2 + c], dev) for dev in column]
    nbuf[z * 2 + c] = squares[0]
    for cp in sent:
        cp.wait_recv()
    total = nbuf[0]
    for i in range(1, 8):
        total = total + nbuf[i]
    mown[...] = total
    sent = [remote(mown, mbuf.at[y * 2 + x], dev) for dev in plane]
    mbuf[y * 2 + x] = total
    for cp in sent:
        cp.wait_recv()
    total = mbuf[0]
    for i in range(1, 4):
        total = total + mbuf[i]
    total = jnp.sum(jnp.sum(total, axis=0, keepdims=True), axis=1, keepdims=True)
    norm_ref[...] = jnp.broadcast_to(jnp.sqrt(total), norm_ref.shape)
    for cp in tots[1]:
        cp.wait_recv()
    for cp in started:
        cp.wait_send()


RCUTS = 3
RLAG = 2
NRED = 7 * (3 * RCUTS + 1) + 20


def reduce_all(g, small):
    rows, width = g.shape[-2:]
    vmem = pl.BlockSpec(memory_space=pltpu.VMEM)
    anyb = pl.BlockSpec(memory_space=pl.ANY)
    dma = pltpu.SemaphoreType.DMA
    blk, sblk = (rows, width), small.shape[-2:]
    return pl.pallas_call(
        reduce_kernel,
        out_shape=(
            jax.ShapeDtypeStruct((3,) + blk, F32),
            jax.ShapeDtypeStruct(small.shape, F32),
            jax.ShapeDtypeStruct((8, 128), F32),
        ),
        in_specs=[anyb, vmem],
        out_specs=[vmem] * 3,
        scratch_shapes=[
            pltpu.VMEM((3, 2, 2, 4) + blk, BF),
            pltpu.VMEM((3, 2, 2, 4) + blk, BF),
            pltpu.VMEM((3, 2, 4) + blk, BF),
            pltpu.VMEM((3, 4) + blk, BF),
            pltpu.VMEM((3, 3) + blk, BF),
            pltpu.VMEM((2, 2, 4) + sblk, F32),
            pltpu.VMEM((2, 2, 4) + sblk, F32),
            pltpu.VMEM((2, 4) + sblk, F32),
            pltpu.VMEM((4,) + sblk, F32),
            pltpu.VMEM((3,) + sblk, F32),
            pltpu.VMEM((8, 8, 128), F32),
            pltpu.VMEM((4, 8, 128), F32),
            pltpu.VMEM((8, 128), F32),
            pltpu.VMEM((8, 128), F32),
            dma((NRED,)), dma((NRED,)), dma((4,)),
        ],
        compiler_params=pltpu.CompilerParams(
            collective_id=1, has_side_effects=True, vmem_limit_bytes=60 * 2**20
        ),
        name="reduce",
    )(g, small)


STEP = 10
BETA_FIRST = 0.9
BETA_SECOND = 0.95
ADAM_EPS = 1e-08
DECAY_RATE = 0.05
RATE_MATRIX = 0.05
RATE_VECTOR = 0.8
CLIP_BOUND = 1.0
BOTH = ("dp", "fsdp")


def adam_step(weight, first, second, gradient, step_rate, weight_decay):
    first_new = BETA_FIRST * first + (1.0 - BETA_FIRST) * gradient
    second_new = BETA_SECOND * second + (1.0 - BETA_SECOND) * gradient * gradient
    first_hat = first_new * (1.0 / (1.0 - BETA_FIRST**STEP))
    second_hat = second_new * (1.0 / (1.0 - BETA_SECOND**STEP))
    weight_new = weight - step_rate * (
        first_hat / (jnp.sqrt(second_hat) + ADAM_EPS) + weight_decay * weight
    )
    return (weight_new, first_new, second_new)


def adam_kernel(red, tot, norm, iw, i1, i2, ow, o1, o2, sw, s1, s2, *outs):
    clip = CLIP_BOUND / jnp.maximum(norm[0:1, 0:1], CLIP_BOUND)
    rows = ow.shape[0]
    for q in range(2):
        for r in range(0, rows, 8):
            cut = slice(r, r + 8)
            new = adam_step(
                iw[q, cut], i1[q, cut], i2[q, cut], red[q, cut] * clip, RATE_MATRIX, DECAY_RATE
            )
            for ref, val in zip(outs[0:3], new):
                ref[q, cut] = val
    for r in range(0, rows, 8):
        cut = slice(r, r + 8)
        new = adam_step(ow[cut], o1[cut], o2[cut], red[2, cut] * clip, RATE_MATRIX, DECAY_RATE)
        for ref, val in zip(outs[3:6], new):
            ref[cut] = val
    side, cols = sw.shape
    grad = tot[SPATIAL_ROW : SPATIAL_ROW + side, 0:cols] * clip
    last = lax.broadcasted_iota(jnp.int32, (side, 1), 0) == side - 1
    rate = jnp.where(last, RATE_VECTOR, RATE_MATRIX)
    decay = jnp.where(last, 0.0, DECAY_RATE)
    new = adam_step(sw[...], s1[...], s2[...], grad, rate, decay)
    for ref, val in zip(outs[6:9], new):
        ref[...] = val


def adam_all(red, tot, norm, inner, outer, spatial):
    vmem = pl.BlockSpec(memory_space=pltpu.VMEM)
    shape = lambda a: jax.ShapeDtypeStruct(a.shape, F32)
    return pl.pallas_call(
        adam_kernel,
        out_shape=tuple(shape(a) for a in inner + outer + spatial),
        in_specs=[vmem] * 12,
        out_specs=[vmem] * 9,
        compiler_params=pltpu.CompilerParams(vmem_limit_bytes=60 * 2**20),
        name="adam",
    )(red, tot, norm, *inner, *outer, *spatial)


def slow_prepare(inner_t, outer_weight, vectors, tokens, cot, mask, keep, pool_cot, spatial):
    patches, images, width = tokens.shape
    pad = -(-patches // LOT) * LOT
    wt = jnp.concatenate(
        [
            lax.all_gather(inner_t.astype(BF), BOTH, axis=1, tiled=True),
            lax.all_gather(outer_weight.astype(BF), BOTH, axis=0, tiled=True)[None],
        ],
        axis=0,
    )
    vec = lax.all_gather(vectors.astype(BF), BOTH, axis=0, tiled=True).astype(F32)
    vec = vec.reshape(-1, width)
    counts = jnp.sum(mask, axis=1)
    info = jnp.zeros((images, 128), jnp.int32).at[:, 0].set(counts).at[:, 1].set(keep)
    poolc = pool_cot.astype(F32) / counts.astype(F32)[:, None]
    unit, _ = norm(tokens.astype(F32))
    edge = ((0, 0), (0, pad - patches), (0, 0))
    nm = (unit * vec[0] + vec[1]).astype(BF)
    live = mask.astype(F32).T[:, :, None]
    scale = keep.astype(F32) * (1.0 / (1.0 - DROP_RATE))
    bg = (scale[:, None] * (cot.astype(F32) + live * poolc)).astype(BF)
    bsum = jnp.sum(bg, axis=0, dtype=F32)
    nm = jnp.pad(nm.transpose(1, 0, 2), edge)
    bg = jnp.pad((bg * live.astype(BF)).transpose(1, 0, 2), edge)
    low = spatial[:patches].astype(BF)
    square = ((0, 256 - patches), (0, 256 - patches))
    sbias = jnp.pad(spatial[patches][:, None], ((0, 256 - patches), (0, 0)))
    return wt, vec, nm, bg, info, poolc, bsum, jnp.pad(low, square), jnp.pad(low.T, square), sbias


def slow_reduce(grads, small):
    red = lax.psum_scatter(grads.astype(F32), BOTH, scatter_dimension=1, tiled=True)
    tot = lax.psum(small, BOTH)
    squares = lax.psum(jnp.sum(red * red), BOTH) + jnp.sum(tot * tot)
    return red, tot, jnp.broadcast_to(jnp.sqrt(squares), (8, 128))


def per_device(
    fast,
    tokens,
    valid_mask,
    keep_mask,
    out_cotangent,
    pool_cotangent,
    inner_weight,
    outer_weight,
    vectors,
    spatial,
    inner_first,
    inner_second,
    outer_first,
    outer_second,
    vector_first,
    vector_second,
    spatial_first,
    spatial_second,
):
    own = vectors.shape[0]
    rows, width = outer_weight.shape
    inner_t = tuple(a.transpose(0, 2, 1) for a in (inner_weight, inner_first, inner_second))
    tokens = tokens.transpose(1, 0, 2)
    cot = out_cotangent.transpose(1, 0, 2)
    if fast:
        wt, *ready = gather_all(
            own,
            inner_t[0],
            outer_weight,
            jnp.pad(vectors, (0, 1024 - own)).reshape(8, 128),
            tokens,
            cot,
            valid_mask,
            keep_mask,
            pool_cotangent,
            spatial,
        )
        wt = wt.reshape(3, 32 * rows, width)
    else:
        wt, *ready = slow_prepare(
            inner_t[0], outer_weight, vectors, tokens, cot, valid_mask, keep_mask, pool_cotangent, spatial
        )
    vec, nm, bg, info, poolc, bsum, sp, spt, sbias = ready
    output, input_grad, pooled, grads, small = run_block(
        tokens, cot, nm, bg, info, poolc, bsum, wt, vec, sp, spt, sbias
    )
    output = output.transpose(1, 0, 2)
    input_grad = input_grad.transpose(1, 0, 2)
    if fast:
        red, tot, norm = reduce_all(
            grads.reshape(3, 2, 2, 4, 2, rows, width), small.reshape(2, 2, 4, 2, 8, 256)
        )
        tot = tot.reshape(256, 256)
    else:
        red, tot, norm = slow_reduce(grads, small)
    new = adam_all(
        red,
        tot,
        norm,
        inner_t,
        (outer_weight, outer_first, outer_second),
        (spatial, spatial_first, spatial_second),
    )
    grad_norm = norm[0, 0]
    clip_factor = CLIP_BOUND / jnp.maximum(grad_norm, CLIP_BOUND)
    me = lax.axis_index("dp") * lax.axis_size("fsdp") + lax.axis_index("fsdp")
    total_vec = own * lax.axis_size("dp") * lax.axis_size("fsdp")
    flat = tot[: total_vec // 256].reshape(-1)
    vector_red = lax.dynamic_slice(flat, (me * own,), (own,))
    vector_out = adam_step(
        vectors, vector_first, vector_second, vector_red * clip_factor, RATE_VECTOR, 0.0
    )
    return (
        (output, input_grad, pooled, grad_norm)
        + tuple(a.transpose(0, 2, 1) for a in new[0:3])
        + tuple(new[3:6])
        + vector_out
        + tuple(new[6:9])
    )


def solution(mesh):
    fast = mesh.shape["dp"] == 4 and mesh.shape["fsdp"] == 8
    rows3 = P(BOTH, None, None)
    rows2 = P(BOTH, None)
    rows1 = P(BOTH)
    cols3 = P(None, None, BOTH)
    in_specs = (
        (rows3, rows2, rows1, rows3, rows2, cols3, rows2, rows1, P())
        + (cols3,) * 2
        + (rows2,) * 2
        + (rows1,) * 2
        + (P(),) * 2
    )
    out_specs = (
        (rows3, rows3, rows2, P()) + (cols3,) * 3 + (rows2,) * 3 + (rows1,) * 3 + (P(),) * 3
    )
    return jax.shard_map(
        functools.partial(per_device, fast),
        mesh=mesh,
        in_specs=in_specs,
        out_specs=out_specs,
        check_vma=False,
    )
```

```python
import functools

import jax
import jax.numpy as jnp
from jax import lax
from jax.experimental import pallas as pl
from jax.experimental.pallas import tpu as pltpu
from jax.sharding import PartitionSpec as P

NORM_EPS = 1e-05
DROP_RATE = 0.1
BF = jnp.bfloat16
F32 = jnp.float32
MESH = pl.DeviceIdType.MESH
GELU_K = 0.7978845608
GELU_C = 0.044715
NN = (((1,), (0,)), ((), ()))
NT = (((1,), (1,)), ((), ()))
TN = (((0,), (0,)), ((), ()))
LOT = 16
CUTS = 3
SLAB = 2


def dot(a, b, dims):
    return lax.dot_general(a, b, dims, preferred_element_type=F32)


def norm(x):
    c = x - jnp.mean(x, axis=-1, keepdims=True)
    inv = lax.rsqrt(jnp.mean(c * c, axis=-1, keepdims=True) + NORM_EPS)
    return c * inv, inv


def swap_matrix(images):
    side = LOT * images
    r = lax.broadcasted_iota(jnp.int32, (side, side), 0)
    s = lax.broadcasted_iota(jnp.int32, (side, side), 1)
    return jnp.where(s == (r % LOT) * images + r // LOT, 1.0, 0.0).astype(BF)


def unswap_matrix(images):
    side = LOT * images
    r = lax.broadcasted_iota(jnp.int32, (side, side), 0)
    s = lax.broadcasted_iota(jnp.int32, (side, side), 1)
    return jnp.where(s == (r % images) * LOT + r // images, 1.0, 0.0).astype(BF)


def place():
    d = lax.axis_index("dp")
    f = lax.axis_index("fsdp")
    return d % 2, d // 2, f // 2, f % 2


def device(x, y, z, c):
    return (y * 2 + x, z * 2 + c)


def greet_partners():
    x, y, z, c = place()
    barrier = pltpu.get_barrier_semaphore()
    peers = [device(1 - x, y, z, c), device(x, 1 - y, z, c), device(x, y, z, 1 - c)]
    peers += [device(x, y, (z + k) % 4, c) for k in (1, 2, 3)]
    for peer in peers:
        pl.semaphore_signal(barrier, inc=1, device_id=peer, device_id_type=MESH)
    pl.semaphore_wait(barrier, len(peers))


def gather_kernel(
    own_len,
    inner_ref, outer_ref, vec_ref, tokens_hbm, cot_hbm, mask_ref, keep_ref, pool_ref, spatial_ref,
    all_ref, vecs_ref, nm_ref, bg_ref, info_ref, poolc_ref, bsum_ref, sp_ref, spt_ref, sbias_ref,
    own, vown, vgot, wide, xblk, cblk, nrow, brow, nm_v, bg_v, send, recv, lsem, isem, osem,
):
    x, y, z, c = place()
    patches, images, width = tokens_hbm.shape
    own[0] = inner_ref[0].astype(BF)
    own[1] = inner_ref[1].astype(BF)
    own[2] = outer_ref[...].astype(BF)
    vown[...] = vec_ref[...].astype(BF).astype(F32)
    loads = [
        pltpu.make_async_copy(tokens_hbm, xblk, isem.at[0]),
        pltpu.make_async_copy(cot_hbm, cblk, isem.at[1]),
    ]
    for cp in loads:
        cp.start()
    greet_partners()
    local = pltpu.make_async_copy(own, all_ref.at[:, y, x, z, c], lsem)
    local.start()
    vgot[y, x, z, c] = vown[...]

    px, py = jnp.where(c == 0, 1 - x, x), jnp.where(c == 0, y, 1 - y)
    rx, ry = jnp.where(c == 0, x, 1 - x), jnp.where(c == 0, 1 - y, y)
    dx, dy = 1 - x, 1 - y
    index = [0]
    pnbr, rnbr, core = device(px, py, z, c), device(rx, ry, z, c), device(x, y, z, 1 - c)
    cut = outer_ref.shape[0] // CUTS
    started = []

    def remote(src, dst, dev):
        k = index[0]
        index[0] += 1
        cp = pltpu.make_async_remote_copy(
            src_ref=src, dst_ref=dst, send_sem=send.at[k], recv_sem=recv.at[k],
            device_id=dev, device_id_type=MESH,
        )
        cp.start()
        started.append(cp)
        return cp

    def span(s):
        return pl.ds(s * cut, cut)

    def block(q, s, by, bx):
        if q == 3:
            return vgot.at[by, bx, z, c]
        return all_ref.at[q, by, bx, z, c, span(s)]

    def z_sends(src, q, s, by, bx):
        return [remote(src, block(q, s, by, bx), device(x, y, (z + k) % 4, c)) for k in (1, 2, 3)]

    def send_line(q, s, ly, lx, dev):
        ref = vgot.at[ly, lx, :, c] if q == 3 else all_ref.at[q, ly, lx, :, c, span(s)]
        return remote(ref, ref, dev)

    cuts = [(3, 0)] + [(q, s) for s in range(CUTS) for q in range(3)]
    zs = [None] * len(cuts)

    def start_z(k):
        if k < len(cuts):
            q, s = cuts[k]
            src = vown if q == 3 else own.at[q, span(s)]
            zs[k] = z_sends(src, q, s, y, x)

    for k in range(WINDOW):
        start_z(k)
    local.wait()

    counts = jnp.sum(mask_ref[...], axis=1, keepdims=True)
    keeps = jnp.zeros((images, 1), jnp.int32)
    image = lax.broadcasted_iota(jnp.int32, (images, 1), 0)
    for b in range(images):
        keeps = jnp.where(image == b, keep_ref[b], keeps)
    scale = keeps.astype(F32) * (1.0 / (1.0 - DROP_RATE))
    lane = lax.broadcasted_iota(jnp.int32, info_ref.shape, 1)
    info_ref[...] = jnp.where(lane == 0, counts, keeps)
    poolc = pool_ref[...].astype(F32) / counts.astype(F32)
    poolc_ref[...] = poolc
    side = spatial_ref.shape[1]
    wide[...] = jnp.zeros_like(wide)
    wide[0 : side + 1, 0:side] = spatial_ref[...]
    mat = wide[...]
    mat_t = mat.T
    span_a = lax.broadcasted_iota(jnp.int32, mat.shape, 0)
    span_b = lax.broadcasted_iota(jnp.int32, mat.shape, 1)
    sp_ref[...] = jnp.where(span_a < side, mat, 0.0).astype(BF)
    spt_ref[...] = jnp.where(span_b < side, mat_t, 0.0).astype(BF)
    sbias_ref[...] = mat_t[:, side : side + 1]
    bsum_ref[...] = jnp.zeros_like(bsum_ref)
    vecs_ref[...] = jnp.zeros_like(vecs_ref)

    def stack_vectors():
        per = width // 128
        for d in range(32):
            start = own_len * d
            shift = start % 128
            blk = vgot[d // 16, d // 8 % 2, d // 2 % 4, d % 2]
            row = jnp.concatenate(
                [jnp.broadcast_to(blk[i : i + 1, :], (8, 128)) for i in range(3)], axis=1
            )
            row = pltpu.roll(row, shift, 1) if shift else row
            for i in range(3):
                r = start // 128 + i
                if r * 128 < start + own_len:
                    at = (slice(r // per, r // per + 1), slice(r % per * 128, r % per * 128 + 128))
                    vecs_ref[at] += row[0:1, i * 128 : i * 128 + 128]

    swap = swap_matrix(images)

    def token_block(k, many):
        gain, shift = vecs_ref[0:1, :], vecs_ref[1:2, :]
        total = jnp.zeros((images, width), F32)
        for p in range(0, many, SLAB):
            patch = lax.broadcasted_iota(jnp.int32, (SLAB, images, 1), 0) + (k * LOT + p)
            at = pl.ds(k * LOT + p, SLAB)
            cut = slice(p * images, (p + SLAB) * images)
            unit, _ = norm(xblk[at].astype(F32))
            nrow[cut, :] = (unit * gain + shift).astype(BF).reshape(SLAB * images, width)
            live = jnp.where(counts > patch, 1.0, 0.0)
            og = cblk[at].astype(F32) + live * poolc
            bg = (scale * og).astype(BF).astype(F32)
            total = total + jnp.sum(bg, axis=0)
            brow[cut, :] = (live * bg).astype(BF).reshape(SLAB * images, width)
        bsum_ref[...] += total
        part = swap[:, 0 : many * images]
        for src, dst in ((nrow, nm_v), (brow, bg_v)):
            moved = dot(part, src[0 : many * images, :], NN).astype(BF)
            at = pl.ds(pl.multiple_of(k * LOT, LOT), LOT)
            dst[:, at, :] = moved.reshape(images, LOT, width)

    full = patches // LOT
    todo = list(range(full + (1 if patches % LOT else 0)))

    stores = []
    pad = nm_v.shape[1]
    marks = [pad // (2 * LOT) * LOT, pad]

    def some_tokens(many):
        for _ in range(many):
            if not todo:
                return
            k = todo.pop(0)
            token_block(k, LOT if k < full else patches % LOT)
            end = (k + 1) * LOT
            if end in marks:
                at = pl.ds(0, end) if end == marks[0] else pl.ds(marks[0], end - marks[0])
                for src, dst in ((nm_v, nm_ref), (bg_v, bg_ref)):
                    cp = pltpu.make_async_copy(src.at[:, at], dst.at[:, at], osem.at[len(stores)])
                    cp.start()
                    stores.append(cp)

    lines_p, lines_r, lines_r2, cores = {}, {}, {}, {}

    def swap_core(k, cp):
        cores.setdefault(k, []).append(cp)


    def stage_two(k):
        q, s = cuts[k]
        for cp in zs[k]:
            cp.wait_recv()
        start_z(k + WINDOW)
        lines_p[k] = send_line(q, s, y, x, pnbr)
        lines_r[k] = send_line(q, s, y, x, rnbr)
        swap_core(k, send_line(q, s, y, x, core))

    def stage_three(k):
        q, s = cuts[k]
        lines_p[k].wait_recv()
        lines_r2[k] = send_line(q, s, py, px, rnbr)
        swap_core(k, send_line(q, s, py, px, core))

    def stage_four(k):
        q, s = cuts[k]
        lines_r[k].wait_recv()
        swap_core(k, send_line(q, s, ry, rx, core))

    def stage_five(k):
        q, s = cuts[k]
        lines_r2[k].wait_recv()
        swap_core(k, send_line(q, s, dy, dx, core))

    n = len(cuts)
    for t in range(n + LAG_FIVE):
        if t < n:
            stage_two(t)
        if 0 <= t - LAG_THREE < n:
            stage_three(t - LAG_THREE)
            stage_four(t - LAG_THREE)
        if 0 <= t - LAG_FIVE < n:
            stage_five(t - LAG_FIVE)
        if t == LAG_FIVE + 1:
            for cp in cores[0]:
                cp.wait_recv()
            stack_vectors()
            for cp in loads:
                cp.wait()
        if t > LAG_FIVE:
            some_tokens(-(-13 // (n - 1)))
    some_tokens(len(todo))
    for k in range(1, n):
        for cp in cores[k]:
            cp.wait_recv()
    for cp in started:
        cp.wait_send()
    for cp in stores:
        cp.wait()


NSEND = 10 * (3 * CUTS + 1)
LAG_THREE = 3
LAG_FIVE = 6
WINDOW = 4


def gather_all(own_len, inner, outer, vec, tokens, cot, mask, keep, pool, spatial):
    rows, width = outer.shape
    patches, images, _ = tokens.shape
    pad = -(-patches // LOT) * LOT
    vmem = pl.BlockSpec(memory_space=pltpu.VMEM)
    smem = pl.BlockSpec(memory_space=pltpu.SMEM)
    anyb = pl.BlockSpec(memory_space=pl.ANY)
    dma = pltpu.SemaphoreType.DMA
    shape = jax.ShapeDtypeStruct
    return pl.pallas_call(
        functools.partial(gather_kernel, own_len),
        out_shape=(
            shape((3, 2, 2, 4, 2, rows, width), BF),
            shape((16, width), F32),
            shape((images, pad, width), BF),
            shape((images, pad, width), BF),
            shape((images, 128), jnp.int32),
            shape((images, width), F32),
            shape((images, width), F32),
            shape((256, 256), BF),
            shape((256, 256), BF),
            shape((256, 1), F32),
        ),
        in_specs=[vmem] * 3 + [anyb] * 2 + [vmem, smem, vmem, vmem],
        out_specs=[anyb, vmem, anyb, anyb] + [vmem] * 6,
        scratch_shapes=[
            pltpu.VMEM((3, rows, width), BF),
            pltpu.VMEM((8, 128), F32),
            pltpu.VMEM((2, 2, 4, 2, 8, 128), F32),
            pltpu.VMEM((256, 256), F32),
            pltpu.VMEM((patches, images, width), BF),
            pltpu.VMEM((patches, images, width), BF),
            pltpu.VMEM((LOT * images, width), BF),
            pltpu.VMEM((LOT * images, width), BF),
            pltpu.VMEM((images, pad, width), BF),
            pltpu.VMEM((images, pad, width), BF),
            dma((NSEND,)), dma((NSEND,)), dma, dma((2,)), dma((4,)),
        ],
        compiler_params=pltpu.CompilerParams(
            collective_id=0, has_side_effects=True, vmem_limit_bytes=60 * 2**20
        ),
        name="gather",
    )(inner, outer, vec, tokens, cot, mask, keep, pool, spatial)


def gelu_pair(v):
    u = v * v
    s = 0.5 * jnp.tanh(v * (GELU_K + (GELU_K * GELU_C) * u)) + 0.5
    h = v * s
    d = s + (h - h * s) * (2.0 * GELU_K + (6.0 * GELU_K * GELU_C) * u)
    return h, d


def fold8(x):
    total = x[0:8]
    for r in range(8, x.shape[0], 8):
        total = total + x[r : r + 8]
    return total


def lanes(x):
    total = x[:, 0:128]
    for c in range(128, x.shape[1], 128):
        total = total + x[:, c : c + 128]
    return total


def loop(lo, hi, fn):
    def body(i, c):
        fn(i)
        return c

    lax.fori_loop(lo, hi, body, 0)


def block_kernel(
    cfg,
    info_s,
    tokens_hbm, cot_hbm, nm_hbm, bg_hbm,
    info_ref, poolc_ref, bsum_ref, wt_hbm, vec_ref, sp_ref, spt_ref, sbias_ref,
    out_hbm, ig_hbm, pooled_ref, grads_hbm, small_ref,
    acc, sg_ref, sbg_ref, off_s, gend_s, grows_s,
    wt_ref, wtt, nm_b, bg_b, h0_b, e0_b, mg_b, xm_b, u2_b, d1_b, stat_b, h1_s, t_s,
    xblk, cblk, br_s, ng_s, out_st, ig_st, vacc,
    wt_sem, pack_sem, in_sem, out_sem, grad_sem,
):
    images, patches, width, gate, rows_cap, tm, classes = cfg
    cw = 256
    nj = gate // cw
    chunks = -(-patches // LOT)
    zero_row = nm_b.shape[0] - LOT
    g2_base, s2_base = 3 * width, 3 * width + gate
    b0_base, b1_base = 3 * width + 2 * gate, 3 * width + 3 * gate

    def vrow(base, j):
        start = base + j * cw
        return vec_ref[start // width : start // width + 1, start % width : start % width + cw]

    def count(b):
        return info_s[b, 0]

    def keep(b):
        return info_s[b, 1]

    def need_of(b):
        return keep(b) * ((count(b) + LOT - 1) // LOT)

    wt_loads = [pltpu.make_async_copy(wt_hbm.at[q], wt_ref.at[q], wt_sem.at[q]) for q in range(3)]
    for q in (1, 0, 2):
        wt_loads[q].start()

    def plan(b, carry):
        group, row, first = carry
        need = need_of(b) * LOT
        over = row + need - first > rows_cap
        group = group + over.astype(jnp.int32)
        first = jnp.where(over, row, first)
        off_s[b] = row
        row = row + need
        gend_s[group] = b + 1
        grows_s[group] = row - first
        return group, row, first

    zero = jnp.int32(0)
    last_group, all_rows, _ = lax.fori_loop(0, images, plan, (zero, zero, zero))

    def pack(b, act):
        lots = need_of(b)
        o = off_s[b]
        done = jnp.int32(0)
        for size in (8, 4, 2, 1):
            @pl.when((lots & size) != 0)
            def _(size=size, done=done):
                src = pl.ds(pl.multiple_of(done * LOT, LOT), size * LOT)
                dst = pl.ds(pl.multiple_of(o + done * LOT, LOT), size * LOT)
                for i, (far, near) in enumerate(((nm_hbm, nm_b), (bg_hbm, bg_b))):
                    act(pltpu.make_async_copy(far.at[b, src], near.at[dst], pack_sem.at[i, b]))

            done = done + (lots & size)

    loop(0, images, lambda b: pack(b, lambda cp: cp.start()))

    full = patches // LOT
    rest = patches % LOT

    def load_lot(k, many, slot):
        at = pl.ds(k * LOT, many)
        return (
            pltpu.make_async_copy(tokens_hbm.at[at], xblk.at[slot, pl.ds(0, many)], in_sem.at[0, slot]),
            pltpu.make_async_copy(cot_hbm.at[at], cblk.at[slot, pl.ds(0, many)], in_sem.at[1, slot]),
        )

    for k in (0, 1):
        for cp in load_lot(k, LOT, k):
            cp.start()

    def zero_rows(ref, n_chunks, start):
        z = jnp.zeros((LOT, ref.shape[1]), ref.dtype)

        def body(i):
            ref[pl.ds(pl.multiple_of(start + i * LOT, LOT), LOT), :] = z

        loop(0, n_chunks, body)

    for ref in (mg_b, xm_b, u2_b):
        zero_rows(ref, ref.shape[0] // LOT, 0)
    for ref in (nm_b, bg_b):
        zero_rows(ref, tm // LOT, all_rows)
    z = jnp.zeros((LOT, width), BF)
    nm_b[zero_row : zero_row + LOT, :] = z
    bg_b[zero_row : zero_row + LOT, :] = z
    vacc[...] = jnp.zeros_like(vacc)
    acc[...] = jnp.zeros_like(acc)
    sg_ref[...] = jnp.zeros_like(sg_ref)
    sbg_ref[...] = jnp.zeros_like(sbg_ref)
    for q in (1, 0, 2):
        wt_loads[q].wait()
        for j in range(nj):
            wtt[q, :, j * cw : (j + 1) * cw] = wt_ref[q, j * cw : (j + 1) * cw, :].T
    loop(0, images, lambda b: pack(b, lambda cp: cp.wait()))

    def phase_a(t, gs):
        r0 = pl.multiple_of(t * tm, tm)
        rows = pl.ds(r0, tm)
        here = pl.ds(pl.multiple_of(gs + r0, LOT), tm)
        nb = nm_b[here, :]
        bgt = bg_b[here, :]
        s1 = jnp.zeros((tm, 128), F32)
        for j in range(nj):
            cols = slice(j * cw, (j + 1) * cw)
            a1 = dot(nb, wtt[1, :, cols], NN) + vrow(b1_base, j)
            h1, d1 = gelu_pair(a1)
            h1_s[:, cols] = h1
            d1_b[rows, cols] = d1.astype(BF)
            s1 = s1 + lanes(h1)
        mean = jnp.sum(s1, axis=1, keepdims=True) * (1.0 / gate)
        q1 = jnp.zeros((tm, 128), F32)
        for j in range(nj):
            cols = slice(j * cw, (j + 1) * cw)
            a0 = dot(nb, wtt[0, :, cols], NN) + vrow(b0_base, j)
            h0, d0 = gelu_pair(a0)
            gg = dot(bgt, wtt[2, :, cols], NN)
            mg = gg * h0
            h0_b[rows, cols] = h0.astype(BF)
            mg_b[rows, cols] = mg.astype(BF)
            e0_b[rows, cols] = (gg * d0).astype(BF)
            c = h1_s[:, cols] - mean
            q1 = q1 + lanes(c * c)
        inv = lax.rsqrt(jnp.sum(q1, axis=1, keepdims=True) * (1.0 / gate) + NORM_EPS)
        stat_b[rows, :] = jnp.broadcast_to(inv, (tm, 128))
        for j in range(nj):
            cols = slice(j * cw, (j + 1) * cw)
            u2 = (h1_s[:, cols] - mean) * inv
            u2_b[rows, cols] = u2.astype(BF)
            xm_b[rows, cols] = (u2 * vrow(g2_base, j) + vrow(s2_base, j)).astype(BF)

    def phase_b(b, m, gs):
        n = count(b)
        o = pl.multiple_of(off_s[b] - gs, LOT)
        rows = pl.ds(o, m)
        rid = lax.broadcasted_iota(jnp.int32, (m, 1), 0)
        cid = lax.broadcasted_iota(jnp.int32, (m, m), 1)
        rid2 = lax.broadcasted_iota(jnp.int32, (m, m), 0)
        both = (cid < n) & (rid2 < n)
        sp = jnp.where(both, sp_ref[0:m, 0:m], 0.0).astype(BF)
        spt = jnp.where(both, spt_ref[0:m, 0:m], 0.0).astype(BF)
        valid = rid < n
        fill = jnp.where(rid < need_of(b) * LOT, 0.0, 1.0)
        sbias = jnp.where(valid, sbias_ref[0:m, :], fill)
        inv = jnp.where(valid, stat_b[rows, 0:1], 0.0)
        ones = jnp.ones((LOT, gate), BF)
        tsum = jnp.zeros((m, 128), F32)
        tdot = jnp.zeros((m, 128), F32)
        xm_ones = jnp.concatenate([xm_b[rows, :], ones], axis=0)
        sg = dot(mg_b[rows, :], xm_ones, NT)
        sg_ref[0:m, 0:m] += jnp.where(both, sg[:, 0:m], 0.0)
        sbg_ref[0:m, 0:1] += jnp.where(valid, sg[:, m : m + 1], 0.0)
        for j in range(nj):
            cols = slice(j * cw, (j + 1) * cw)
            xm = xm_b[rows, cols]
            mg = mg_b[rows, cols]
            so = (dot(sp, xm, NN) + sbias).astype(BF)
            mix = dot(spt, mg, NN)
            h0_b[rows, cols] = h0_b[rows, cols] * so
            e0_b[rows, cols] = e0_b[rows, cols] * so
            u2 = u2_b[rows, cols].astype(F32)
            mu = mix * u2
            gain = vrow(g2_base, j)
            t = mix * gain
            t_s[0:m, cols] = t
            tsum = tsum + lanes(t)
            tdot = tdot + lanes(mu * gain)
            vi, lo = j * cw // width, j * cw % width
            vacc[g2_base // width + vi, :, lo : lo + cw] += fold8(mu)
            vacc[s2_base // width + vi, :, lo : lo + cw] += fold8(mix)
        m1 = jnp.sum(tsum, axis=1, keepdims=True) * (1.0 / gate)
        m2 = jnp.sum(tdot, axis=1, keepdims=True) * (1.0 / gate)
        base, slope = fill - inv * m1, inv * m2
        for j in range(nj):
            cols = slice(j * cw, (j + 1) * cw)
            u2 = u2_b[rows, cols].astype(F32)
            sec = (inv * t_s[0:m, cols] + (base - u2 * slope)).astype(BF)
            d1_b[rows, cols] = d1_b[rows, cols] * sec

    def phase_c(t, gs, group_rows):
        r0 = pl.multiple_of(t * tm, tm)
        rows = pl.ds(r0, tm)
        here = pl.ds(pl.multiple_of(gs + r0, LOT), tm)
        nb = nm_b[here, :]
        bgt = bg_b[here, :]
        mine = lax.broadcasted_iota(jnp.int32, (tm, 1), 0) < group_rows - r0
        br = dot(h0_b[rows, :], wt_ref[2], NN)
        bg_b[here, :] = jnp.where(mine, br, bgt.astype(F32)).astype(BF)
        ng = dot(e0_b[rows, :], wt_ref[0], NN) + dot(d1_b[rows, :], wt_ref[1], NN)
        nm_b[here, :] = jnp.where(mine, ng, nb.astype(F32)).astype(BF)
        for j in range(nj):
            cols = slice(j * cw, (j + 1) * cw)
            vi, lo = j * cw // width, j * cw % width
            e0, d1 = e0_b[rows, cols], d1_b[rows, cols]
            acc[0, cols, :] += dot(e0, nb, TN)
            acc[1, cols, :] += dot(d1, nb, TN)
            acc[2, cols, :] += dot(h0_b[rows, cols], bgt, TN)
            vacc[b0_base // width + vi, :, lo : lo + cw] += fold8(e0.astype(F32))
            vacc[b1_base // width + vi, :, lo : lo + cw] += fold8(d1.astype(F32))

    def group(g, carry):
        b_start, gs = carry
        b_end = gend_s[g]
        rows = grows_s[g]
        tiles = (rows + tm - 1) // tm
        loop(0, tiles, lambda t: phase_a(t, gs))

        def do_b(b):
            low = 0
            for m in classes:
                @pl.when((keep(b) == 1) & (count(b) > low) & (count(b) <= m))
                def _(m=m):
                    phase_b(b, m, gs)

                low = m

        loop(b_start, b_end, do_b)
        tail = (tiles * tm - rows) // LOT
        for ref in (h0_b, e0_b, d1_b):
            zero_rows(ref, tail, rows)
        loop(0, tiles, lambda t: phase_c(t, gs, rows))
        return b_end, gs + rows

    lax.fori_loop(0, last_group + 1, group, (zero, zero))

    half = gate // 2
    grad_out = []
    per = gate // width
    for i in range(6):
        q, lo = i // 2, (i % 2) * half
        buf = (h1_s, t_s)[0]
        del buf
        stage = (mg_b, xm_b)[i % 2]
        if i >= 2:
            for cp in grad_out[i - 2]:
                cp.wait()
        cps = []
        for v in range(per):
            third = half // per
            cut = slice(v * width, (v + 1) * width)
            stage[0:third, cut] = acc[q, lo + v * third : lo + (v + 1) * third, :].astype(BF)
            cps.append(
                pltpu.make_async_copy(
                    stage.at[pl.ds(0, third), pl.ds(v * width, width)],
                    grads_hbm.at[q, pl.ds(lo + v * third, third)],
                    grad_sem.at[i, v],
                )
            )
        for cp in cps:
            cp.start()
        grad_out.append(cps)

    counts = info_ref[:, 0:1]
    scale = info_ref[:, 1:2].astype(F32) * (1.0 / (1.0 - DROP_RATE))
    poolc = poolc_ref[...]
    gain_one, bias_out = vec_ref[0:1, :], vec_ref[2:3, :]
    back = unswap_matrix(images)

    def store_lot(k, many, slot):
        at = pl.ds(k * LOT, many)
        return (
            pltpu.make_async_copy(out_st.at[slot, pl.ds(0, many)], out_hbm.at[at], out_sem.at[0, slot]),
            pltpu.make_async_copy(ig_st.at[slot, pl.ds(0, many)], ig_hbm.at[at], out_sem.at[1, slot]),
        )

    pooled_ref[...] = jnp.zeros_like(pooled_ref)

    def lot(k, many, slot):
        for cp in load_lot(k, many, slot):
            cp.wait()
        parts = [[], []]
        for b in range(images):
            there = k < need_of(b)
            row = pl.multiple_of(jnp.where(there, off_s[b] + k * LOT, zero_row), LOT)
            parts[0].append(bg_b[pl.ds(row, LOT), :])
            parts[1].append(nm_b[pl.ds(row, LOT), :])
        mat = back[0 : many * images, :]
        br_s[0 : many * images, :] = dot(mat, jnp.concatenate(parts[0], axis=0), NN)
        ng_s[0 : many * images, :] = dot(mat, jnp.concatenate(parts[1], axis=0), NN)
        psum = jnp.zeros((images, width), F32)
        g1 = jnp.zeros((images, width), F32)
        s1 = jnp.zeros((images, width), F32)
        for p in range(0, many, SLAB):
            patch = lax.broadcasted_iota(jnp.int32, (SLAB, images, 1), 0) + (k * LOT + p)
            x = xblk[slot, p : p + SLAB].astype(F32)
            unit, inv = norm(x)
            live = jnp.where(counts > patch, 1.0, 0.0)
            og = cblk[slot, p : p + SLAB].astype(F32) + live * poolc
            cut = slice(p * images, (p + SLAB) * images)
            br = br_s[cut, :].reshape(SLAB, images, width)
            out = x + scale * (br + bias_out)
            out_st[slot, p : p + SLAB] = out
            psum = psum + jnp.sum(live * out, axis=0)
            ng = ng_s[cut, :].reshape(SLAB, images, width)
            t = ng * gain_one
            m1 = jnp.mean(t, axis=-1, keepdims=True)
            m2 = jnp.mean(t * unit, axis=-1, keepdims=True)
            ig_st[slot, p : p + SLAB] = og + inv * (t - m1 - unit * m2)
            g1 = g1 + jnp.sum(ng * unit, axis=0)
            s1 = s1 + jnp.sum(ng, axis=0)
        pooled_ref[...] += psum
        vacc[0] += fold8(g1)
        vacc[1] += fold8(s1)
        for cp in store_lot(k, many, slot):
            cp.start()

    def lots(k):
        slot = lax.rem(k, 2)

        @pl.when(k >= 2)
        def _():
            for cp in store_lot(k - 2, LOT, slot):
                cp.wait()

        lot(k, LOT, slot)

        @pl.when(k + 2 < full)
        def _():
            for cp in load_lot(k + 2, LOT, slot):
                cp.start()

        if rest:
            @pl.when(k + 2 == full)
            def _():
                for cp in load_lot(full, rest, full % 2):
                    cp.start()

    loop(0, full, lots)
    if rest:
        for cp in store_lot(full - 2, LOT, full % 2):
            cp.wait()
        lot(full, rest, full % 2)
    pooled_ref[...] = pooled_ref[...] / counts.astype(F32)

    vacc[2] += fold8(bsum_ref[...])
    small_ref[...] = jnp.zeros_like(small_ref)
    sums = jnp.sum(vacc[...], axis=1)
    for v in range(sums.shape[0]):
        for h in range(width // 256):
            row = v * (width // 256) + h
            small_ref[row : row + 1, :] = sums[v : v + 1, h * 256 : (h + 1) * 256]
    pad = sg_ref.shape[0]
    small_ref[SPATIAL_ROW : SPATIAL_ROW + pad, 0:pad] = sg_ref[...]
    bias = sbg_ref[:, 0:1]
    eye = lax.broadcasted_iota(jnp.int32, (pad, pad), 0) == lax.broadcasted_iota(jnp.int32, (pad, pad), 1)
    bias_row = jnp.sum(jnp.where(eye, bias, 0.0), axis=0, keepdims=True)
    small_ref[SPATIAL_ROW + patches : SPATIAL_ROW + patches + 1, 0:pad] = bias_row
    for cps in grad_out[4:]:
        for cp in cps:
            cp.wait()
    if rest:
        for cp in store_lot(full - 1, LOT, (full - 1) % 2) + store_lot(full, rest, full % 2):
            cp.wait()
    else:
        for k in (full - 2, full - 1):
            for cp in store_lot(k, LOT, k % 2):
                cp.wait()


SPATIAL_ROW = 32


def run_block(
    tokens, cot, nm, bg, info, poolc, bsum, wt, vec, sp, spt, sbias,
    *, rows_cap=1024, tm=256, classes=(96, 144, 208),
):
    patches, images, width = tokens.shape
    gate = wt.shape[1]
    pad = -(-patches // LOT) * LOT
    classes = tuple(m for m in classes if m < pad) + (pad,)
    cap = rows_cap + pad + 48
    cap = -(-cap // tm) * tm
    long = images * pad + tm + LOT
    cfg = (images, patches, width, gate, rows_cap, tm, classes)
    smem = pl.BlockSpec(memory_space=pltpu.SMEM)
    vmem = pl.BlockSpec(memory_space=pltpu.VMEM)
    anyb = pl.BlockSpec(memory_space=pl.ANY)
    dma = pltpu.SemaphoreType.DMA
    shape = jax.ShapeDtypeStruct
    nvec = 3 + 4 * gate // width
    return pl.pallas_call(
        functools.partial(block_kernel, cfg),
        out_shape=(
            shape((patches, images, width), F32),
            shape((patches, images, width), F32),
            shape((images, width), F32),
            shape((3, gate, width), BF),
            shape((256, 256), F32),
        ),
        in_specs=[smem] + [anyb] * 4 + [vmem] * 3 + [anyb] + [vmem] * 4,
        out_specs=[anyb, anyb, vmem, anyb, vmem],
        scratch_shapes=[
            pltpu.VMEM((3, gate, width), F32),
            pltpu.VMEM((pad, pad), F32),
            pltpu.VMEM((pad, 128), F32),
            pltpu.SMEM((images,), jnp.int32),
            pltpu.SMEM((images,), jnp.int32),
            pltpu.SMEM((images,), jnp.int32),
            pltpu.VMEM((3, gate, width), BF),
            pltpu.VMEM((3, width, gate), BF),
            pltpu.VMEM((long, width), BF),
            pltpu.VMEM((long, width), BF),
        ]
        + [pltpu.VMEM((cap, gate), BF)] * 6
        + [
            pltpu.VMEM((cap, 128), F32),
            pltpu.VMEM((tm, gate), F32),
            pltpu.VMEM((pad, gate), F32),
            pltpu.VMEM((2, LOT, images, width), BF),
            pltpu.VMEM((2, LOT, images, width), BF),
            pltpu.VMEM((LOT * images, width), F32),
            pltpu.VMEM((LOT * images, width), F32),
            pltpu.VMEM((2, LOT, images, width), F32),
            pltpu.VMEM((2, LOT, images, width), F32),
            pltpu.VMEM((nvec, 8, width), F32),
            dma((3,)),
            dma((2, images)),
            dma((2, 2)),
            dma((2, 2)),
            dma((6, gate // width)),
        ],
        compiler_params=pltpu.CompilerParams(vmem_limit_bytes=60 * 2**20),
        name="block",
    )(info, tokens, cot, nm, bg, info, poolc, bsum, wt, vec, sp, spt, sbias)


def reduce_kernel(
    g_hbm, small_ref, red_ref, tot_ref, norm_ref,
    acc, rc, rr, rp, rz, sacc, src, srr, srp, srz, nbuf, mbuf, nown, mown,
    send, recv, lsem,
):
    x, y, z, c = place()
    px, py = jnp.where(c == 0, 1 - x, x), jnp.where(c == 0, y, 1 - y)
    rx, ry = jnp.where(c == 0, x, 1 - x), jnp.where(c == 0, 1 - y, y)
    dx, dy = 1 - x, 1 - y
    pnbr, rnbr, core = device(px, py, z, c), device(rx, ry, z, c), device(x, y, z, 1 - c)
    loads = [pltpu.make_async_copy(g_hbm.at[q, :, :, :, c], acc.at[q], lsem.at[q]) for q in range(3)]
    for cp in loads:
        cp.start()
    column = [device(x, y, (z + k) % 4, c) for k in (1, 2, 3)]
    column += [device(x, y, (z + k) % 4, 1 - c) for k in (0, 1, 2, 3)]
    plane = [device(dx, y, z, c), device(x, dy, z, c), device(dx, dy, z, c)]
    barrier = pltpu.get_barrier_semaphore()
    for peer in column + plane:
        pl.semaphore_signal(barrier, inc=1, device_id=peer, device_id_type=MESH)
    pl.semaphore_wait(barrier, len(column + plane))
    index = [0]
    started = []

    def remote(src_ref, dst_ref, dev):
        k = index[0]
        index[0] += 1
        cp = pltpu.make_async_remote_copy(
            src_ref=src_ref, dst_ref=dst_ref, send_sem=send.at[k], recv_sem=recv.at[k],
            device_id=dev, device_id_type=MESH,
        )
        cp.start()
        started.append(cp)
        return cp

    cut = acc.shape[4] // RCUTS
    cuts = [(3, 0)] + [(q, s) for s in range(RCUTS) for q in range(3)]

    def views(k):
        q, s = cuts[k]
        if q == 3:
            return (
                F32, lambda *i: sacc.at[i], lambda *i: src.at[i], lambda *i: srr.at[i],
                lambda *i: srp.at[i], lambda *i: srz.at[i],
            )
        at = pl.ds(s * cut, cut)

        def of(ref, dims):
            def view(*i):
                rest = (slice(None),) * (dims - len(i))
                return ref.at[(q,) + i + rest + (at,)]

            return view

        return BF, of(acc, 3), of(rc, 3), of(rr, 2), of(rp, 1), of(rz, 1)

    def plus(kind, a, b):
        a[...] = (a[...].astype(F32) + b[...].astype(F32)).astype(kind)

    swaps, r_in, p_in, z_in = {}, {}, {}, {}
    scopy = pltpu.make_async_copy(small_ref.at[:, :, :, c], sacc, lsem.at[3])
    scopy.start()
    for k, (q, s) in enumerate(cuts):
        if q == 3:
            swaps[k] = remote(small_ref.at[:, :, :, 1 - c], src, core)
        else:
            at = pl.ds(s * cut, cut)
            swaps[k] = remote(g_hbm.at[q, :, :, :, 1 - c, at], rc.at[q, :, :, :, at], core)

    def stage_two(k):
        kind, a, b, r, p, zz = views(k)
        if k == 0:
            scopy.wait()
        elif k <= 3:
            loads[cuts[k][0]].wait()
        swaps[k].wait_recv()
        for ly in range(2):
            for lx in range(2):
                for lz in range(4):
                    plus(kind, a(ly, lx, lz), b(ly, lx, lz))
        r_in[k] = [remote(a(dy, dx), r(0), rnbr), remote(a(ry, rx), r(1), rnbr)]

    def stage_three(k):
        kind, a, b, r, p, zz = views(k)
        for cp in r_in[k]:
            cp.wait_recv()
        for lz in range(4):
            plus(kind, a(py, px, lz), r(0, lz))
        p_in[k] = remote(a(py, px), p(), pnbr)
        for lz in range(4):
            plus(kind, a(y, x, lz), r(1, lz))

    def stage_four(k):
        kind, a, b, r, p, zz = views(k)
        p_in[k].wait_recv()
        for lz in range(4):
            plus(kind, a(y, x, lz), p(lz))
        z_in[k] = [
            remote(a(y, x, (z + j) % 4), zz(j - 1), device(x, y, (z + j) % 4, c)) for j in (1, 2, 3)
        ]

    def fold(v):
        t = jnp.zeros((8, 128), F32)
        for r in range(0, v.shape[0], 8):
            for l in range(0, v.shape[1], 128):
                part = v[r : r + 8, l : l + 128]
                t = t + part * part
        return t

    squares = [jnp.zeros((8, 128), F32)]
    tots = []

    def stage_five(k):
        kind, a, b, r, p, zz = views(k)
        for cp in z_in[k]:
            cp.wait_recv()
        v = (a(y, x, z)[...].astype(F32) + zz(0)[...].astype(F32)) + (
            zz(1)[...].astype(F32) + zz(2)[...].astype(F32)
        )
        squares[0] = squares[0] + fold(v)
        q, s = cuts[k]
        if q == 3:
            tot_ref[y, x, z, c] = v
            mine = tot_ref.at[y, x, z, c]
            tots.append([remote(mine, mine, dev) for dev in column])
        else:
            red_ref[q, s * cut : (s + 1) * cut] = v

    n = len(cuts)
    for t in range(n + 3 * RLAG):
        if t < n:
            stage_two(t)
        if 0 <= t - RLAG < n:
            stage_three(t - RLAG)
        if 0 <= t - 2 * RLAG < n:
            stage_four(t - 2 * RLAG)
        if 0 <= t - 3 * RLAG < n:
            stage_five(t - 3 * RLAG)
        if t == n:
            for cp in tots[0]:
                cp.wait_recv()
            lines = tot_ref.at[y, x]
            tots.append([remote(lines, lines, dev) for dev in plane])
    nown[...] = squares[0]
    sent = [remote(nown, nbuf.at[z * 2 + c], dev) for dev in column]
    nbuf[z * 2 + c] = squares[0]
    for cp in sent:
        cp.wait_recv()
    total = nbuf[0]
    for i in range(1, 8):
        total = total + nbuf[i]
    mown[...] = total
    sent = [remote(mown, mbuf.at[y * 2 + x], dev) for dev in plane]
    mbuf[y * 2 + x] = total
    for cp in sent:
        cp.wait_recv()
    total = mbuf[0]
    for i in range(1, 4):
        total = total + mbuf[i]
    total = jnp.sum(jnp.sum(total, axis=0, keepdims=True), axis=1, keepdims=True)
    norm_ref[...] = jnp.broadcast_to(jnp.sqrt(total), norm_ref.shape)
    for cp in tots[1]:
        cp.wait_recv()
    for cp in started:
        cp.wait_send()


RCUTS = 3
RLAG = 2
NRED = 7 * (3 * RCUTS + 1) + 20


def reduce_all(g, small):
    rows, width = g.shape[-2:]
    vmem = pl.BlockSpec(memory_space=pltpu.VMEM)
    anyb = pl.BlockSpec(memory_space=pl.ANY)
    dma = pltpu.SemaphoreType.DMA
    blk, sblk = (rows, width), small.shape[-2:]
    return pl.pallas_call(
        reduce_kernel,
        out_shape=(
            jax.ShapeDtypeStruct((3,) + blk, F32),
            jax.ShapeDtypeStruct(small.shape, F32),
            jax.ShapeDtypeStruct((8, 128), F32),
        ),
        in_specs=[anyb, vmem],
        out_specs=[vmem] * 3,
        scratch_shapes=[
            pltpu.VMEM((3, 2, 2, 4) + blk, BF),
            pltpu.VMEM((3, 2, 2, 4) + blk, BF),
            pltpu.VMEM((3, 2, 4) + blk, BF),
            pltpu.VMEM((3, 4) + blk, BF),
            pltpu.VMEM((3, 3) + blk, BF),
            pltpu.VMEM((2, 2, 4) + sblk, F32),
            pltpu.VMEM((2, 2, 4) + sblk, F32),
            pltpu.VMEM((2, 4) + sblk, F32),
            pltpu.VMEM((4,) + sblk, F32),
            pltpu.VMEM((3,) + sblk, F32),
            pltpu.VMEM((8, 8, 128), F32),
            pltpu.VMEM((4, 8, 128), F32),
            pltpu.VMEM((8, 128), F32),
            pltpu.VMEM((8, 128), F32),
            dma((NRED,)), dma((NRED,)), dma((4,)),
        ],
        compiler_params=pltpu.CompilerParams(
            collective_id=1, has_side_effects=True, vmem_limit_bytes=60 * 2**20
        ),
        name="reduce",
    )(g, small)


STEP = 10
BETA_FIRST = 0.9
BETA_SECOND = 0.95
ADAM_EPS = 1e-08
DECAY_RATE = 0.05
RATE_MATRIX = 0.05
RATE_VECTOR = 0.8
CLIP_BOUND = 1.0
BOTH = ("dp", "fsdp")


def adam_step(weight, first, second, gradient, step_rate, weight_decay):
    first_new = BETA_FIRST * first + (1.0 - BETA_FIRST) * gradient
    second_new = BETA_SECOND * second + (1.0 - BETA_SECOND) * gradient * gradient
    first_hat = first_new * (1.0 / (1.0 - BETA_FIRST**STEP))
    second_hat = second_new * (1.0 / (1.0 - BETA_SECOND**STEP))
    weight_new = weight - step_rate * (
        first_hat / (jnp.sqrt(second_hat) + ADAM_EPS) + weight_decay * weight
    )
    return (weight_new, first_new, second_new)


def adam_kernel(own, red, tot, norm, iw, i1, i2, ow, o1, o2, sw, s1, s2, *outs):
    clip = CLIP_BOUND / jnp.maximum(norm[0:1, 0:1], CLIP_BOUND)
    rows = ow.shape[0]
    for q in range(2):
        for r in range(0, rows, 8):
            cut = slice(r, r + 8)
            new = adam_step(
                iw[q, cut], i1[q, cut], i2[q, cut], red[q, cut] * clip, RATE_MATRIX, DECAY_RATE
            )
            for ref, val in zip(outs[0:3], new):
                ref[q, cut] = val
    for r in range(0, rows, 8):
        cut = slice(r, r + 8)
        new = adam_step(ow[cut], o1[cut], o2[cut], red[2, cut] * clip, RATE_MATRIX, DECAY_RATE)
        for ref, val in zip(outs[3:6], new):
            ref[cut] = val
    me = lax.axis_index("dp") * lax.axis_size("fsdp") + lax.axis_index("fsdp")
    start = me * own
    row, off = start // 256, start % 256
    pair = [jnp.broadcast_to(tot[pl.ds(row + i, 1), :], (8, 256)) for i in (0, 1)]
    pair = pltpu.roll(jnp.concatenate(pair, axis=1), (512 - off) % 512, 1)
    outs[9][...] = pair[0:1, 0:256] * clip
    outs[10][...] = norm[0:1, 0:1]
    side, cols = sw.shape
    grad = tot[SPATIAL_ROW : SPATIAL_ROW + side, 0:cols] * clip
    last = lax.broadcasted_iota(jnp.int32, (side, 1), 0) == side - 1
    rate = jnp.where(last, RATE_VECTOR, RATE_MATRIX)
    decay = jnp.where(last, 0.0, DECAY_RATE)
    new = adam_step(sw[...], s1[...], s2[...], grad, rate, decay)
    for ref, val in zip(outs[6:9], new):
        ref[...] = val


def adam_all(own, red, tot, norm, inner, outer, spatial):
    vmem = pl.BlockSpec(memory_space=pltpu.VMEM)
    shape = lambda a: jax.ShapeDtypeStruct(a.shape, F32)
    return pl.pallas_call(
        functools.partial(adam_kernel, own),
        out_shape=tuple(shape(a) for a in inner + outer + spatial)
        + (jax.ShapeDtypeStruct((1, 256), F32), jax.ShapeDtypeStruct((1, 1), F32)),
        in_specs=[vmem] * 12,
        out_specs=[vmem] * 11,
        compiler_params=pltpu.CompilerParams(vmem_limit_bytes=60 * 2**20),
        name="adam",
    )(red, tot, norm, *inner, *outer, *spatial)


def slow_prepare(inner_t, outer_weight, vectors, tokens, cot, mask, keep, pool_cot, spatial):
    patches, images, width = tokens.shape
    pad = -(-patches // LOT) * LOT
    wt = jnp.concatenate(
        [
            lax.all_gather(inner_t.astype(BF), BOTH, axis=1, tiled=True),
            lax.all_gather(outer_weight.astype(BF), BOTH, axis=0, tiled=True)[None],
        ],
        axis=0,
    )
    vec = lax.all_gather(vectors.astype(BF), BOTH, axis=0, tiled=True).astype(F32)
    vec = vec.reshape(-1, width)
    counts = jnp.sum(mask, axis=1)
    info = jnp.zeros((images, 128), jnp.int32).at[:, 0].set(counts).at[:, 1].set(keep)
    poolc = pool_cot.astype(F32) / counts.astype(F32)[:, None]
    unit, _ = norm(tokens.astype(F32))
    edge = ((0, 0), (0, pad - patches), (0, 0))
    nm = (unit * vec[0] + vec[1]).astype(BF)
    live = mask.astype(F32).T[:, :, None]
    scale = keep.astype(F32) * (1.0 / (1.0 - DROP_RATE))
    bg = (scale[:, None] * (cot.astype(F32) + live * poolc)).astype(BF)
    bsum = jnp.sum(bg, axis=0, dtype=F32)
    nm = jnp.pad(nm.transpose(1, 0, 2), edge)
    bg = jnp.pad((bg * live.astype(BF)).transpose(1, 0, 2), edge)
    low = spatial[:patches].astype(BF)
    square = ((0, 256 - patches), (0, 256 - patches))
    sbias = jnp.pad(spatial[patches][:, None], ((0, 256 - patches), (0, 0)))
    return wt, vec, nm, bg, info, poolc, bsum, jnp.pad(low, square), jnp.pad(low.T, square), sbias


def slow_reduce(grads, small):
    red = lax.psum_scatter(grads.astype(F32), BOTH, scatter_dimension=1, tiled=True)
    tot = lax.psum(small, BOTH)
    squares = lax.psum(jnp.sum(red * red), BOTH) + jnp.sum(tot * tot)
    return red, tot, jnp.broadcast_to(jnp.sqrt(squares), (8, 128))


def per_device(
    fast,
    tokens,
    valid_mask,
    keep_mask,
    out_cotangent,
    pool_cotangent,
    inner_weight,
    outer_weight,
    vectors,
    spatial,
    inner_first,
    inner_second,
    outer_first,
    outer_second,
    vector_first,
    vector_second,
    spatial_first,
    spatial_second,
):
    own = vectors.shape[0]
    rows, width = outer_weight.shape
    inner_t = tuple(a.transpose(0, 2, 1) for a in (inner_weight, inner_first, inner_second))
    tokens = tokens.transpose(1, 0, 2)
    cot = out_cotangent.transpose(1, 0, 2)
    if fast:
        wt, *ready = gather_all(
            own,
            inner_t[0],
            outer_weight,
            jnp.pad(vectors, (0, 1024 - own)).reshape(8, 128),
            tokens,
            cot,
            valid_mask,
            keep_mask,
            pool_cotangent,
            spatial,
        )
        wt = wt.reshape(3, 32 * rows, width)
    else:
        wt, *ready = slow_prepare(
            inner_t[0], outer_weight, vectors, tokens, cot, valid_mask, keep_mask, pool_cotangent, spatial
        )
    vec, nm, bg, info, poolc, bsum, sp, spt, sbias = ready
    output, input_grad, pooled, grads, small = run_block(
        tokens, cot, nm, bg, info, poolc, bsum, wt, vec, sp, spt, sbias
    )
    output = output.transpose(1, 0, 2)
    input_grad = input_grad.transpose(1, 0, 2)
    if fast:
        red, tot, norm = reduce_all(
            grads.reshape(3, 2, 2, 4, 2, rows, width), small.reshape(2, 2, 4, 2, 8, 256)
        )
        tot = tot.reshape(256, 256)
    else:
        red, tot, norm = slow_reduce(grads, small)
    new = adam_all(
        own,
        red,
        tot,
        norm,
        inner_t,
        (outer_weight, outer_first, outer_second),
        (spatial, spatial_first, spatial_second),
    )
    grad_norm = new[10].reshape(())
    vector_out = adam_step(
        vectors, vector_first, vector_second, new[9].reshape(-1)[:own], RATE_VECTOR, 0.0
    )
    return (
        (output, input_grad, pooled, grad_norm)
        + tuple(a.transpose(0, 2, 1) for a in new[0:3])
        + tuple(new[3:6])
        + vector_out
        + tuple(new[6:9])
    )


def solution(mesh):
    fast = mesh.shape["dp"] == 4 and mesh.shape["fsdp"] == 8
    rows3 = P(BOTH, None, None)
    rows2 = P(BOTH, None)
    rows1 = P(BOTH)
    cols3 = P(None, None, BOTH)
    in_specs = (
        (rows3, rows2, rows1, rows3, rows2, cols3, rows2, rows1, P())
        + (cols3,) * 2
        + (rows2,) * 2
        + (rows1,) * 2
        + (P(),) * 2
    )
    out_specs = (
        (rows3, rows3, rows2, P()) + (cols3,) * 3 + (rows2,) * 3 + (rows1,) * 3 + (P(),) * 3
    )
    return jax.shard_map(
        functools.partial(per_device, fast),
        mesh=mesh,
        in_specs=in_specs,
        out_specs=out_specs,
        check_vma=False,
    )
```

```python
import functools

import jax
import jax.numpy as jnp
from jax import lax
from jax.experimental import pallas as pl
from jax.experimental.pallas import tpu as pltpu
from jax.sharding import PartitionSpec as P

NORM_EPS = 1e-05
DROP_RATE = 0.1
BF = jnp.bfloat16
F32 = jnp.float32
MESH = pl.DeviceIdType.MESH
GELU_K = 0.7978845608
GELU_C = 0.044715
NN = (((1,), (0,)), ((), ()))
NT = (((1,), (1,)), ((), ()))
TN = (((0,), (0,)), ((), ()))
LOT = 16
CUTS = 3
SLAB = 2


def dot(a, b, dims):
    return lax.dot_general(a, b, dims, preferred_element_type=F32)


def norm(x):
    c = x - jnp.mean(x, axis=-1, keepdims=True)
    inv = lax.rsqrt(jnp.mean(c * c, axis=-1, keepdims=True) + NORM_EPS)
    return c * inv, inv


def swap_matrix(images):
    side = LOT * images
    r = lax.broadcasted_iota(jnp.int32, (side, side), 0)
    s = lax.broadcasted_iota(jnp.int32, (side, side), 1)
    return jnp.where(s == (r % LOT) * images + r // LOT, 1.0, 0.0).astype(BF)


def unswap_matrix(images):
    side = LOT * images
    r = lax.broadcasted_iota(jnp.int32, (side, side), 0)
    s = lax.broadcasted_iota(jnp.int32, (side, side), 1)
    return jnp.where(s == (r % images) * LOT + r // images, 1.0, 0.0).astype(BF)


def place():
    d = lax.axis_index("dp")
    f = lax.axis_index("fsdp")
    return d % 2, d // 2, f // 2, f % 2


def device(x, y, z, c):
    return (y * 2 + x, z * 2 + c)


def greet_partners():
    x, y, z, c = place()
    barrier = pltpu.get_barrier_semaphore()
    peers = [device(1 - x, y, z, c), device(x, 1 - y, z, c), device(x, y, z, 1 - c)]
    peers += [device(x, y, (z + k) % 4, c) for k in (1, 2, 3)]
    for peer in peers:
        pl.semaphore_signal(barrier, inc=1, device_id=peer, device_id_type=MESH)
    pl.semaphore_wait(barrier, len(peers))


def gather_kernel(
    own_len,
    inner_ref, outer_ref, vec_ref, tokens_hbm, cot_hbm, mask_ref, keep_ref, pool_ref, spatial_ref,
    all_ref, vecs_ref, nm_ref, bg_ref, info_ref, poolc_ref, bsum_ref, sp_ref, spt_ref, sbias_ref,
    own, vown, vgot, wide, xblk, cblk, nrow, brow, nm_v, bg_v, send, recv, lsem, isem, osem,
):
    x, y, z, c = place()
    patches, images, width = tokens_hbm.shape
    own[0] = inner_ref[0].astype(BF)
    own[1] = inner_ref[1].astype(BF)
    own[2] = outer_ref[...].astype(BF)
    vown[...] = vec_ref[...].astype(BF).astype(F32)
    loads = [
        pltpu.make_async_copy(tokens_hbm, xblk, isem.at[0]),
        pltpu.make_async_copy(cot_hbm, cblk, isem.at[1]),
    ]
    for cp in loads:
        cp.start()
    greet_partners()
    local = pltpu.make_async_copy(own, all_ref.at[:, y, x, z, c], lsem)
    local.start()
    vgot[y, x, z, c] = vown[...]

    px, py = jnp.where(c == 0, 1 - x, x), jnp.where(c == 0, y, 1 - y)
    rx, ry = jnp.where(c == 0, x, 1 - x), jnp.where(c == 0, 1 - y, y)
    dx, dy = 1 - x, 1 - y
    index = [0]
    pnbr, rnbr, core = device(px, py, z, c), device(rx, ry, z, c), device(x, y, z, 1 - c)
    cut = outer_ref.shape[0] // CUTS
    started = []

    def remote(src, dst, dev):
        k = index[0]
        index[0] += 1
        cp = pltpu.make_async_remote_copy(
            src_ref=src, dst_ref=dst, send_sem=send.at[k], recv_sem=recv.at[k],
            device_id=dev, device_id_type=MESH,
        )
        cp.start()
        started.append(cp)
        return cp

    def span(s):
        return pl.ds(s * cut, cut)

    def block(q, s, by, bx):
        if q == 3:
            return vgot.at[by, bx, z, c]
        return all_ref.at[q, by, bx, z, c, span(s)]

    def z_sends(src, q, s, by, bx):
        return [remote(src, block(q, s, by, bx), device(x, y, (z + k) % 4, c)) for k in (1, 2, 3)]

    def send_line(q, s, ly, lx, dev):
        ref = vgot.at[ly, lx, :, c] if q == 3 else all_ref.at[q, ly, lx, :, c, span(s)]
        return remote(ref, ref, dev)

    cuts = [(3, 0)] + [(q, s) for s in range(CUTS) for q in range(3)]
    zs = [None] * len(cuts)

    def start_z(k):
        if k < len(cuts):
            q, s = cuts[k]
            src = vown if q == 3 else own.at[q, span(s)]
            zs[k] = z_sends(src, q, s, y, x)

    for k in range(WINDOW):
        start_z(k)
    local.wait()

    counts = jnp.sum(mask_ref[...], axis=1, keepdims=True)
    keeps = jnp.zeros((images, 1), jnp.int32)
    image = lax.broadcasted_iota(jnp.int32, (images, 1), 0)
    for b in range(images):
        keeps = jnp.where(image == b, keep_ref[b], keeps)
    scale = keeps.astype(F32) * (1.0 / (1.0 - DROP_RATE))
    lane = lax.broadcasted_iota(jnp.int32, info_ref.shape, 1)
    info_ref[...] = jnp.where(lane == 0, counts, keeps)
    poolc = pool_ref[...].astype(F32) / counts.astype(F32)
    poolc_ref[...] = poolc
    side = spatial_ref.shape[1]
    wide[...] = jnp.zeros_like(wide)
    wide[0 : side + 1, 0:side] = spatial_ref[...]
    mat = wide[...]
    mat_t = mat.T
    span_a = lax.broadcasted_iota(jnp.int32, mat.shape, 0)
    span_b = lax.broadcasted_iota(jnp.int32, mat.shape, 1)
    sp_ref[...] = jnp.where(span_a < side, mat, 0.0).astype(BF)
    spt_ref[...] = jnp.where(span_b < side, mat_t, 0.0).astype(BF)
    sbias_ref[...] = mat_t[:, side : side + 1]
    bsum_ref[...] = jnp.zeros_like(bsum_ref)
    vecs_ref[...] = jnp.zeros_like(vecs_ref)

    def stack_vectors():
        per = width // 128
        for d in range(32):
            start = own_len * d
            shift = start % 128
            blk = vgot[d // 16, d // 8 % 2, d // 2 % 4, d % 2]
            row = jnp.concatenate(
                [jnp.broadcast_to(blk[i : i + 1, :], (8, 128)) for i in range(3)], axis=1
            )
            row = pltpu.roll(row, shift, 1) if shift else row
            for i in range(3):
                r = start // 128 + i
                if r * 128 < start + own_len:
                    at = (slice(r // per, r // per + 1), slice(r % per * 128, r % per * 128 + 128))
                    vecs_ref[at] += row[0:1, i * 128 : i * 128 + 128]

    swap = swap_matrix(images)

    def token_block(k, many):
        gain, shift = vecs_ref[0:1, :], vecs_ref[1:2, :]
        total = jnp.zeros((images, width), F32)
        for p in range(0, many, SLAB):
            patch = lax.broadcasted_iota(jnp.int32, (SLAB, images, 1), 0) + (k * LOT + p)
            at = pl.ds(k * LOT + p, SLAB)
            cut = slice(p * images, (p + SLAB) * images)
            unit, _ = norm(xblk[at].astype(F32))
            nrow[cut, :] = (unit * gain + shift).astype(BF).reshape(SLAB * images, width)
            live = jnp.where(counts > patch, 1.0, 0.0)
            og = cblk[at].astype(F32) + live * poolc
            bg = (scale * og).astype(BF).astype(F32)
            total = total + jnp.sum(bg, axis=0)
            brow[cut, :] = (live * bg).astype(BF).reshape(SLAB * images, width)
        bsum_ref[...] += total
        part = swap[:, 0 : many * images]
        for src, dst in ((nrow, nm_v), (brow, bg_v)):
            moved = dot(part, src[0 : many * images, :], NN).astype(BF)
            at = pl.ds(pl.multiple_of(k * LOT, LOT), LOT)
            dst[:, at, :] = moved.reshape(images, LOT, width)

    full = patches // LOT
    todo = list(range(full + (1 if patches % LOT else 0)))

    stores = []
    pad = nm_v.shape[1]
    marks = [pad // (2 * LOT) * LOT, pad]

    def some_tokens(many):
        for _ in range(many):
            if not todo:
                return
            k = todo.pop(0)
            token_block(k, LOT if k < full else patches % LOT)
            end = (k + 1) * LOT
            if end in marks:
                at = pl.ds(0, end) if end == marks[0] else pl.ds(marks[0], end - marks[0])
                for src, dst in ((nm_v, nm_ref), (bg_v, bg_ref)):
                    cp = pltpu.make_async_copy(src.at[:, at], dst.at[:, at], osem.at[len(stores)])
                    cp.start()
                    stores.append(cp)

    lines_p, lines_r, lines_r2, cores = {}, {}, {}, {}

    def swap_core(k, cp):
        cores.setdefault(k, []).append(cp)


    def stage_two(k):
        q, s = cuts[k]
        for cp in zs[k]:
            cp.wait_recv()
        start_z(k + WINDOW)
        lines_p[k] = send_line(q, s, y, x, pnbr)
        lines_r[k] = send_line(q, s, y, x, rnbr)
        swap_core(k, send_line(q, s, y, x, core))

    def stage_three(k):
        q, s = cuts[k]
        lines_p[k].wait_recv()
        lines_r2[k] = send_line(q, s, py, px, rnbr)
        swap_core(k, send_line(q, s, py, px, core))

    def stage_four(k):
        q, s = cuts[k]
        lines_r[k].wait_recv()
        swap_core(k, send_line(q, s, ry, rx, core))

    def stage_five(k):
        q, s = cuts[k]
        lines_r2[k].wait_recv()
        swap_core(k, send_line(q, s, dy, dx, core))

    n = len(cuts)
    for t in range(n + LAG_FIVE):
        if t < n:
            stage_two(t)
        if 0 <= t - LAG_THREE < n:
            stage_three(t - LAG_THREE)
            stage_four(t - LAG_THREE)
        if 0 <= t - LAG_FIVE < n:
            stage_five(t - LAG_FIVE)
        if t == LAG_FIVE + 1:
            for cp in cores[0]:
                cp.wait_recv()
            stack_vectors()
            for cp in loads:
                cp.wait()
        if t > LAG_FIVE:
            some_tokens(-(-13 // (n - 1)))
    some_tokens(len(todo))
    for k in range(1, n):
        for cp in cores[k]:
            cp.wait_recv()
    for cp in started:
        cp.wait_send()
    for cp in stores:
        cp.wait()


NSEND = 10 * (3 * CUTS + 1)
LAG_THREE = 3
LAG_FIVE = 6
WINDOW = 4


def gather_all(own_len, inner, outer, vec, tokens, cot, mask, keep, pool, spatial):
    rows, width = outer.shape
    patches, images, _ = tokens.shape
    pad = -(-patches // LOT) * LOT
    vmem = pl.BlockSpec(memory_space=pltpu.VMEM)
    smem = pl.BlockSpec(memory_space=pltpu.SMEM)
    anyb = pl.BlockSpec(memory_space=pl.ANY)
    dma = pltpu.SemaphoreType.DMA
    shape = jax.ShapeDtypeStruct
    return pl.pallas_call(
        functools.partial(gather_kernel, own_len),
        out_shape=(
            shape((3, 2, 2, 4, 2, rows, width), BF),
            shape((16, width), F32),
            shape((images, pad, width), BF),
            shape((images, pad, width), BF),
            shape((images, 128), jnp.int32),
            shape((images, width), F32),
            shape((images, width), F32),
            shape((256, 256), BF),
            shape((256, 256), BF),
            shape((256, 1), F32),
        ),
        in_specs=[vmem] * 3 + [anyb] * 2 + [vmem, smem, vmem, vmem],
        out_specs=[anyb, vmem, anyb, anyb] + [vmem] * 6,
        scratch_shapes=[
            pltpu.VMEM((3, rows, width), BF),
            pltpu.VMEM((8, 128), F32),
            pltpu.VMEM((2, 2, 4, 2, 8, 128), F32),
            pltpu.VMEM((256, 256), F32),
            pltpu.VMEM((patches, images, width), BF),
            pltpu.VMEM((patches, images, width), BF),
            pltpu.VMEM((LOT * images, width), BF),
            pltpu.VMEM((LOT * images, width), BF),
            pltpu.VMEM((images, pad, width), BF),
            pltpu.VMEM((images, pad, width), BF),
            dma((NSEND,)), dma((NSEND,)), dma, dma((2,)), dma((4,)),
        ],
        compiler_params=pltpu.CompilerParams(
            collective_id=0, has_side_effects=True, vmem_limit_bytes=60 * 2**20
        ),
        name="gather",
    )(inner, outer, vec, tokens, cot, mask, keep, pool, spatial)


def gelu_pair(v):
    u = v * v
    s = 0.5 * jnp.tanh(v * (GELU_K + (GELU_K * GELU_C) * u)) + 0.5
    h = v * s
    d = s + (h - h * s) * (2.0 * GELU_K + (6.0 * GELU_K * GELU_C) * u)
    return h, d


def fold8(x):
    total = x[0:8]
    for r in range(8, x.shape[0], 8):
        total = total + x[r : r + 8]
    return total


def lanes(x):
    total = x[:, 0:128]
    for c in range(128, x.shape[1], 128):
        total = total + x[:, c : c + 128]
    return total


def loop(lo, hi, fn):
    def body(i, c):
        fn(i)
        return c

    lax.fori_loop(lo, hi, body, 0)


def block_kernel(
    cfg,
    info_s,
    tokens_hbm, cot_hbm, nm_hbm, bg_hbm,
    info_ref, poolc_ref, bsum_ref, wt_hbm, vec_ref, sp_ref, spt_ref, sbias_ref,
    out_hbm, ig_hbm, pooled_ref, grads_hbm, small_ref,
    acc, sg_ref, sbg_ref, off_s, gend_s, grows_s,
    wt_ref, wtt, nm_b, bg_b, h0_b, e0_b, mg_b, xm_b, u2_b, d1_b, stat_b, h1_s, t_s,
    xblk, cblk, br_s, ng_s, out_st, ig_st, vacc,
    wt_sem, pack_sem, in_sem, out_sem, grad_sem,
):
    images, patches, width, gate, rows_cap, tm, classes = cfg
    cw = 256
    nj = gate // cw
    chunks = -(-patches // LOT)
    zero_row = nm_b.shape[0] - LOT
    g2_base, s2_base = 3 * width, 3 * width + gate
    b0_base, b1_base = 3 * width + 2 * gate, 3 * width + 3 * gate

    def vrow(base, j):
        start = base + j * cw
        return vec_ref[start // width : start // width + 1, start % width : start % width + cw]

    def count(b):
        return info_s[b, 0]

    def keep(b):
        return info_s[b, 1]

    def need_of(b):
        return keep(b) * ((count(b) + LOT - 1) // LOT)

    wt_loads = [pltpu.make_async_copy(wt_hbm.at[q], wt_ref.at[q], wt_sem.at[q]) for q in range(3)]
    for q in (1, 0, 2):
        wt_loads[q].start()

    def plan(b, carry):
        group, row, first = carry
        need = need_of(b) * LOT
        over = row + need - first > rows_cap
        group = group + over.astype(jnp.int32)
        first = jnp.where(over, row, first)
        off_s[b] = row
        row = row + need
        gend_s[group] = b + 1
        grows_s[group] = row - first
        return group, row, first

    zero = jnp.int32(0)
    last_group, all_rows, _ = lax.fori_loop(0, images, plan, (zero, zero, zero))

    def pack(b, act):
        lots = need_of(b)
        o = off_s[b]
        done = jnp.int32(0)
        for size in (8, 4, 2, 1):
            @pl.when((lots & size) != 0)
            def _(size=size, done=done):
                src = pl.ds(pl.multiple_of(done * LOT, LOT), size * LOT)
                dst = pl.ds(pl.multiple_of(o + done * LOT, LOT), size * LOT)
                for i, (far, near) in enumerate(((nm_hbm, nm_b), (bg_hbm, bg_b))):
                    act(pltpu.make_async_copy(far.at[b, src], near.at[dst], pack_sem.at[i, b]))

            done = done + (lots & size)

    loop(0, images, lambda b: pack(b, lambda cp: cp.start()))

    full = patches // LOT
    rest = patches % LOT

    def load_lot(k, many, slot):
        at = pl.ds(k * LOT, many)
        return (
            pltpu.make_async_copy(tokens_hbm.at[at], xblk.at[slot, pl.ds(0, many)], in_sem.at[0, slot]),
            pltpu.make_async_copy(cot_hbm.at[at], cblk.at[slot, pl.ds(0, many)], in_sem.at[1, slot]),
        )

    for k in (0, 1):
        for cp in load_lot(k, LOT, k):
            cp.start()

    def zero_rows(ref, n_chunks, start):
        z = jnp.zeros((LOT, ref.shape[1]), ref.dtype)

        def body(i):
            ref[pl.ds(pl.multiple_of(start + i * LOT, LOT), LOT), :] = z

        loop(0, n_chunks, body)

    for ref in (mg_b, xm_b, u2_b):
        zero_rows(ref, ref.shape[0] // LOT, 0)
    for ref in (nm_b, bg_b):
        zero_rows(ref, tm // LOT, all_rows)
    z = jnp.zeros((LOT, width), BF)
    nm_b[zero_row : zero_row + LOT, :] = z
    bg_b[zero_row : zero_row + LOT, :] = z
    vacc[...] = jnp.zeros_like(vacc)
    acc[...] = jnp.zeros_like(acc)
    sg_ref[...] = jnp.zeros_like(sg_ref)
    sbg_ref[...] = jnp.zeros_like(sbg_ref)
    for q in (1, 0, 2):
        wt_loads[q].wait()
        for j in range(nj):
            wtt[q, :, j * cw : (j + 1) * cw] = wt_ref[q, j * cw : (j + 1) * cw, :].T
    loop(0, images, lambda b: pack(b, lambda cp: cp.wait()))

    def phase_a(t, gs):
        r0 = pl.multiple_of(t * tm, tm)
        rows = pl.ds(r0, tm)
        here = pl.ds(pl.multiple_of(gs + r0, LOT), tm)
        nb = nm_b[here, :]
        bgt = bg_b[here, :]
        s1 = jnp.zeros((tm, 128), F32)
        for j in range(nj):
            cols = slice(j * cw, (j + 1) * cw)
            a1 = dot(nb, wtt[1, :, cols], NN) + vrow(b1_base, j)
            h1, d1 = gelu_pair(a1)
            h1_s[:, cols] = h1
            d1_b[rows, cols] = d1.astype(BF)
            s1 = s1 + lanes(h1)
        mean = jnp.sum(s1, axis=1, keepdims=True) * (1.0 / gate)
        q1 = jnp.zeros((tm, 128), F32)
        for j in range(nj):
            cols = slice(j * cw, (j + 1) * cw)
            a0 = dot(nb, wtt[0, :, cols], NN) + vrow(b0_base, j)
            h0, d0 = gelu_pair(a0)
            gg = dot(bgt, wtt[2, :, cols], NN)
            mg = gg * h0
            h0_b[rows, cols] = h0.astype(BF)
            mg_b[rows, cols] = mg.astype(BF)
            e0_b[rows, cols] = (gg * d0).astype(BF)
            c = h1_s[:, cols] - mean
            q1 = q1 + lanes(c * c)
        inv = lax.rsqrt(jnp.sum(q1, axis=1, keepdims=True) * (1.0 / gate) + NORM_EPS)
        stat_b[rows, :] = jnp.broadcast_to(inv, (tm, 128))
        for j in range(nj):
            cols = slice(j * cw, (j + 1) * cw)
            u2 = (h1_s[:, cols] - mean) * inv
            u2_b[rows, cols] = u2.astype(BF)
            xm_b[rows, cols] = (u2 * vrow(g2_base, j) + vrow(s2_base, j)).astype(BF)

    def phase_b(b, m, gs):
        n = count(b)
        o = pl.multiple_of(off_s[b] - gs, LOT)
        rows = pl.ds(o, m)
        rid = lax.broadcasted_iota(jnp.int32, (m, 1), 0)
        cid = lax.broadcasted_iota(jnp.int32, (m, m), 1)
        rid2 = lax.broadcasted_iota(jnp.int32, (m, m), 0)
        both = (cid < n) & (rid2 < n)
        sp = jnp.where(both, sp_ref[0:m, 0:m], 0.0).astype(BF)
        spt = jnp.where(both, spt_ref[0:m, 0:m], 0.0).astype(BF)
        valid = rid < n
        fill = jnp.where(rid < need_of(b) * LOT, 0.0, 1.0)
        sbias = jnp.where(valid, sbias_ref[0:m, :], fill)
        inv = jnp.where(valid, stat_b[rows, 0:1], 0.0)
        ones = jnp.ones((LOT, gate), BF)
        tsum = jnp.zeros((m, 128), F32)
        tdot = jnp.zeros((m, 128), F32)
        xm_ones = jnp.concatenate([xm_b[rows, :], ones], axis=0)
        sg = dot(mg_b[rows, :], xm_ones, NT)
        sg_ref[0:m, 0:m] += jnp.where(both, sg[:, 0:m], 0.0)
        sbg_ref[0:m, 0:1] += jnp.where(valid, sg[:, m : m + 1], 0.0)
        for j in range(nj):
            cols = slice(j * cw, (j + 1) * cw)
            xm = xm_b[rows, cols]
            mg = mg_b[rows, cols]
            so = (dot(sp, xm, NN) + sbias).astype(BF)
            mix = dot(spt, mg, NN)
            h0_b[rows, cols] = h0_b[rows, cols] * so
            e0_b[rows, cols] = e0_b[rows, cols] * so
            u2 = u2_b[rows, cols].astype(F32)
            mu = mix * u2
            gain = vrow(g2_base, j)
            t = mix * gain
            t_s[0:m, cols] = t
            tsum = tsum + lanes(t)
            tdot = tdot + lanes(mu * gain)
            vi, lo = j * cw // width, j * cw % width
            vacc[g2_base // width + vi, :, lo : lo + cw] += fold8(mu)
            vacc[s2_base // width + vi, :, lo : lo + cw] += fold8(mix)
        m1 = jnp.sum(tsum, axis=1, keepdims=True) * (1.0 / gate)
        m2 = jnp.sum(tdot, axis=1, keepdims=True) * (1.0 / gate)
        base, slope = fill - inv * m1, inv * m2
        for j in range(nj):
            cols = slice(j * cw, (j + 1) * cw)
            u2 = u2_b[rows, cols].astype(F32)
            sec = (inv * t_s[0:m, cols] + (base - u2 * slope)).astype(BF)
            d1_b[rows, cols] = d1_b[rows, cols] * sec

    def phase_c(t, gs, group_rows):
        r0 = pl.multiple_of(t * tm, tm)
        rows = pl.ds(r0, tm)
        here = pl.ds(pl.multiple_of(gs + r0, LOT), tm)
        nb = nm_b[here, :]
        bgt = bg_b[here, :]
        mine = lax.broadcasted_iota(jnp.int32, (tm, 1), 0) < group_rows - r0
        br = dot(h0_b[rows, :], wt_ref[2], NN)
        bg_b[here, :] = jnp.where(mine, br, bgt.astype(F32)).astype(BF)
        ng = dot(e0_b[rows, :], wt_ref[0], NN) + dot(d1_b[rows, :], wt_ref[1], NN)
        nm_b[here, :] = jnp.where(mine, ng, nb.astype(F32)).astype(BF)
        for j in range(nj):
            cols = slice(j * cw, (j + 1) * cw)
            vi, lo = j * cw // width, j * cw % width
            e0, d1 = e0_b[rows, cols], d1_b[rows, cols]
            acc[0, cols, :] += dot(e0, nb, TN)
            acc[1, cols, :] += dot(d1, nb, TN)
            acc[2, cols, :] += dot(h0_b[rows, cols], bgt, TN)
            vacc[b0_base // width + vi, :, lo : lo + cw] += fold8(e0.astype(F32))
            vacc[b1_base // width + vi, :, lo : lo + cw] += fold8(d1.astype(F32))

    def group(g, carry):
        b_start, gs = carry
        b_end = gend_s[g]
        rows = grows_s[g]
        tiles = (rows + tm - 1) // tm
        loop(0, tiles, lambda t: phase_a(t, gs))

        def do_b(b):
            low = 0
            for m in classes:
                @pl.when((keep(b) == 1) & (count(b) > low) & (count(b) <= m))
                def _(m=m):
                    phase_b(b, m, gs)

                low = m

        loop(b_start, b_end, do_b)
        tail = (tiles * tm - rows) // LOT
        for ref in (h0_b, e0_b, d1_b):
            zero_rows(ref, tail, rows)
        loop(0, tiles, lambda t: phase_c(t, gs, rows))
        return b_end, gs + rows

    lax.fori_loop(0, last_group + 1, group, (zero, zero))

    half = gate // 2
    grad_out = []
    per = gate // width
    for i in range(6):
        q, lo = i // 2, (i % 2) * half
        buf = (h1_s, t_s)[0]
        del buf
        stage = (mg_b, xm_b)[i % 2]
        if i >= 2:
            for cp in grad_out[i - 2]:
                cp.wait()
        cps = []
        for v in range(per):
            third = half // per
            cut = slice(v * width, (v + 1) * width)
            stage[0:third, cut] = acc[q, lo + v * third : lo + (v + 1) * third, :].astype(BF)
            cps.append(
                pltpu.make_async_copy(
                    stage.at[pl.ds(0, third), pl.ds(v * width, width)],
                    grads_hbm.at[q, pl.ds(lo + v * third, third)],
                    grad_sem.at[i, v],
                )
            )
        for cp in cps:
            cp.start()
        grad_out.append(cps)

    counts = info_ref[:, 0:1]
    scale = info_ref[:, 1:2].astype(F32) * (1.0 / (1.0 - DROP_RATE))
    poolc = poolc_ref[...]
    gain_one, bias_out = vec_ref[0:1, :], vec_ref[2:3, :]
    back = unswap_matrix(images)

    def store_lot(k, many, slot):
        at = pl.ds(k * LOT, many)
        return (
            pltpu.make_async_copy(out_st.at[slot, pl.ds(0, many)], out_hbm.at[at], out_sem.at[0, slot]),
            pltpu.make_async_copy(ig_st.at[slot, pl.ds(0, many)], ig_hbm.at[at], out_sem.at[1, slot]),
        )

    pooled_ref[...] = jnp.zeros_like(pooled_ref)

    def lot(k, many, slot):
        for cp in load_lot(k, many, slot):
            cp.wait()
        parts = [[], []]
        for b in range(images):
            there = k < need_of(b)
            row = pl.multiple_of(jnp.where(there, off_s[b] + k * LOT, zero_row), LOT)
            parts[0].append(bg_b[pl.ds(row, LOT), :])
            parts[1].append(nm_b[pl.ds(row, LOT), :])
        mat = back[0 : many * images, :]
        br_s[0 : many * images, :] = dot(mat, jnp.concatenate(parts[0], axis=0), NN)
        ng_s[0 : many * images, :] = dot(mat, jnp.concatenate(parts[1], axis=0), NN)
        psum = jnp.zeros((images, width), F32)
        g1 = jnp.zeros((images, width), F32)
        s1 = jnp.zeros((images, width), F32)
        for p in range(0, many, SLAB):
            patch = lax.broadcasted_iota(jnp.int32, (SLAB, images, 1), 0) + (k * LOT + p)
            x = xblk[slot, p : p + SLAB].astype(F32)
            unit, inv = norm(x)
            live = jnp.where(counts > patch, 1.0, 0.0)
            og = cblk[slot, p : p + SLAB].astype(F32) + live * poolc
            cut = slice(p * images, (p + SLAB) * images)
            br = br_s[cut, :].reshape(SLAB, images, width)
            out = x + scale * (br + bias_out)
            out_st[slot, p : p + SLAB] = out
            psum = psum + jnp.sum(live * out, axis=0)
            ng = ng_s[cut, :].reshape(SLAB, images, width)
            t = ng * gain_one
            m1 = jnp.mean(t, axis=-1, keepdims=True)
            m2 = jnp.mean(t * unit, axis=-1, keepdims=True)
            ig_st[slot, p : p + SLAB] = og + inv * (t - m1 - unit * m2)
            g1 = g1 + jnp.sum(ng * unit, axis=0)
            s1 = s1 + jnp.sum(ng, axis=0)
        pooled_ref[...] += psum
        vacc[0] += fold8(g1)
        vacc[1] += fold8(s1)
        for cp in store_lot(k, many, slot):
            cp.start()

    def lots(k):
        slot = lax.rem(k, 2)

        @pl.when(k >= 2)
        def _():
            for cp in store_lot(k - 2, LOT, slot):
                cp.wait()

        lot(k, LOT, slot)

        @pl.when(k + 2 < full)
        def _():
            for cp in load_lot(k + 2, LOT, slot):
                cp.start()

        if rest:
            @pl.when(k + 2 == full)
            def _():
                for cp in load_lot(full, rest, full % 2):
                    cp.start()

    loop(0, full, lots)
    if rest:
        for cp in store_lot(full - 2, LOT, full % 2):
            cp.wait()
        lot(full, rest, full % 2)
    pooled_ref[...] = pooled_ref[...] / counts.astype(F32)

    vacc[2] += fold8(bsum_ref[...])
    small_ref[...] = jnp.zeros_like(small_ref)
    sums = jnp.sum(vacc[...], axis=1)
    for v in range(sums.shape[0]):
        for h in range(width // 256):
            row = v * (width // 256) + h
            small_ref[row : row + 1, :] = sums[v : v + 1, h * 256 : (h + 1) * 256]
    pad = sg_ref.shape[0]
    small_ref[SPATIAL_ROW : SPATIAL_ROW + pad, 0:pad] = sg_ref[...]
    bias = sbg_ref[:, 0:1]
    eye = lax.broadcasted_iota(jnp.int32, (pad, pad), 0) == lax.broadcasted_iota(jnp.int32, (pad, pad), 1)
    bias_row = jnp.sum(jnp.where(eye, bias, 0.0), axis=0, keepdims=True)
    small_ref[SPATIAL_ROW + patches : SPATIAL_ROW + patches + 1, 0:pad] = bias_row
    for cps in grad_out[4:]:
        for cp in cps:
            cp.wait()
    if rest:
        for cp in store_lot(full - 1, LOT, (full - 1) % 2) + store_lot(full, rest, full % 2):
            cp.wait()
    else:
        for k in (full - 2, full - 1):
            for cp in store_lot(k, LOT, k % 2):
                cp.wait()


SPATIAL_ROW = 32


def run_block(
    tokens, cot, nm, bg, info, poolc, bsum, wt, vec, sp, spt, sbias,
    *, rows_cap=1024, tm=256, classes=(80, 112, 144, 176, 208),
):
    patches, images, width = tokens.shape
    gate = wt.shape[1]
    pad = -(-patches // LOT) * LOT
    classes = tuple(m for m in classes if m < pad) + (pad,)
    cap = rows_cap + pad + 48
    cap = -(-cap // tm) * tm
    long = images * pad + tm + LOT
    cfg = (images, patches, width, gate, rows_cap, tm, classes)
    smem = pl.BlockSpec(memory_space=pltpu.SMEM)
    vmem = pl.BlockSpec(memory_space=pltpu.VMEM)
    anyb = pl.BlockSpec(memory_space=pl.ANY)
    dma = pltpu.SemaphoreType.DMA
    shape = jax.ShapeDtypeStruct
    nvec = 3 + 4 * gate // width
    return pl.pallas_call(
        functools.partial(block_kernel, cfg),
        out_shape=(
            shape((patches, images, width), F32),
            shape((patches, images, width), F32),
            shape((images, width), F32),
            shape((3, gate, width), BF),
            shape((256, 256), F32),
        ),
        in_specs=[smem] + [anyb] * 4 + [vmem] * 3 + [anyb] + [vmem] * 4,
        out_specs=[anyb, anyb, vmem, anyb, vmem],
        scratch_shapes=[
            pltpu.VMEM((3, gate, width), F32),
            pltpu.VMEM((pad, pad), F32),
            pltpu.VMEM((pad, 128), F32),
            pltpu.SMEM((images,), jnp.int32),
            pltpu.SMEM((images,), jnp.int32),
            pltpu.SMEM((images,), jnp.int32),
            pltpu.VMEM((3, gate, width), BF),
            pltpu.VMEM((3, width, gate), BF),
            pltpu.VMEM((long, width), BF),
            pltpu.VMEM((long, width), BF),
        ]
        + [pltpu.VMEM((cap, gate), BF)] * 6
        + [
            pltpu.VMEM((cap, 128), F32),
            pltpu.VMEM((tm, gate), F32),
            pltpu.VMEM((pad, gate), F32),
            pltpu.VMEM((2, LOT, images, width), BF),
            pltpu.VMEM((2, LOT, images, width), BF),
            pltpu.VMEM((LOT * images, width), F32),
            pltpu.VMEM((LOT * images, width), F32),
            pltpu.VMEM((2, LOT, images, width), F32),
            pltpu.VMEM((2, LOT, images, width), F32),
            pltpu.VMEM((nvec, 8, width), F32),
            dma((3,)),
            dma((2, images)),
            dma((2, 2)),
            dma((2, 2)),
            dma((6, gate // width)),
        ],
        compiler_params=pltpu.CompilerParams(vmem_limit_bytes=60 * 2**20),
        name="block",
    )(info, tokens, cot, nm, bg, info, poolc, bsum, wt, vec, sp, spt, sbias)


def reduce_kernel(
    g_hbm, small_ref, red_ref, tot_ref, norm_ref,
    acc, rc, rr, rp, rz, sacc, src, srr, srp, srz, nbuf, mbuf, nown, mown,
    send, recv, lsem,
):
    x, y, z, c = place()
    px, py = jnp.where(c == 0, 1 - x, x), jnp.where(c == 0, y, 1 - y)
    rx, ry = jnp.where(c == 0, x, 1 - x), jnp.where(c == 0, 1 - y, y)
    dx, dy = 1 - x, 1 - y
    pnbr, rnbr, core = device(px, py, z, c), device(rx, ry, z, c), device(x, y, z, 1 - c)
    loads = [pltpu.make_async_copy(g_hbm.at[q, :, :, :, c], acc.at[q], lsem.at[q]) for q in range(3)]
    for cp in loads:
        cp.start()
    column = [device(x, y, (z + k) % 4, c) for k in (1, 2, 3)]
    column += [device(x, y, (z + k) % 4, 1 - c) for k in (0, 1, 2, 3)]
    plane = [device(dx, y, z, c), device(x, dy, z, c), device(dx, dy, z, c)]
    barrier = pltpu.get_barrier_semaphore()
    for peer in column + plane:
        pl.semaphore_signal(barrier, inc=1, device_id=peer, device_id_type=MESH)
    pl.semaphore_wait(barrier, len(column + plane))
    index = [0]
    started = []

    def remote(src_ref, dst_ref, dev):
        k = index[0]
        index[0] += 1
        cp = pltpu.make_async_remote_copy(
            src_ref=src_ref, dst_ref=dst_ref, send_sem=send.at[k], recv_sem=recv.at[k],
            device_id=dev, device_id_type=MESH,
        )
        cp.start()
        started.append(cp)
        return cp

    cut = acc.shape[4] // RCUTS
    cuts = [(3, 0)] + [(q, s) for s in range(RCUTS) for q in range(3)]

    def views(k):
        q, s = cuts[k]
        if q == 3:
            return (
                F32, lambda *i: sacc.at[i], lambda *i: src.at[i], lambda *i: srr.at[i],
                lambda *i: srp.at[i], lambda *i: srz.at[i],
            )
        at = pl.ds(s * cut, cut)

        def of(ref, dims):
            def view(*i):
                rest = (slice(None),) * (dims - len(i))
                return ref.at[(q,) + i + rest + (at,)]

            return view

        return BF, of(acc, 3), of(rc, 3), of(rr, 2), of(rp, 1), of(rz, 1)

    def plus(kind, a, b):
        a[...] = (a[...].astype(F32) + b[...].astype(F32)).astype(kind)

    swaps, r_in, p_in, z_in = {}, {}, {}, {}
    scopy = pltpu.make_async_copy(small_ref.at[:, :, :, c], sacc, lsem.at[3])
    scopy.start()
    for k, (q, s) in enumerate(cuts):
        if q == 3:
            swaps[k] = remote(small_ref.at[:, :, :, 1 - c], src, core)
        else:
            at = pl.ds(s * cut, cut)
            swaps[k] = remote(g_hbm.at[q, :, :, :, 1 - c, at], rc.at[q, :, :, :, at], core)

    def stage_two(k):
        kind, a, b, r, p, zz = views(k)
        if k == 0:
            scopy.wait()
        elif k <= 3:
            loads[cuts[k][0]].wait()
        swaps[k].wait_recv()
        for ly in range(2):
            for lx in range(2):
                for lz in range(4):
                    plus(kind, a(ly, lx, lz), b(ly, lx, lz))
        r_in[k] = [remote(a(dy, dx), r(0), rnbr), remote(a(ry, rx), r(1), rnbr)]

    def stage_three(k):
        kind, a, b, r, p, zz = views(k)
        for cp in r_in[k]:
            cp.wait_recv()
        for lz in range(4):
            plus(kind, a(py, px, lz), r(0, lz))
        p_in[k] = remote(a(py, px), p(), pnbr)
        for lz in range(4):
            plus(kind, a(y, x, lz), r(1, lz))

    def stage_four(k):
        kind, a, b, r, p, zz = views(k)
        p_in[k].wait_recv()
        for lz in range(4):
            plus(kind, a(y, x, lz), p(lz))
        z_in[k] = [
            remote(a(y, x, (z + j) % 4), zz(j - 1), device(x, y, (z + j) % 4, c)) for j in (1, 2, 3)
        ]

    def fold(v):
        t = jnp.zeros((8, 128), F32)
        for r in range(0, v.shape[0], 8):
            for l in range(0, v.shape[1], 128):
                part = v[r : r + 8, l : l + 128]
                t = t + part * part
        return t

    squares = [jnp.zeros((8, 128), F32)]
    tots = []

    def stage_five(k):
        kind, a, b, r, p, zz = views(k)
        for cp in z_in[k]:
            cp.wait_recv()
        v = (a(y, x, z)[...].astype(F32) + zz(0)[...].astype(F32)) + (
            zz(1)[...].astype(F32) + zz(2)[...].astype(F32)
        )
        squares[0] = squares[0] + fold(v)
        q, s = cuts[k]
        if q == 3:
            tot_ref[y, x, z, c] = v
            mine = tot_ref.at[y, x, z, c]
            tots.append([remote(mine, mine, dev) for dev in column])
        else:
            red_ref[q, s * cut : (s + 1) * cut] = v

    n = len(cuts)
    for t in range(n + 3 * RLAG):
        if t < n:
            stage_two(t)
        if 0 <= t - RLAG < n:
            stage_three(t - RLAG)
        if 0 <= t - 2 * RLAG < n:
            stage_four(t - 2 * RLAG)
        if 0 <= t - 3 * RLAG < n:
            stage_five(t - 3 * RLAG)
        if t == n:
            for cp in tots[0]:
                cp.wait_recv()
            lines = tot_ref.at[y, x]
            tots.append([remote(lines, lines, dev) for dev in plane])
    nown[...] = squares[0]
    sent = [remote(nown, nbuf.at[z * 2 + c], dev) for dev in column]
    nbuf[z * 2 + c] = squares[0]
    for cp in sent:
        cp.wait_recv()
    total = nbuf[0]
    for i in range(1, 8):
        total = total + nbuf[i]
    mown[...] = total
    sent = [remote(mown, mbuf.at[y * 2 + x], dev) for dev in plane]
    mbuf[y * 2 + x] = total
    for cp in sent:
        cp.wait_recv()
    total = mbuf[0]
    for i in range(1, 4):
        total = total + mbuf[i]
    total = jnp.sum(jnp.sum(total, axis=0, keepdims=True), axis=1, keepdims=True)
    norm_ref[...] = jnp.broadcast_to(jnp.sqrt(total), norm_ref.shape)
    for cp in tots[1]:
        cp.wait_recv()
    for cp in started:
        cp.wait_send()


RCUTS = 3
RLAG = 2
NRED = 7 * (3 * RCUTS + 1) + 20


def reduce_all(g, small):
    rows, width = g.shape[-2:]
    vmem = pl.BlockSpec(memory_space=pltpu.VMEM)
    anyb = pl.BlockSpec(memory_space=pl.ANY)
    dma = pltpu.SemaphoreType.DMA
    blk, sblk = (rows, width), small.shape[-2:]
    return pl.pallas_call(
        reduce_kernel,
        out_shape=(
            jax.ShapeDtypeStruct((3,) + blk, F32),
            jax.ShapeDtypeStruct(small.shape, F32),
            jax.ShapeDtypeStruct((8, 128), F32),
        ),
        in_specs=[anyb, vmem],
        out_specs=[vmem] * 3,
        scratch_shapes=[
            pltpu.VMEM((3, 2, 2, 4) + blk, BF),
            pltpu.VMEM((3, 2, 2, 4) + blk, BF),
            pltpu.VMEM((3, 2, 4) + blk, BF),
            pltpu.VMEM((3, 4) + blk, BF),
            pltpu.VMEM((3, 3) + blk, BF),
            pltpu.VMEM((2, 2, 4) + sblk, F32),
            pltpu.VMEM((2, 2, 4) + sblk, F32),
            pltpu.VMEM((2, 4) + sblk, F32),
            pltpu.VMEM((4,) + sblk, F32),
            pltpu.VMEM((3,) + sblk, F32),
            pltpu.VMEM((8, 8, 128), F32),
            pltpu.VMEM((4, 8, 128), F32),
            pltpu.VMEM((8, 128), F32),
            pltpu.VMEM((8, 128), F32),
            dma((NRED,)), dma((NRED,)), dma((4,)),
        ],
        compiler_params=pltpu.CompilerParams(
            collective_id=1, has_side_effects=True, vmem_limit_bytes=60 * 2**20
        ),
        name="reduce",
    )(g, small)


STEP = 10
BETA_FIRST = 0.9
BETA_SECOND = 0.95
ADAM_EPS = 1e-08
DECAY_RATE = 0.05
RATE_MATRIX = 0.05
RATE_VECTOR = 0.8
CLIP_BOUND = 1.0
BOTH = ("dp", "fsdp")


def adam_step(weight, first, second, gradient, step_rate, weight_decay):
    first_new = BETA_FIRST * first + (1.0 - BETA_FIRST) * gradient
    second_new = BETA_SECOND * second + (1.0 - BETA_SECOND) * gradient * gradient
    first_hat = first_new * (1.0 / (1.0 - BETA_FIRST**STEP))
    second_hat = second_new * (1.0 / (1.0 - BETA_SECOND**STEP))
    weight_new = weight - step_rate * (
        first_hat / (jnp.sqrt(second_hat) + ADAM_EPS) + weight_decay * weight
    )
    return (weight_new, first_new, second_new)


def adam_kernel(own, red, tot, norm, iw, i1, i2, ow, o1, o2, sw, s1, s2, *outs):
    clip = CLIP_BOUND / jnp.maximum(norm[0:1, 0:1], CLIP_BOUND)
    rows = ow.shape[0]
    for q in range(2):
        for r in range(0, rows, 8):
            cut = slice(r, r + 8)
            new = adam_step(
                iw[q, cut], i1[q, cut], i2[q, cut], red[q, cut] * clip, RATE_MATRIX, DECAY_RATE
            )
            for ref, val in zip(outs[0:3], new):
                ref[q, cut] = val
    for r in range(0, rows, 8):
        cut = slice(r, r + 8)
        new = adam_step(ow[cut], o1[cut], o2[cut], red[2, cut] * clip, RATE_MATRIX, DECAY_RATE)
        for ref, val in zip(outs[3:6], new):
            ref[cut] = val
    me = lax.axis_index("dp") * lax.axis_size("fsdp") + lax.axis_index("fsdp")
    start = me * own
    row, off = start // 256, start % 256
    pair = [jnp.broadcast_to(tot[pl.ds(row + i, 1), :], (8, 256)) for i in (0, 1)]
    pair = pltpu.roll(jnp.concatenate(pair, axis=1), (512 - off) % 512, 1)
    outs[9][...] = pair[0:1, 0:256] * clip
    outs[10][...] = norm[0:1, 0:1]
    side, cols = sw.shape
    grad = tot[SPATIAL_ROW : SPATIAL_ROW + side, 0:cols] * clip
    last = lax.broadcasted_iota(jnp.int32, (side, 1), 0) == side - 1
    rate = jnp.where(last, RATE_VECTOR, RATE_MATRIX)
    decay = jnp.where(last, 0.0, DECAY_RATE)
    new = adam_step(sw[...], s1[...], s2[...], grad, rate, decay)
    for ref, val in zip(outs[6:9], new):
        ref[...] = val


def adam_all(own, red, tot, norm, inner, outer, spatial):
    vmem = pl.BlockSpec(memory_space=pltpu.VMEM)
    shape = lambda a: jax.ShapeDtypeStruct(a.shape, F32)
    return pl.pallas_call(
        functools.partial(adam_kernel, own),
        out_shape=tuple(shape(a) for a in inner + outer + spatial)
        + (jax.ShapeDtypeStruct((1, 256), F32), jax.ShapeDtypeStruct((1, 1), F32)),
        in_specs=[vmem] * 12,
        out_specs=[vmem] * 11,
        compiler_params=pltpu.CompilerParams(vmem_limit_bytes=60 * 2**20),
        name="adam",
    )(red, tot, norm, *inner, *outer, *spatial)


def slow_prepare(inner_t, outer_weight, vectors, tokens, cot, mask, keep, pool_cot, spatial):
    patches, images, width = tokens.shape
    pad = -(-patches // LOT) * LOT
    wt = jnp.concatenate(
        [
            lax.all_gather(inner_t.astype(BF), BOTH, axis=1, tiled=True),
            lax.all_gather(outer_weight.astype(BF), BOTH, axis=0, tiled=True)[None],
        ],
        axis=0,
    )
    vec = lax.all_gather(vectors.astype(BF), BOTH, axis=0, tiled=True).astype(F32)
    vec = vec.reshape(-1, width)
    counts = jnp.sum(mask, axis=1)
    info = jnp.zeros((images, 128), jnp.int32).at[:, 0].set(counts).at[:, 1].set(keep)
    poolc = pool_cot.astype(F32) / counts.astype(F32)[:, None]
    unit, _ = norm(tokens.astype(F32))
    edge = ((0, 0), (0, pad - patches), (0, 0))
    nm = (unit * vec[0] + vec[1]).astype(BF)
    live = mask.astype(F32).T[:, :, None]
    scale = keep.astype(F32) * (1.0 / (1.0 - DROP_RATE))
    bg = (scale[:, None] * (cot.astype(F32) + live * poolc)).astype(BF)
    bsum = jnp.sum(bg, axis=0, dtype=F32)
    nm = jnp.pad(nm.transpose(1, 0, 2), edge)
    bg = jnp.pad((bg * live.astype(BF)).transpose(1, 0, 2), edge)
    low = spatial[:patches].astype(BF)
    square = ((0, 256 - patches), (0, 256 - patches))
    sbias = jnp.pad(spatial[patches][:, None], ((0, 256 - patches), (0, 0)))
    return wt, vec, nm, bg, info, poolc, bsum, jnp.pad(low, square), jnp.pad(low.T, square), sbias


def slow_reduce(grads, small):
    red = lax.psum_scatter(grads.astype(F32), BOTH, scatter_dimension=1, tiled=True)
    tot = lax.psum(small, BOTH)
    squares = lax.psum(jnp.sum(red * red), BOTH) + jnp.sum(tot * tot)
    return red, tot, jnp.broadcast_to(jnp.sqrt(squares), (8, 128))


def per_device(
    fast,
    tokens,
    valid_mask,
    keep_mask,
    out_cotangent,
    pool_cotangent,
    inner_weight,
    outer_weight,
    vectors,
    spatial,
    inner_first,
    inner_second,
    outer_first,
    outer_second,
    vector_first,
    vector_second,
    spatial_first,
    spatial_second,
):
    own = vectors.shape[0]
    rows, width = outer_weight.shape
    inner_t = tuple(a.transpose(0, 2, 1) for a in (inner_weight, inner_first, inner_second))
    tokens = tokens.transpose(1, 0, 2)
    cot = out_cotangent.transpose(1, 0, 2)
    if fast:
        wt, *ready = gather_all(
            own,
            inner_t[0],
            outer_weight,
            jnp.pad(vectors, (0, 1024 - own)).reshape(8, 128),
            tokens,
            cot,
            valid_mask,
            keep_mask,
            pool_cotangent,
            spatial,
        )
        wt = wt.reshape(3, 32 * rows, width)
    else:
        wt, *ready = slow_prepare(
            inner_t[0], outer_weight, vectors, tokens, cot, valid_mask, keep_mask, pool_cotangent, spatial
        )
    vec, nm, bg, info, poolc, bsum, sp, spt, sbias = ready
    output, input_grad, pooled, grads, small = run_block(
        tokens, cot, nm, bg, info, poolc, bsum, wt, vec, sp, spt, sbias
    )
    output = output.transpose(1, 0, 2)
    input_grad = input_grad.transpose(1, 0, 2)
    if fast:
        red, tot, norm = reduce_all(
            grads.reshape(3, 2, 2, 4, 2, rows, width), small.reshape(2, 2, 4, 2, 8, 256)
        )
        tot = tot.reshape(256, 256)
    else:
        red, tot, norm = slow_reduce(grads, small)
    new = adam_all(
        own,
        red,
        tot,
        norm,
        inner_t,
        (outer_weight, outer_first, outer_second),
        (spatial, spatial_first, spatial_second),
    )
    grad_norm = new[10].reshape(())
    vector_out = adam_step(
        vectors, vector_first, vector_second, new[9].reshape(-1)[:own], RATE_VECTOR, 0.0
    )
    return (
        (output, input_grad, pooled, grad_norm)
        + tuple(a.transpose(0, 2, 1) for a in new[0:3])
        + tuple(new[3:6])
        + vector_out
        + tuple(new[6:9])
    )


def solution(mesh):
    fast = mesh.shape["dp"] == 4 and mesh.shape["fsdp"] == 8
    rows3 = P(BOTH, None, None)
    rows2 = P(BOTH, None)
    rows1 = P(BOTH)
    cols3 = P(None, None, BOTH)
    in_specs = (
        (rows3, rows2, rows1, rows3, rows2, cols3, rows2, rows1, P())
        + (cols3,) * 2
        + (rows2,) * 2
        + (rows1,) * 2
        + (P(),) * 2
    )
    out_specs = (
        (rows3, rows3, rows2, P()) + (cols3,) * 3 + (rows2,) * 3 + (rows1,) * 3 + (P(),) * 3
    )
    return jax.shard_map(
        functools.partial(per_device, fast),
        mesh=mesh,
        in_specs=in_specs,
        out_specs=out_specs,
        check_vma=False,
    )
```
